128 devices in a mesh: dp: 16 (over y, x), row: 2 (over core), col: 4 (over z).
Axes of the slice: x: 4, y: 4, z: 4, core: 2. Of those that a mesh axis runs over, the one named last changes fastest.
Arguments:
- tokens_in: bfloat16 [2048, 6144], P('dp', 'row'), may hold values from -6 to 6
- out_grad: bfloat16 [2048, 6144], P('dp', 'row'), may hold values from -6 to 6
- up_weight: bfloat16 [2, 4, 288, 128, 128], P('row', 'col'), may hold values from -0.15625 to 0.15625
- down_weight: bfloat16 [2, 4, 288, 128, 128], P('row', 'col'), may hold values from -0.15625 to 0.15625
- up_blocks: int32 [2, 4, 288], P('row', 'col'), may hold values from 0 to 1151, as said below
- down_blocks: int32 [2, 4, 288], P('row', 'col'), may hold values from 0 to 1151, as said below
- owners: int32 [2, 4, 288], P('row', 'col'), may hold values from 0 to 287, as said below
Outputs:
- input_grad: bfloat16 [2048, 6144], P(('dp', 'col'), 'row')
- up_grad: bfloat16 [2, 4, 288, 128, 128], P('row', 'col', 'dp')
- down_grad: bfloat16 [2, 4, 288, 128, 128], P('row', 'col', 'dp')
The draws below stay inside these ranges and needn't reach their ends.
Inputs may be any that keep to these rules, and one draw needn't show every extreme that they name: `up_blocks`: within each cell the entries are distinct; their number is 288. `down_blocks`: within each cell the entries are distinct; their number is 288. `owners`: within each cell the entries are a permutation of the slots.
All inputs are finite; a program needn't handle non-finite values.
Results may differ from the reference program's by a relative error of at most 0.024.
Values may be sent and summed in bfloat16 or wider, within the bound.
A program may use at most 192 MiB of HBM per device.

```python
import jax
import jax.numpy as jnp
from jax import lax

D = 6144
H = 24576
BLK = 128
TOK_DEV = 128
TOKENS = 2048
CELL_ROWS = 24
CELL_COLS = 48
KCELL = 288
N_DP = 16
N_ROW = 2
N_COL = 4


def pick_cells(key, choices_all, keep_count):
    cell_keys = jax.random.split(key, N_ROW * N_COL)
    picked = jax.vmap(lambda one_key: jax.random.permutation(one_key, choices_all)[:keep_count])(cell_keys)
    return picked.reshape(N_ROW, N_COL, keep_count).astype(jnp.int32)


def draw_up_blocks(key, part):
    key = jax.random.fold_in(key, 11)
    return pick_cells(key, CELL_ROWS * CELL_COLS, KCELL)


def draw_down_blocks(key, part):
    key = jax.random.fold_in(key, 23)
    return pick_cells(key, CELL_ROWS * CELL_COLS, KCELL)


def draw_owners(key, part):
    key = jax.random.fold_in(key, 37)
    return pick_cells(key, KCELL, KCELL)


def block_scale(stream_key, dims, cuts, low, high):
    level, own = 1.0, jax.random.fold_in(stream_key, 6)
    for axis_at, blocks in cuts:
        heights = jnp.exp(jax.random.uniform(jax.random.fold_in(own, axis_at), (blocks,), jnp.float32, low / len(cuts), high / len(cuts)))
        level = level * jnp.repeat(heights, dims[axis_at] // blocks).reshape([-1 if axis == axis_at else 1 for axis in range(len(dims))])
    return level


def centred(own_key, dims, spread, limit, pieces=(), dtype=jnp.bfloat16):
    values = jax.random.normal(own_key, dims, jnp.float32) * spread
    if len(pieces) > 0:
        values = block_scale(own_key, dims, pieces, -0.22, 0.18) * values
    return jnp.clip(values, min=-limit, max=limit).astype(dtype)


def setup_inputs(seed: int = 0) -> dict:
    seeds = jax.random.split(jax.random.key(seed), 8)
    tokens_in = centred(seeds[0], (TOKENS, D), 1.0, 6.0, ((0, 16), (1, 2)))
    out_grad = centred(seeds[1], (TOKENS, D), 1.0, 6.0, ((0, 16), (1, 2)))
    up_weight = centred(seeds[2], (N_ROW, N_COL, KCELL, BLK, BLK), (D // 4) ** -0.5, 0.15625, ((0, 2), (1, 4)))
    down_weight = centred(seeds[3], (N_ROW, N_COL, KCELL, BLK, BLK), (D // 4) ** -0.5, 0.15625, ((0, 2), (1, 4)))
    up_blocks = draw_up_blocks(jax.random.fold_in(seeds[7], 71), 0)
    down_blocks = draw_down_blocks(jax.random.fold_in(seeds[7], 71), 0)
    owners = draw_owners(jax.random.fold_in(seeds[7], 71), 0)
    return {"tokens_in": tokens_in, "out_grad": out_grad, "up_weight": up_weight, "down_weight": down_weight, "up_blocks": up_blocks, "down_blocks": down_blocks, "owners": owners}


root_two_pi = 0.7978845608028654
cubic_coef = 0.044715


def gelu_both(pre_act):
    inner_arg = root_two_pi * (pre_act + cubic_coef * pre_act * pre_act * pre_act)
    tanh_inner = jnp.tanh(inner_arg)
    gelu_value = 0.5 * pre_act * (1.0 + tanh_inner)
    gelu_slope = 0.5 * (1.0 + tanh_inner) + 0.5 * pre_act * (1.0 - tanh_inner * tanh_inner) * root_two_pi * (1.0 + 3.0 * cubic_coef * pre_act * pre_act)
    return gelu_value, gelu_slope


def rounded(values):
    narrow = lax.optimization_barrier(values.astype(jnp.bfloat16))
    return narrow.astype(jnp.float32)


def place_blocks(left, weights, pick_in, pick_out, width_out, transposed):
    row_count = left.shape[0]
    block_size = weights.shape[-1]
    picked = left.reshape(row_count, -1, block_size)[:, pick_in, :].astype(jnp.float32)
    if transposed:
        product = jnp.einsum("tkb,kcb->tkc", picked, weights.astype(jnp.float32), precision=lax.Precision.HIGHEST)
    else:
        product = jnp.einsum("tkb,kbc->tkc", picked, weights.astype(jnp.float32), precision=lax.Precision.HIGHEST)
    summed = jnp.zeros((row_count, width_out, block_size), jnp.float32).at[:, pick_out, :].add(product)
    return summed.reshape(row_count, width_out * block_size)


def block_grads(left, right, pick_left, pick_right, block_size):
    row_count = left.shape[0]
    left_blocks = left.reshape(row_count, -1, block_size)[:, pick_left, :].astype(jnp.float32)
    right_blocks = right.reshape(row_count, -1, block_size)[:, pick_right, :].astype(jnp.float32)
    return jnp.einsum("tkb,tkc->kbc", left_blocks, right_blocks, precision=lax.Precision.HIGHEST)


def reference(tokens_in, out_grad, up_weight, down_weight, up_blocks, down_blocks, owners):
    width_row = D // N_ROW
    width_col = H // N_COL

    def one_shard(carried, shard):
        x_shard, g_shard = shard
        hidden_cols = []
        grad_cols = []
        for col_cell in range(N_COL):
            pre_sum = jnp.zeros((TOK_DEV, width_col), jnp.float32)
            back_sum = jnp.zeros((TOK_DEV, width_col), jnp.float32)
            for row_cell in range(N_ROW):
                x_part = x_shard[:, row_cell * width_row:(row_cell + 1) * width_row]
                g_part = g_shard[:, row_cell * width_row:(row_cell + 1) * width_row]
                up_idx = up_blocks[row_cell, col_cell]
                down_idx = down_blocks[row_cell, col_cell]
                pre_sum = pre_sum + rounded(place_blocks(x_part, up_weight[row_cell, col_cell], up_idx // CELL_COLS, up_idx % CELL_COLS, CELL_COLS, False))
                back_sum = back_sum + rounded(place_blocks(g_part, down_weight[row_cell, col_cell], down_idx % CELL_ROWS, down_idx // CELL_ROWS, CELL_COLS, True))
            gelu_value, gelu_slope = gelu_both(pre_sum)
            hidden_cols.append(gelu_value.astype(jnp.bfloat16))
            grad_cols.append((back_sum * gelu_slope).astype(jnp.bfloat16))
        dx_rows = []
        up_rows = []
        down_rows = []
        for row_cell in range(N_ROW):
            x_part = x_shard[:, row_cell * width_row:(row_cell + 1) * width_row]
            g_part = g_shard[:, row_cell * width_row:(row_cell + 1) * width_row]
            dx_sum = jnp.zeros((TOK_DEV, width_row), jnp.float32)
            up_cells = []
            down_cells = []
            for col_cell in range(N_COL):
                up_idx = up_blocks[row_cell, col_cell]
                down_idx = down_blocks[row_cell, col_cell]
                dx_sum = dx_sum + rounded(place_blocks(grad_cols[col_cell], up_weight[row_cell, col_cell], up_idx % CELL_COLS, up_idx // CELL_COLS, CELL_ROWS, True))
                up_cells.append(rounded(block_grads(x_part, grad_cols[col_cell], up_idx // CELL_COLS, up_idx % CELL_COLS, BLK)))
                down_cells.append(rounded(block_grads(hidden_cols[col_cell], g_part, down_idx // CELL_ROWS, down_idx % CELL_ROWS, BLK)))
            dx_rows.append(dx_sum.astype(jnp.bfloat16))
            up_rows.append(jnp.stack(up_cells))
            down_rows.append(jnp.stack(down_cells))
        up_total = carried[0] + jnp.stack(up_rows)
        down_total = carried[1] + jnp.stack(down_rows)
        return (up_total, down_total), jnp.concatenate(dx_rows, axis=1)

    zeros_grad = jnp.zeros((N_ROW, N_COL, KCELL, BLK, BLK), jnp.float32)
    shards = (tokens_in.reshape(N_DP, TOK_DEV, D), out_grad.reshape(N_DP, TOK_DEV, D))
    totals, dx_all = lax.scan(one_shard, (zeros_grad, zeros_grad), shards)
    inverse = jnp.argsort(owners, axis=-1).astype(jnp.int32)
    up_grad = jnp.take_along_axis(totals[0], inverse[:, :, :, None, None], axis=2).astype(jnp.bfloat16)
    down_grad = jnp.take_along_axis(totals[1], inverse[:, :, :, None, None], axis=2).astype(jnp.bfloat16)
    return dx_all.reshape(TOKENS, D), up_grad, down_grad
```

```python
import functools

import jax
import jax.numpy as jnp
from jax import lax
from jax.experimental import pallas as pl
from jax.experimental.pallas import tpu as pltpu
from jax.sharding import PartitionSpec as P

BF = jnp.bfloat16
F32 = jnp.float32
B = 128
ROWS = 24
COLS = 48
NBLK = 288
SIDE = 4
SHARE = 18
CH = 12
NN = (((1,), (0,)), ((), ()))
NT = (((1,), (1,)), ((), ()))
MESH = pl.DeviceIdType.MESH

root_two_pi = 0.7978845608028654
cubic_coef = 0.044715


def activate(pre_sum, back_sum):
    square = pre_sum * pre_sum
    inner_arg = root_two_pi * (pre_sum + cubic_coef * square * pre_sum)
    tanh_inner = jnp.tanh(inner_arg)
    half = 0.5 * (1.0 + tanh_inner)
    slope = half + 0.5 * pre_sum * (1.0 - tanh_inner * tanh_inner) * root_two_pi * (
        1.0 + 3.0 * cubic_coef * square
    )
    return pre_sum * half, back_sum * slope


def dot(left, right, dims):
    return lax.dot_general(left, right, dims, preferred_element_type=F32)


def lanes(index):
    return pl.ds(pl.multiple_of(index * B, B), B)


def forward_kernel(
    steps, unroll, uf, uh, df, dh, x_ref, g_ref, wu_ref, wd_ref, pre_ref, back_ref, xt_ref, gb_ref, pacc, bacc
):
    step = pl.program_id(0)
    chunk = wu_ref.shape[0]

    @pl.when(step == 0)
    def _():
        pacc[...] = jnp.zeros_like(pacc)
        bacc[...] = jnp.zeros_like(bacc)
        for f in range(ROWS):
            xt_ref[f] = x_ref[:, f * B : (f + 1) * B].T
            gb_ref[f] = g_ref[:, f * B : (f + 1) * B]

    def group(i, carry):
        ups, downs = [], []
        for j in range(unroll):
            k = step * chunk + i * unroll + j
            ups.append((uh[k], dot(x_ref[:, lanes(uf[k])], wu_ref[i * unroll + j], NN)))
            downs.append((dh[k], dot(g_ref[:, lanes(df[k])], wd_ref[i * unroll + j], NT)))
        for j in range(unroll):
            pacc[ups[j][0]] += ups[j][1]
            bacc[downs[j][0]] += downs[j][1]
        return carry

    lax.fori_loop(0, chunk // unroll, group, 0)

    @pl.when(step == steps - 1)
    def _():
        pre_ref[...] = pacc[...].astype(BF)
        back_ref[...] = bacc[...].astype(BF)


def forward(uf, uh, df, dh, x, g, wu, wd, steps=12, unroll=12):
    chunk = NBLK // steps

    def whole(shape):
        return pl.BlockSpec(shape, lambda s, *_: (0,) * len(shape))

    weights = pl.BlockSpec((chunk, B, B), lambda s, *_: (s, 0, 0))
    return pl.pallas_call(
        functools.partial(forward_kernel, steps, unroll),
        grid_spec=pltpu.PrefetchScalarGridSpec(
            num_scalar_prefetch=4,
            grid=(steps,),
            in_specs=[whole((B, ROWS * B)), whole((B, ROWS * B)), weights, weights],
            out_specs=[whole((COLS, B, B)), whole((COLS, B, B)), whole((ROWS, B, B)), whole((ROWS, B, B))],
            scratch_shapes=[pltpu.VMEM((COLS, B, B), F32), pltpu.VMEM((COLS, B, B), F32)],
        ),
        out_shape=[
            jax.ShapeDtypeStruct((COLS, B, B), BF),
            jax.ShapeDtypeStruct((COLS, B, B), BF),
            jax.ShapeDtypeStruct((ROWS, B, B), BF),
            jax.ShapeDtypeStruct((ROWS, B, B), BF),
        ],
        compiler_params=pltpu.CompilerParams(vmem_limit_bytes=48 * 2**20),
        name="forward",
    )(uf, uh, df, dh, x, g, wu, wd)


def back_kernel(*refs):
    (gu_f, gu_h, gd_f, gd_h, sx_h, sx_k, keep, last, some) = refs[:9]
    pre_ref, back_ref, xt_own, og_own, wu_hbm = refs[9:14]
    dx_out, up_out, dn_out = refs[14:17]
    (
        pre_in, back_in, pg_own, ht_own,
        xt_l, xt_r, xt_o, og_l, og_r, og_o,
        pg_l, pg_r, pg_o, ht_l, ht_r, ht_o,
        wu, runs, dxp, zin,
        uf_s, ur_s, ul_s, ua_t, ub_t, ul_v, ur_v, u_acc,
        df_s, dr_s, dl_s, da_t, db_t, dl_v, dr_v, d_acc,
        ex_s, ex_r, ag_s, ag_r, pa_s, pa_r, rs_s, rs_r, z_s, z_r, w_s,
    ) = refs[17:]
    dp, row, col = lax.axis_index("dp"), lax.axis_index("row"), lax.axis_index("col")
    y, x = dp // SIDE, dp % SIDE
    other = (dp, 1 - row, col)
    x_right = (y * SIDE + (x + 1) % SIDE, row, col)
    x_left = (y * SIDE + (x + 3) % SIDE, row, col)
    y_right = (((y + 1) % SIDE) * SIDE + x, row, col)
    y_left = (((y + 3) % SIDE) * SIDE + x, row, col)
    z_peers = [(dp, row, (col + d) % SIDE) for d in range(1, SIDE)]

    barrier = pltpu.get_barrier_semaphore()
    peers = [other, x_right, x_left, y_right, y_left] + z_peers
    for peer in peers:
        pl.semaphore_signal(barrier, inc=1, device_id=peer, device_id_type=MESH)
    pl.semaphore_wait(barrier, len(peers))

    started = []

    def send(src, dst, send_sem, recv_sem, peer):
        copy = pltpu.make_async_remote_copy(
            src_ref=src, dst_ref=dst, send_sem=send_sem, recv_sem=recv_sem, device_id=peer, device_id_type=MESH
        )
        copy.start()
        started.append(copy)

    def arrived(dst, send_sem, recv_sem, peer):
        pltpu.make_async_remote_copy(
            src_ref=dst, dst_ref=dst, send_sem=send_sem, recv_sem=recv_sem, device_id=peer, device_id_type=MESH
        ).wait_recv()

    for c in range(2):
        theirs = pl.ds((1 - row) * ROWS + c * CH, CH)
        here = pl.ds(c * CH, CH)
        send(pre_ref.at[theirs], pre_in.at[here], ex_s.at[c], ex_r.at[c], other)
        send(back_ref.at[theirs], back_in.at[here], ex_s.at[2 + c], ex_r.at[2 + c], other)

    weights = pltpu.make_async_copy(wu_hbm, wu, w_s)
    weights.start()

    kinds = {
        "xt": (0, xt_own, xt_l, xt_r, xt_o, x_right, x_left, 0),
        "og": (1, og_own, og_l, og_r, og_o, y_right, y_left, 0),
        "pg": (2, pg_own, pg_l, pg_r, pg_o, x_right, x_left, row * ROWS),
        "ht": (3, ht_own, ht_l, ht_r, ht_o, y_right, y_left, row * ROWS),
    }

    def part(base, c):
        return pl.ds(base + c * CH, CH)

    def ring_out(kind, c, way):
        n, own, left, right, _, to_right, to_left, base = kinds[kind]
        at = part(base, c)
        if way == "r":
            send(own.at[at], left.at[at], ag_s.at[n, c], ag_r.at[n, c], to_right)
        else:
            send(own.at[at], right.at[at], ag_s.at[n, 2 + c], ag_r.at[n, 2 + c], to_left)

    def ring_wait(kind, slot):
        n, _, left, right, far, to_right, to_left, base = kinds[kind]
        dst = (left, left, right, right, far, far)[slot].at[part(base, slot % 2)]
        arrived(dst, ag_s.at[n, slot], ag_r.at[n, slot], to_right)

    def ring_forward(kind, way):
        n, _, left, right, far, to_right, to_left, base = kinds[kind]
        if way == "r":
            at = part(base, 0)
            send(left.at[at], far.at[at], ag_s.at[n, 4], ag_r.at[n, 4], to_right)
        else:
            at = part(base, 1)
            send(right.at[at], far.at[at], ag_s.at[n, 5], ag_r.at[n, 5], to_left)

    def pair_buffer(kind, slot):
        _, own, left, right, far, _, _, _ = kinds[kind]
        return (own, own, left, left, right, right, far, far)[slot]

    def pair_out(kind, slot):
        n, base = kinds[kind][0] - 2, kinds[kind][7]
        ref = pair_buffer(kind, slot).at[part(base, slot % 2)]
        send(ref, ref, pa_s.at[n, slot], pa_r.at[n, slot], other)

    def pair_wait(kind, slot):
        n = kinds[kind][0] - 2
        ref = pair_buffer(kind, slot).at[part((1 - row) * ROWS, slot % 2)]
        arrived(ref, pa_s.at[n, slot], pa_r.at[n, slot], other)

    for kind in ("xt", "og"):
        ring_out(kind, 0, "r")
        ring_out(kind, 1, "l")
    for kind in ("xt", "og"):
        ring_out(kind, 1, "r")
        ring_out(kind, 0, "l")

    for c in range(2):
        here = pl.ds(c * CH, CH)
        arrived(pre_in.at[here], ex_s.at[c], ex_r.at[c], other)
        arrived(back_in.at[here], ex_s.at[2 + c], ex_r.at[2 + c], other)

        def one(i, carry, c=c):
            mine = row * ROWS + c * CH + i
            pre = pre_ref[mine].astype(F32) + pre_in[c * CH + i].astype(F32)
            back = back_ref[mine].astype(F32) + back_in[c * CH + i].astype(F32)
            hidden, pre_grad = activate(pre, back)
            pg_own[mine] = pre_grad.astype(BF)
            ht_own[mine] = hidden.astype(BF).T
            return carry

        lax.fori_loop(0, CH, one, 0)
        for kind in ("pg", "ht"):
            pair_out(kind, c)
    for kind in ("pg", "ht"):
        ring_out(kind, 0, "r")
        ring_out(kind, 1, "l")
    for kind in ("pg", "ht"):
        ring_out(kind, 1, "r")
        ring_out(kind, 0, "l")
    for kind in ("xt", "og"):
        ring_wait(kind, 0)
        ring_forward(kind, "r")
        ring_wait(kind, 3)
        ring_forward(kind, "l")

    pair_wait("pg", 0)
    pair_wait("pg", 1)
    weights.wait()
    unroll = 12

    def run(i, total):
        products = []
        for j in range(unroll):
            r = i * unroll + j
            products.append(dot(pg_own[sx_h[r]], wu[sx_k[r]], NT))
        for j in range(unroll):
            r = i * unroll + j
            total = total * keep[r] + products[j]
            runs[r] = total.astype(BF)
        return total

    lax.fori_loop(0, NBLK // unroll, run, jnp.zeros((B, B), F32))
    for f in range(ROWS):
        dxp[:, f * B : (f + 1) * B] = (runs[last[f]].astype(F32) * some[f]).astype(BF)
    for d in range(1, SIDE):
        theirs = pl.ds(pl.multiple_of(((col + d) % SIDE) * 32, 32), 32)
        send(dxp.at[theirs], zin.at[d - 1], z_s.at[d - 1], z_r.at[d - 1], z_peers[d - 1])

    for kind in ("xt", "og"):
        for slot in (1, 2):
            ring_wait(kind, slot)
    for kind in ("pg", "ht"):
        ring_wait(kind, 0)
        ring_forward(kind, "r")
        pair_out(kind, 2)
        ring_wait(kind, 3)
        ring_forward(kind, "l")
        pair_out(kind, 5)
    for kind in ("pg", "ht"):
        ring_wait(kind, 1)
        pair_out(kind, 3)
        ring_wait(kind, 2)
        pair_out(kind, 4)
    for kind in ("xt", "og"):
        for slot in (4, 5):
            ring_wait(kind, slot)
    for slot in (4, 5):
        for kind in ("pg", "ht"):
            ring_wait(kind, slot)
            pair_out(kind, slot + 2)
    for kind in ("ht",):
        for slot in range(2):
            pair_wait(kind, slot)
    for slot in range(2, 8):
        for kind in ("pg", "ht"):
            pair_wait(kind, slot)

    def up_block(s):
        f, h = gu_f[s], gu_h[s]
        left = jnp.concatenate([xt_own[f], xt_l[f], xt_r[f], xt_o[f]], axis=1)
        right = jnp.concatenate([pg_own[h], pg_l[h], pg_r[h], pg_o[h]], axis=0)
        return dot(left, right, NN)

    def dn_block(s):
        f, h = gd_f[s], gd_h[s]
        left = jnp.concatenate([ht_own[h], ht_l[h], ht_r[h], ht_o[h]], axis=1)
        right = jnp.concatenate([og_own[f], og_l[f], og_r[f], og_o[f]], axis=0)
        return dot(left, right, NN)

    def up_base(d):
        return ((y + d) % SIDE) * (SIDE * SHARE) + x * SHARE

    def dn_base(d):
        return y * (SIDE * SHARE) + ((x + d) % SIDE) * SHARE

    half = SHARE // 2

    def fill(block, base, out, first, added=None):
        def body(i, carry):
            for j in range(3):
                at = first + i * 3 + j
                value = block(base + at)
                if added is not None:
                    value = value + added[i * 3 + j].astype(F32)
                out[at] = value.astype(out.dtype)
            return carry

        lax.fori_loop(0, half // 3, body, 0)

    sides = (
        (0, up_block, up_base, y_right, y_left, uf_s, ur_s, ul_s, ua_t, ub_t, ul_v, ur_v, u_acc, up_out),
        (1, dn_block, dn_base, x_right, x_left, df_s, dr_s, dl_s, da_t, db_t, dl_v, dr_v, d_acc, dn_out),
    )
    for n, block, base, to_right, to_left, f_s, r_s, l_s, a_t, b_t, l_v, r_v, acc, out in sides:
        fill(block, base(2), f_s, 0)
        send(f_s.at[pl.ds(0, half)], a_t, rs_s.at[n, 0], rs_r.at[n, 0], to_right)
        fill(block, base(2), f_s, half)
        send(f_s.at[pl.ds(half, half)], b_t, rs_s.at[n, 1], rs_r.at[n, 1], to_left)
    for n, block, base, to_right, to_left, f_s, r_s, l_s, a_t, b_t, l_v, r_v, acc, out in sides:
        fill(block, base(1), r_s, half)
        arrived(a_t, rs_s.at[n, 0], rs_r.at[n, 0], to_left)
        fill(block, base(1), r_s, 0, a_t)
        send(r_s, l_v, rs_s.at[n, 2], rs_r.at[n, 2], to_right)
        fill(block, base(3), l_s, 0)
        arrived(b_t, rs_s.at[n, 1], rs_r.at[n, 1], to_right)
        fill(block, base(3), l_s, half, b_t)
        send(l_s, r_v, rs_s.at[n, 3], rs_r.at[n, 3], to_left)
    for n, block, base, to_right, to_left, f_s, r_s, l_s, a_t, b_t, l_v, r_v, acc, out in sides:
        fill(block, base(0), acc, 0)
        fill(block, base(0), acc, half)

    for d in range(1, SIDE):
        arrived(zin.at[d - 1], z_s.at[d - 1], z_r.at[d - 1], z_peers[d - 1])
    own_rows = pl.ds(pl.multiple_of(col * 32, 32), 32)
    dx_out[...] = (
        dxp[own_rows, :].astype(F32) + zin[0].astype(F32) + zin[1].astype(F32) + zin[2].astype(F32)
    ).astype(BF)
    for n, block, base, to_right, to_left, f_s, r_s, l_s, a_t, b_t, l_v, r_v, acc, out in sides:
        arrived(l_v, rs_s.at[n, 2], rs_r.at[n, 2], to_left)
        arrived(r_v, rs_s.at[n, 3], rs_r.at[n, 3], to_right)

        def total(i, carry, acc=acc, l_v=l_v, r_v=r_v, out=out):
            out[i] = (acc[i] + l_v[i].astype(F32) + r_v[i].astype(F32)).astype(BF)
            return carry

        lax.fori_loop(0, SHARE, total, 0)
    for copy in started:
        copy.wait_send()


def backward(tables, pre, back, xt, ogb, wu):
    smem = pl.BlockSpec(memory_space=pltpu.SMEM)
    vmem = pl.BlockSpec(memory_space=pltpu.VMEM)

    def blocks(n, dtype=BF):
        return pltpu.VMEM((n, B, B), dtype)

    side = [blocks(SHARE)] * 3 + [blocks(SHARE // 2)] * 2 + [blocks(SHARE)] * 2 + [blocks(SHARE, F32)]
    dma = pltpu.SemaphoreType.DMA
    scratch = (
        [blocks(ROWS)] * 2
        + [blocks(COLS)] * 2
        + [blocks(ROWS)] * 6
        + [blocks(COLS)] * 6
        + [blocks(NBLK), blocks(NBLK), pltpu.VMEM((B, ROWS * B), BF), pltpu.VMEM((3, 32, ROWS * B), BF)]
        + side
        + side
        + [dma((4,))] * 2
        + [dma((4, 6))] * 2
        + [dma((2, 8))] * 2
        + [dma((2, 4))] * 2
        + [dma((3,))] * 2
        + [dma(())]
    )
    return pl.pallas_call(
        back_kernel,
        out_shape=[
            jax.ShapeDtypeStruct((32, ROWS * B), BF),
            jax.ShapeDtypeStruct((SHARE, B, B), BF),
            jax.ShapeDtypeStruct((SHARE, B, B), BF),
        ],
        in_specs=[smem] * 9 + [vmem] * 4 + [pl.BlockSpec(memory_space=pl.ANY)],
        out_specs=[vmem] * 3,
        scratch_shapes=scratch,
        compiler_params=pltpu.CompilerParams(
            collective_id=0, has_side_effects=True, vmem_limit_bytes=62 * 2**20
        ),
        name="backward",
    )(*tables, pre, back, xt, ogb, wu)


def shards(tokens_in, out_grad, up_weight, down_weight, up_blocks, down_blocks, owners):
    up, down, owner = up_blocks[0, 0], down_blocks[0, 0], owners[0, 0]
    slots = jnp.arange(NBLK, dtype=jnp.int32)
    at_owner = owner[None, :] == slots[:, None]
    up_owned = jnp.sum(jnp.where(at_owner, up[None, :], 0), axis=1)
    down_owned = jnp.sum(jnp.where(at_owner, down[None, :], 0), axis=1)
    rank = jnp.sum((up[None, :] < up[:, None]).astype(jnp.int32), axis=1)
    at_rank = rank[None, :] == slots[:, None]
    order = jnp.sum(jnp.where(at_rank, slots[None, :], 0), axis=1)
    ranked = jnp.sum(jnp.where(at_rank, up[None, :], 0), axis=1)
    feature = ranked // COLS
    keep = jnp.concatenate([jnp.zeros((1,), F32), (feature[1:] == feature[:-1]).astype(F32)])
    below = jnp.sum(
        (up[None, :] < (jnp.arange(ROWS, dtype=jnp.int32)[:, None] + 1) * COLS).astype(jnp.int32), axis=1
    )
    some = (below > jnp.concatenate([jnp.zeros((1,), jnp.int32), below[:-1]])).astype(F32)
    last = jnp.maximum(below - 1, 0)
    tables = (
        up_owned // COLS, up_owned % COLS, down_owned % ROWS, down_owned // ROWS,
        ranked % COLS, order, keep, last, some,
    )
    pre, back, xt, ogb = forward(
        up // COLS, up % COLS, down % ROWS, down // ROWS, tokens_in, out_grad, up_weight[0, 0], down_weight[0, 0]
    )
    input_grad, up_grad, down_grad = backward(tables, pre, back, xt, ogb, up_weight[0, 0])
    return input_grad, up_grad[None, None], down_grad[None, None]


def solution(mesh):
    placed = (
        P("dp", "row"),
        P("dp", "row"),
        P("row", "col", None, None, None),
        P("row", "col", None, None, None),
        P("row", "col", None),
        P("row", "col", None),
        P("row", "col", None),
    )
    return jax.shard_map(
        shards,
        mesh=mesh,
        in_specs=placed,
        out_specs=(
            P(("dp", "col"), "row"),
            P("row", "col", "dp", None, None),
            P("row", "col", "dp", None, None),
        ),
        check_vma=False,
    )
```

```python
import functools

import jax
import jax.numpy as jnp
from jax import lax
from jax.experimental import pallas as pl
from jax.experimental.pallas import tpu as pltpu
from jax.sharding import PartitionSpec as P

BF = jnp.bfloat16
F32 = jnp.float32
B = 128
ROWS = 24
COLS = 48
NBLK = 288
SIDE = 4
SHARE = 18
CH = 12
PAIRS = 168
WIDE = 384
NN = (((1,), (0,)), ((), ()))
NT = (((1,), (1,)), ((), ()))
MESH = pl.DeviceIdType.MESH

root_two_pi = 0.7978845608028654
cubic_coef = 0.044715


def activate(pre_sum, back_sum):
    square = pre_sum * pre_sum
    inner_arg = root_two_pi * (pre_sum + cubic_coef * square * pre_sum)
    tanh_inner = jnp.tanh(inner_arg)
    half = 0.5 * (1.0 + tanh_inner)
    slope = half + 0.5 * pre_sum * (1.0 - tanh_inner * tanh_inner) * root_two_pi * (
        1.0 + 3.0 * cubic_coef * square
    )
    return pre_sum * half, back_sum * slope


def dot(left, right, dims):
    return lax.dot_general(left, right, dims, preferred_element_type=F32)


def prepare_kernel(up_ref, dn_ref, own_ref, out_ref):
    def iota(shape, axis):
        return lax.broadcasted_iota(jnp.int32, shape, axis)

    square = (NBLK, NBLK)
    sub, lane = iota(square, 0), iota(square, 1)
    wide = iota((NBLK, WIDE), 1)
    one, zero = jnp.float32(1), jnp.float32(0)

    def count(mask, axis):
        return jnp.sum(jnp.where(mask, one, zero), axis=axis, keepdims=True)

    def column(row):
        picked = jnp.where(sub == lane, jnp.broadcast_to(row, square).astype(F32), zero)
        return jnp.sum(picked, axis=1, keepdims=True).astype(jnp.int32)

    def pairs(e_row, e_col, split, segment, operand):
        seg_row, seg_col = segment(e_row), segment(e_col)
        same = seg_col == seg_row
        turn = count(same & (lane < sub), 1).astype(jnp.int32)
        even = (turn & 1) == 0
        turn_row = count(same & (sub < lane), 0).astype(jnp.int32)
        even_row = (turn_row & 1) == 0
        offset = count((seg_row < seg_col) & even_row, 1).astype(jnp.int32)
        place = 2 * (offset + (turn >> 1)) + (turn & 1)
        block = NBLK - iota((NBLK, 1), 0)
        value = block * 64 + operand(e_col) + jnp.where(turn >= 2, 65536, 0)
        table = jnp.sum(jnp.where(place == wide, value.astype(F32), zero), axis=0, keepdims=True)
        through = count((seg_col <= wide) & even, 0)
        here = count((seg_col == wide) & even, 0)
        last = jnp.where(here > zero, through - one, jnp.float32(PAIRS))
        return table.astype(jnp.int32), last.astype(jnp.int32)

    up_row, dn_row, owner_row = up_ref[...], dn_ref[...], own_ref[...]
    up_col, dn_col, owner_col = column(up_row), column(dn_row), column(owner_row)

    def owned(value):
        picked = jnp.where(owner_col == wide, value.astype(F32), zero)
        return jnp.sum(picked, axis=0, keepdims=True).astype(jnp.int32)

    def div(value, by):
        return (value.astype(F32) * jnp.float32(1.0 / by) + jnp.float32(0.5 / by)).astype(jnp.int32)

    def rem(value, by):
        return value - div(value, by) * by

    t0, l0 = pairs(up_row, up_col, COLS, lambda e: rem(e, COLS), lambda e: div(e, COLS))
    t1, l1 = pairs(dn_row, dn_col, ROWS, lambda e: div(e, ROWS), lambda e: rem(e, ROWS))
    t2, l2 = pairs(up_row, up_col, COLS, lambda e: div(e, COLS), lambda e: rem(e, COLS))
    rows = (
        t0, t1, t2, l0, l1, l2,
        owned(div(up_col, COLS) * 64 + rem(up_col, COLS)),
        owned(rem(dn_col, ROWS) * 64 + div(dn_col, ROWS)),
    )
    for n, value in enumerate(rows):
        out_ref[n : n + 1, :] = value


def prepare(up, down, owner):
    return pl.pallas_call(
        prepare_kernel,
        out_shape=jax.ShapeDtypeStruct((8, WIDE), jnp.int32),
        name="prepare",
    )(up, down, owner)


def main_kernel(*refs):
    tab, x_hbm, g_hbm, wu_hbm, wd_hbm = refs[:5]
    dx_out, up_out, dn_out = refs[5:8]
    (
        x_in, og_own, xt_own, wu, wd, runs,
        pre_ref, back_ref, pre_to, back_to, pre_in, back_in, pg_own, ht_own,
        xt_l, xt_r, xt_o, og_l, og_r, og_o,
        pg_l, pg_r, pg_o, ht_l, ht_r, ht_o,
        dxp, zin,
        uf_s, ur_s, ul_s, ua_t, ub_t, ul_v, ur_v, u_acc,
        df_s, dr_s, dl_s, da_t, db_t, dl_v, dr_v, d_acc,
        ex_s, ex_r, ag_s, ag_r, pa_s, pa_r, rs_s, rs_r, z_s, z_r, in_s, col_s,
    ) = refs[8:]
    def column_loads(src, dst, n):
        return [
            pltpu.make_async_copy(src.at[:, pl.ds(f * B, B)], dst.at[f], col_s.at[n, f]) for f in range(ROWS)
        ]

    loads = [
        column_loads(g_hbm, og_own, 0),
        column_loads(x_hbm, x_in, 1),
        [pltpu.make_async_copy(wu_hbm, wu.at[pl.ds(0, NBLK)], in_s.at[0])],
        [pltpu.make_async_copy(wd_hbm, wd.at[pl.ds(0, NBLK)], in_s.at[1])],
    ]

    def loaded(n):
        for load in loads[n]:
            load.wait()

    for group in loads:
        for load in group:
            load.start()
    wu[NBLK] = jnp.zeros((B, B), BF)
    wd[NBLK] = jnp.zeros((B, B), BF)
    runs[PAIRS] = jnp.zeros((B, B), BF)
    dp, row, col = lax.axis_index("dp"), lax.axis_index("row"), lax.axis_index("col")
    y, x = dp // SIDE, dp % SIDE
    other = (dp, 1 - row, col)
    x_right = (y * SIDE + (x + 1) % SIDE, row, col)
    x_left = (y * SIDE + (x + 3) % SIDE, row, col)
    y_right = (((y + 1) % SIDE) * SIDE + x, row, col)
    y_left = (((y + 3) % SIDE) * SIDE + x, row, col)
    z_peers = [(dp, row, (col + d) % SIDE) for d in range(1, SIDE)]

    barrier = pltpu.get_barrier_semaphore()
    peers = [other, x_right, x_left, y_right, y_left] + z_peers
    for peer in peers:
        pl.semaphore_signal(barrier, inc=1, device_id=peer, device_id_type=MESH)
    pl.semaphore_wait(barrier, len(peers))

    started = []

    def send(src, dst, send_sem, recv_sem, peer):
        copy = pltpu.make_async_remote_copy(
            src_ref=src, dst_ref=dst, send_sem=send_sem, recv_sem=recv_sem, device_id=peer, device_id_type=MESH
        )
        copy.start()
        started.append(copy)

    def arrived(dst, send_sem, recv_sem, peer):
        pltpu.make_async_remote_copy(
            src_ref=dst, dst_ref=dst, send_sem=send_sem, recv_sem=recv_sem, device_id=peer, device_id_type=MESH
        ).wait_recv()

    kinds = {
        "xt": (0, xt_own, xt_l, xt_r, xt_o, x_right, x_left),
        "og": (1, og_own, og_l, og_r, og_o, y_right, y_left),
        "pg": (2, pg_own, pg_l, pg_r, pg_o, x_right, x_left),
        "ht": (3, ht_own, ht_l, ht_r, ht_o, y_right, y_left),
    }

    def part(kind, c, whose=row):
        return pl.ds((whose * ROWS if kind in ("pg", "ht") else 0) + c * CH, CH)

    def ring_out(kind, c, way):
        n, own, left, right, _, to_right, to_left = kinds[kind]
        at = part(kind, c)
        if way == "r":
            send(own.at[at], left.at[at], ag_s.at[n, c], ag_r.at[n, c], to_right)
        else:
            send(own.at[at], right.at[at], ag_s.at[n, 2 + c], ag_r.at[n, 2 + c], to_left)

    def ring_wait(kind, slot):
        n, _, left, right, far, to_right, to_left = kinds[kind]
        dst = (left, left, right, right, far, far)[slot].at[part(kind, slot % 2)]
        arrived(dst, ag_s.at[n, slot], ag_r.at[n, slot], to_right)

    def ring_forward(kind, way):
        n, _, left, right, far, to_right, to_left = kinds[kind]
        if way == "r":
            at = part(kind, 0)
            send(left.at[at], far.at[at], ag_s.at[n, 4], ag_r.at[n, 4], to_right)
        else:
            at = part(kind, 1)
            send(right.at[at], far.at[at], ag_s.at[n, 5], ag_r.at[n, 5], to_left)

    def pair_buffer(kind, slot):
        _, own, left, right, far, _, _ = kinds[kind]
        return (own, own, left, left, right, right, far, far)[slot]

    def pair_out(kind, slot):
        n = kinds[kind][0] - 2
        ref = pair_buffer(kind, slot).at[part(kind, slot % 2)]
        send(ref, ref, pa_s.at[n, slot], pa_r.at[n, slot], other)

    def pair_wait(kind, slot):
        n = kinds[kind][0] - 2
        ref = pair_buffer(kind, slot).at[part(kind, slot % 2, 1 - row)]
        arrived(ref, pa_s.at[n, slot], pa_r.at[n, slot], other)

    loaded(0)
    ring_out("og", 0, "r")
    ring_out("og", 1, "l")
    ring_out("og", 1, "r")
    ring_out("og", 0, "l")
    loaded(1)
    for f in range(ROWS):
        xt_own[f] = x_in[f].T
    ring_out("xt", 0, "r")
    ring_out("xt", 1, "l")
    ring_out("xt", 1, "r")
    ring_out("xt", 0, "l")

    def products(n, left, weights, axis, count, unroll):
        def body(i, total):
            parts = []
            for j in range(unroll):
                p = i * unroll + j
                first, second = tab[n, 2 * p], tab[n, 2 * p + 1]
                lhs = jnp.concatenate([left(first & 63), left(second & 63)], axis=1)
                rhs = jnp.concatenate(
                    [weights[NBLK - ((first >> 6) & 1023)], weights[NBLK - ((second >> 6) & 1023)]], axis=axis
                )
                parts.append(((first >> 16).astype(F32), dot(lhs, rhs, NT if axis else NN)))
            for j in range(unroll):
                total = total * parts[j][0] + parts[j][1]
                runs[i * unroll + j] = total.astype(BF)
            return total

        lax.fori_loop(0, count // unroll, body, jnp.zeros((B, B), F32))

    def exchange(n, to, mine, into):
        def pick(i, carry):
            for j in range(6):
                at = i * 6 + j
                to[at] = runs[tab[3 + n, (1 - row) * ROWS + at]]
            return carry

        def own(i, carry):
            for j in range(6):
                at = i * 6 + j
                mine[at] = runs[tab[3 + n, row * ROWS + at]]
            return carry

        for c in range(2):
            lax.fori_loop(2 * c, 2 * c + 2, pick, 0)
            here = pl.ds(c * CH, CH)
            send(to.at[here], into.at[here], ex_s.at[2 * n + c], ex_r.at[2 * n + c], other)
        lax.fori_loop(0, 4, own, 0)

    loaded(2)
    products(0, lambda f: x_in[f], wu, 0, PAIRS, 12)
    exchange(0, pre_to, pre_ref, pre_in)
    for kind in ("og", "xt"):
        ring_wait(kind, 0)
        ring_forward(kind, "r")
        ring_wait(kind, 3)
        ring_forward(kind, "l")
    loaded(3)
    products(1, lambda f: og_own[f], wd, 1, PAIRS, 12)
    exchange(1, back_to, back_ref, back_in)

    for c in range(2):
        here = pl.ds(c * CH, CH)
        arrived(pre_in.at[here], ex_s.at[c], ex_r.at[c], other)
        arrived(back_in.at[here], ex_s.at[2 + c], ex_r.at[2 + c], other)

        def one(i, carry, c=c):
            mine = row * ROWS + c * CH + i
            pre = pre_ref[c * CH + i].astype(F32) + pre_in[c * CH + i].astype(F32)
            back = back_ref[c * CH + i].astype(F32) + back_in[c * CH + i].astype(F32)
            hidden, pre_grad = activate(pre, back)
            pg_own[mine] = pre_grad.astype(BF)
            ht_own[mine] = hidden.astype(BF).T
            return carry

        lax.fori_loop(0, CH, one, 0)
        for kind in ("pg", "ht"):
            pair_out(kind, c)
    for kind in ("pg", "ht"):
        ring_out(kind, 0, "r")
        ring_out(kind, 1, "l")
    for kind in ("pg", "ht"):
        ring_out(kind, 1, "r")
        ring_out(kind, 0, "l")

    pair_wait("pg", 0)
    pair_wait("pg", 1)
    products(2, lambda h: pg_own[h], wu, 1, 156, 12)
    for f in range(ROWS):
        dxp[:, f * B : (f + 1) * B] = runs[tab[5, f]]
    for d in range(1, SIDE):
        theirs = pl.ds(pl.multiple_of(((col + d) % SIDE) * 32, 32), 32)
        send(dxp.at[theirs], zin.at[d - 1], z_s.at[d - 1], z_r.at[d - 1], z_peers[d - 1])

    for kind in ("xt", "og"):
        for slot in (1, 2):
            ring_wait(kind, slot)
    for kind in ("pg", "ht"):
        ring_wait(kind, 0)
        ring_forward(kind, "r")
        pair_out(kind, 2)
        ring_wait(kind, 3)
        ring_forward(kind, "l")
        pair_out(kind, 5)
    for kind in ("pg", "ht"):
        ring_wait(kind, 1)
        pair_out(kind, 3)
        ring_wait(kind, 2)
        pair_out(kind, 4)
    for kind in ("xt", "og"):
        for slot in (4, 5):
            ring_wait(kind, slot)
    for slot in (4, 5):
        for kind in ("pg", "ht"):
            ring_wait(kind, slot)
            pair_out(kind, slot + 2)
    for kind in ("ht",):
        for slot in range(2):
            pair_wait(kind, slot)
    for slot in range(2, 8):
        for kind in ("pg", "ht"):
            pair_wait(kind, slot)

    def up_block(s):
        e = tab[6, s]
        f, h = e >> 6, e & 63
        left = jnp.concatenate([xt_own[f], xt_l[f], xt_r[f], xt_o[f]], axis=1)
        right = jnp.concatenate([pg_own[h], pg_l[h], pg_r[h], pg_o[h]], axis=0)
        return dot(left, right, NN)

    def dn_block(s):
        e = tab[7, s]
        f, h = e >> 6, e & 63
        left = jnp.concatenate([ht_own[h], ht_l[h], ht_r[h], ht_o[h]], axis=1)
        right = jnp.concatenate([og_own[f], og_l[f], og_r[f], og_o[f]], axis=0)
        return dot(left, right, NN)

    def up_base(d):
        return ((y + d) % SIDE) * (SIDE * SHARE) + x * SHARE

    def dn_base(d):
        return y * (SIDE * SHARE) + ((x + d) % SIDE) * SHARE

    half = SHARE // 2

    def fill(block, base, out, first, added=None):
        def body(i, carry):
            for j in range(9):
                at = first + i * 9 + j
                value = block(base + at)
                if added is not None:
                    value = value + added[i * 9 + j].astype(F32)
                out[at] = value.astype(out.dtype)
            return carry

        lax.fori_loop(0, half // 9, body, 0)

    sides = (
        (0, up_block, up_base, y_right, y_left, uf_s, ur_s, ul_s, ua_t, ub_t, ul_v, ur_v, u_acc, up_out),
        (1, dn_block, dn_base, x_right, x_left, df_s, dr_s, dl_s, da_t, db_t, dl_v, dr_v, d_acc, dn_out),
    )
    for n, block, base, to_right, to_left, f_s, r_s, l_s, a_t, b_t, l_v, r_v, acc, out in sides:
        fill(block, base(2), f_s, 0)
        send(f_s.at[pl.ds(0, half)], a_t, rs_s.at[n, 0], rs_r.at[n, 0], to_right)
        fill(block, base(2), f_s, half)
        send(f_s.at[pl.ds(half, half)], b_t, rs_s.at[n, 1], rs_r.at[n, 1], to_left)
    for n, block, base, to_right, to_left, f_s, r_s, l_s, a_t, b_t, l_v, r_v, acc, out in sides:
        fill(block, base(1), r_s, half)
        arrived(a_t, rs_s.at[n, 0], rs_r.at[n, 0], to_left)
        fill(block, base(1), r_s, 0, a_t)
        send(r_s, l_v, rs_s.at[n, 2], rs_r.at[n, 2], to_right)
        fill(block, base(3), l_s, 0)
        arrived(b_t, rs_s.at[n, 1], rs_r.at[n, 1], to_right)
        fill(block, base(3), l_s, half, b_t)
        send(l_s, r_v, rs_s.at[n, 3], rs_r.at[n, 3], to_left)
    for n, block, base, to_right, to_left, f_s, r_s, l_s, a_t, b_t, l_v, r_v, acc, out in sides:
        fill(block, base(0), acc, 0)
        fill(block, base(0), acc, half)

    for d in range(1, SIDE):
        arrived(zin.at[d - 1], z_s.at[d - 1], z_r.at[d - 1], z_peers[d - 1])
    own_rows = pl.ds(pl.multiple_of(col * 32, 32), 32)
    dx_out[...] = (
        dxp[own_rows, :].astype(F32) + zin[0].astype(F32) + zin[1].astype(F32) + zin[2].astype(F32)
    ).astype(BF)
    for n, block, base, to_right, to_left, f_s, r_s, l_s, a_t, b_t, l_v, r_v, acc, out in sides:
        arrived(l_v, rs_s.at[n, 2], rs_r.at[n, 2], to_left)
        arrived(r_v, rs_s.at[n, 3], rs_r.at[n, 3], to_right)

        def total(i, carry, acc=acc, l_v=l_v, r_v=r_v, out=out):
            out[i] = (acc[i] + l_v[i].astype(F32) + r_v[i].astype(F32)).astype(BF)
            return carry

        lax.fori_loop(0, SHARE, total, 0)
    for copy in started:
        copy.wait_send()


def main(table, x, g, wu, wd):
    vmem = pl.BlockSpec(memory_space=pltpu.VMEM)
    far = pl.BlockSpec(memory_space=pl.ANY)

    def blocks(n, dtype=BF):
        return pltpu.VMEM((n, B, B), dtype)

    tokens = pltpu.VMEM((B, ROWS * B), BF)
    side = [blocks(SHARE)] * 3 + [blocks(SHARE // 2)] * 2 + [blocks(SHARE)] * 2 + [blocks(SHARE, F32)]
    dma = pltpu.SemaphoreType.DMA
    scratch = (
        [blocks(ROWS)] * 3 + [blocks(NBLK + 1), blocks(NBLK + 1), blocks(PAIRS + 1)]
        + [blocks(ROWS)] * 6
        + [blocks(COLS)] * 2
        + [blocks(ROWS)] * 3
        + [blocks(ROWS)] * 3
        + [blocks(COLS)] * 6
        + [tokens, pltpu.VMEM((3, 32, ROWS * B), BF)]
        + side
        + side
        + [dma((4,))] * 2
        + [dma((4, 6))] * 2
        + [dma((2, 8))] * 2
        + [dma((2, 4))] * 2
        + [dma((3,))] * 2
        + [dma((2,)), dma((2, ROWS))]
    )
    return pl.pallas_call(
        main_kernel,
        out_shape=[
            jax.ShapeDtypeStruct((32, ROWS * B), BF),
            jax.ShapeDtypeStruct((SHARE, B, B), BF),
            jax.ShapeDtypeStruct((SHARE, B, B), BF),
        ],
        in_specs=[pl.BlockSpec(memory_space=pltpu.SMEM)] + [far] * 4,
        out_specs=[vmem] * 3,
        scratch_shapes=scratch,
        compiler_params=pltpu.CompilerParams(
            collective_id=0, has_side_effects=True, vmem_limit_bytes=62 * 2**20
        ),
        name="backward",
    )(table, x, g, wu, wd)


def shards(tokens_in, out_grad, up_weight, down_weight, up_blocks, down_blocks, owners):
    table = prepare(up_blocks[0], down_blocks[0], owners[0])
    input_grad, up_grad, down_grad = main(table, tokens_in, out_grad, up_weight[0, 0], down_weight[0, 0])
    return input_grad, up_grad[None, None], down_grad[None, None]


def solution(mesh):
    placed = (
        P("dp", "row"),
        P("dp", "row"),
        P("row", "col", None, None, None),
        P("row", "col", None, None, None),
        P("row", "col", None),
        P("row", "col", None),
        P("row", "col", None),
    )
    return jax.shard_map(
        shards,
        mesh=mesh,
        in_specs=placed,
        out_specs=(
            P(("dp", "col"), "row"),
            P("row", "col", "dp", None, None),
            P("row", "col", "dp", None, None),
        ),
        check_vma=False,
    )
```

```python
import functools

import jax
import jax.numpy as jnp
from jax import lax
from jax.experimental import pallas as pl
from jax.experimental.pallas import tpu as pltpu
from jax.sharding import PartitionSpec as P

BF = jnp.bfloat16
F32 = jnp.float32
B = 128
ROWS = 24
COLS = 48
NBLK = 288
SIDE = 4
SHARE = 18
CH = 12
PAIRS = 168
WIDE = 384
NN = (((1,), (0,)), ((), ()))
NT = (((1,), (1,)), ((), ()))
MESH = pl.DeviceIdType.MESH

root_two_pi = 0.7978845608028654
cubic_coef = 0.044715


def activate(pre_sum, back_sum):
    square = pre_sum * pre_sum
    inner_arg = root_two_pi * (pre_sum + cubic_coef * square * pre_sum)
    tanh_inner = jnp.tanh(inner_arg)
    half = 0.5 * (1.0 + tanh_inner)
    slope = half + 0.5 * pre_sum * (1.0 - tanh_inner * tanh_inner) * root_two_pi * (
        1.0 + 3.0 * cubic_coef * square
    )
    return pre_sum * half, back_sum * slope


def dot(left, right, dims):
    return lax.dot_general(left, right, dims, preferred_element_type=F32)


def prepare_kernel(up_ref, dn_ref, own_ref, out_ref):
    def iota(shape, axis):
        return lax.broadcasted_iota(jnp.int32, shape, axis)

    square = (NBLK, NBLK)
    sub, lane = iota(square, 0), iota(square, 1)
    wide = iota((NBLK, WIDE), 1)
    one, zero = jnp.float32(1), jnp.float32(0)

    def count(mask, axis):
        return jnp.sum(jnp.where(mask, one, zero), axis=axis, keepdims=True)

    def column(row):
        picked = jnp.where(sub == lane, jnp.broadcast_to(row, square).astype(F32), zero)
        return jnp.sum(picked, axis=1, keepdims=True).astype(jnp.int32)

    def pairs(e_row, e_col, split, segment, operand):
        seg_row, seg_col = segment(e_row), segment(e_col)
        same = seg_col == seg_row
        turn = count(same & (lane < sub), 1).astype(jnp.int32)
        even = (turn & 1) == 0
        turn_row = count(same & (sub < lane), 0).astype(jnp.int32)
        even_row = (turn_row & 1) == 0
        offset = count((seg_row < seg_col) & even_row, 1).astype(jnp.int32)
        place = 2 * (offset + (turn >> 1)) + (turn & 1)
        block = NBLK - iota((NBLK, 1), 0)
        value = block * 64 + operand(e_col) + jnp.where(turn >= 2, 65536, 0)
        table = jnp.sum(jnp.where(place == wide, value.astype(F32), zero), axis=0, keepdims=True)
        through = count((seg_col <= wide) & even, 0)
        here = count((seg_col == wide) & even, 0)
        last = jnp.where(here > zero, through - one, jnp.float32(PAIRS))
        return table.astype(jnp.int32), last.astype(jnp.int32)

    up_row, dn_row, owner_row = up_ref[...], dn_ref[...], own_ref[...]
    up_col, dn_col, owner_col = column(up_row), column(dn_row), column(owner_row)

    def owned(value):
        picked = jnp.where(owner_col == wide, value.astype(F32), zero)
        return jnp.sum(picked, axis=0, keepdims=True).astype(jnp.int32)

    def div(value, by):
        return (value.astype(F32) * jnp.float32(1.0 / by) + jnp.float32(0.5 / by)).astype(jnp.int32)

    def rem(value, by):
        return value - div(value, by) * by

    t0, l0 = pairs(up_row, up_col, COLS, lambda e: rem(e, COLS), lambda e: div(e, COLS))
    t1, l1 = pairs(dn_row, dn_col, ROWS, lambda e: div(e, ROWS), lambda e: rem(e, ROWS))
    t2, l2 = pairs(up_row, up_col, COLS, lambda e: div(e, COLS), lambda e: rem(e, COLS))
    rows = (
        t0, t1, t2, l0, l1, l2,
        owned(div(up_col, COLS) * 64 + rem(up_col, COLS)),
        owned(rem(dn_col, ROWS) * 64 + div(dn_col, ROWS)),
    )
    for n, value in enumerate(rows):
        out_ref[n : n + 1, :] = value


def prepare(up, down, owner):
    return pl.pallas_call(
        prepare_kernel,
        out_shape=jax.ShapeDtypeStruct((8, WIDE), jnp.int32),
        name="prepare",
    )(up, down, owner)


def main_kernel(*refs):
    tab, x_hbm, g_hbm, wu_hbm, wd_hbm = refs[:5]
    dx_out, up_out, dn_out = refs[5:8]
    (
        x_in, og_own, xt_own, wu, wd, runs,
        pre_ref, back_ref, pre_to, back_to, pre_in, back_in, pg_own, ht_own,
        xt_l, xt_r, xt_o, og_l, og_r, og_o,
        pg_l, pg_r, pg_o, ht_l, ht_r, ht_o,
        dxp, zin,
        uf_s, ur_s, ul_s, ua_t, ub_t, ul_v, ur_v, u_acc,
        df_s, dr_s, dl_s, da_t, db_t, dl_v, dr_v, d_acc,
        ex_s, ex_r, ag_s, ag_r, pa_s, pa_r, rs_s, rs_r, z_s, z_r, in_s, col_s,
    ) = refs[8:]
    dp, row, col = lax.axis_index("dp"), lax.axis_index("row"), lax.axis_index("col")
    y, x = dp // SIDE, dp % SIDE
    other = (dp, 1 - row, col)
    x_right = (y * SIDE + (x + 1) % SIDE, row, col)
    x_left = (y * SIDE + (x + 3) % SIDE, row, col)
    y_right = (((y + 1) % SIDE) * SIDE + x, row, col)
    y_left = (((y + 3) % SIDE) * SIDE + x, row, col)
    z_peers = [(dp, row, (col + d) % SIDE) for d in range(1, SIDE)]

    barrier = pltpu.get_barrier_semaphore()
    peers = [other, x_right, x_left, y_right, y_left] + z_peers
    for peer in peers:
        pl.semaphore_signal(barrier, inc=1, device_id=peer, device_id_type=MESH)

    def column_loads(src, dst, n):
        return [
            pltpu.make_async_copy(src.at[:, pl.ds(f * B, B)], dst.at[f], col_s.at[n, f]) for f in range(ROWS)
        ]

    loads = [
        column_loads(g_hbm, og_own, 0),
        column_loads(x_hbm, x_in, 1),
        [pltpu.make_async_copy(wu_hbm, wu.at[pl.ds(0, NBLK)], in_s.at[0])],
        [pltpu.make_async_copy(wd_hbm, wd.at[pl.ds(0, NBLK)], in_s.at[1])],
    ]

    def loaded(n):
        for load in loads[n]:
            load.wait()

    for group in loads:
        for load in group:
            load.start()
    wu[NBLK] = jnp.zeros((B, B), BF)
    wd[NBLK] = jnp.zeros((B, B), BF)
    runs[PAIRS] = jnp.zeros((B, B), BF)

    started = []

    def send(src, dst, send_sem, recv_sem, peer):
        copy = pltpu.make_async_remote_copy(
            src_ref=src, dst_ref=dst, send_sem=send_sem, recv_sem=recv_sem, device_id=peer, device_id_type=MESH
        )
        copy.start()
        started.append(copy)

    def arrived(dst, send_sem, recv_sem, peer):
        pltpu.make_async_remote_copy(
            src_ref=dst, dst_ref=dst, send_sem=send_sem, recv_sem=recv_sem, device_id=peer, device_id_type=MESH
        ).wait_recv()

    kinds = {
        "xt": (0, xt_own, xt_l, xt_r, xt_o, x_right, x_left),
        "og": (1, og_own, og_l, og_r, og_o, y_right, y_left),
        "pg": (2, pg_own, pg_l, pg_r, pg_o, x_right, x_left),
        "ht": (3, ht_own, ht_l, ht_r, ht_o, y_right, y_left),
    }

    def part(kind, c, whose=row):
        return pl.ds((whose * ROWS if kind in ("pg", "ht") else 0) + c * CH, CH)

    def ring_out(kind, c, way):
        n, own, left, right, _, to_right, to_left = kinds[kind]
        at = part(kind, c)
        if way == "r":
            send(own.at[at], left.at[at], ag_s.at[n, c], ag_r.at[n, c], to_right)
        else:
            send(own.at[at], right.at[at], ag_s.at[n, 2 + c], ag_r.at[n, 2 + c], to_left)

    def spot(kind, slot, whose=row):
        _, own, left, right, far, _, _ = kinds[kind]
        buffer = (own, own, left, left, right, right, far, far, far, far)[slot]
        if slot < 6:
            return buffer.at[part(kind, slot % 2, whose)]
        base = whose * ROWS if kind in ("pg", "ht") else 0
        return buffer.at[pl.ds(base + (slot - 6) * (CH // 2), CH // 2)]

    def ring_wait(kind, slot):
        n, to_right = kinds[kind][0], kinds[kind][5]
        arrived(spot(kind, slot + 2), ag_s.at[n, slot], ag_r.at[n, slot], to_right)

    def ring_forward(kind, way):
        n, _, left, right, far, to_right, to_left = kinds[kind]
        base = row * ROWS if kind in ("pg", "ht") else 0
        source, first, peer = (left, 4, to_right) if way == "r" else (right, 6, to_left)
        for slot in (first, first + 1):
            at = pl.ds(base + (slot - 4) * (CH // 2), CH // 2)
            send(source.at[at], far.at[at], ag_s.at[n, slot], ag_r.at[n, slot], peer)

    def pair_out(kind, slot):
        n = kinds[kind][0] - 2
        ref = spot(kind, slot)
        send(ref, ref, pa_s.at[n, slot], pa_r.at[n, slot], other)

    def pair_wait(kind, slot):
        n = kinds[kind][0] - 2
        ref = spot(kind, slot, 1 - row)
        arrived(ref, pa_s.at[n, slot], pa_r.at[n, slot], other)

    loaded(1)
    for f in range(ROWS):
        xt_own[f] = x_in[f].T

    def products(n, left, weights, axis, count, unroll):
        def body(i, total):
            parts = []
            for j in range(unroll):
                p = i * unroll + j
                first, second = tab[n, 2 * p], tab[n, 2 * p + 1]
                lhs = jnp.concatenate([left(first & 63), left(second & 63)], axis=1)
                rhs = jnp.concatenate(
                    [weights[NBLK - ((first >> 6) & 1023)], weights[NBLK - ((second >> 6) & 1023)]], axis=axis
                )
                parts.append(((first >> 16).astype(F32), dot(lhs, rhs, NT if axis else NN)))
            for j in range(unroll):
                total = total * parts[j][0] + parts[j][1]
                runs[i * unroll + j] = total.astype(BF)
            return total

        lax.fori_loop(0, count // unroll, body, jnp.zeros((B, B), F32))

    def exchange(n, to, mine, into):
        def pick(i, carry):
            for j in range(6):
                at = i * 6 + j
                to[at] = runs[tab[3 + n, (1 - row) * ROWS + at]]
            return carry

        def own(i, carry):
            for j in range(6):
                at = i * 6 + j
                mine[at] = runs[tab[3 + n, row * ROWS + at]]
            return carry

        for c in range(2):
            lax.fori_loop(2 * c, 2 * c + 2, pick, 0)
            here = pl.ds(c * CH, CH)
            send(to.at[here], into.at[here], ex_s.at[2 * n + c], ex_r.at[2 * n + c], other)
        lax.fori_loop(0, 4, own, 0)

    loaded(2)
    products(0, lambda f: x_in[f], wu, 0, PAIRS, 12)
    loaded(0)
    pl.semaphore_wait(barrier, len(peers))
    for kind in ("og", "xt"):
        ring_out(kind, 0, "r")
        ring_out(kind, 1, "l")
    for kind in ("og", "xt"):
        ring_out(kind, 1, "r")
        ring_out(kind, 0, "l")
    exchange(0, pre_to, pre_ref, pre_in)
    loaded(3)
    products(1, lambda f: og_own[f], wd, 1, PAIRS, 12)
    exchange(1, back_to, back_ref, back_in)
    for kind in ("og", "xt"):
        ring_wait(kind, 0)
        ring_forward(kind, "r")
        ring_wait(kind, 3)
        ring_forward(kind, "l")

    for c in range(2):
        here = pl.ds(c * CH, CH)
        arrived(pre_in.at[here], ex_s.at[c], ex_r.at[c], other)
        arrived(back_in.at[here], ex_s.at[2 + c], ex_r.at[2 + c], other)

        def one(i, carry, c=c):
            mine = row * ROWS + c * CH + i
            pre = pre_ref[c * CH + i].astype(F32) + pre_in[c * CH + i].astype(F32)
            back = back_ref[c * CH + i].astype(F32) + back_in[c * CH + i].astype(F32)
            hidden, pre_grad = activate(pre, back)
            pg_own[mine] = pre_grad.astype(BF)
            ht_own[mine] = hidden.astype(BF).T
            return carry

        lax.fori_loop(0, CH, one, 0)
        for kind in ("pg", "ht"):
            ring_out(kind, c, "rl"[c])
            pair_out(kind, c)
    for kind in ("pg", "ht"):
        ring_out(kind, 1, "r")
        ring_out(kind, 0, "l")

    pair_wait("pg", 0)
    pair_wait("pg", 1)
    products(2, lambda h: pg_own[h], wu, 1, 156, 12)
    for f in range(ROWS):
        dxp[:, f * B : (f + 1) * B] = runs[tab[5, f]]
    for d in range(1, SIDE):
        theirs = pl.ds(pl.multiple_of(((col + d) % SIDE) * 32, 32), 32)
        send(dxp.at[theirs], zin.at[d - 1], z_s.at[d - 1], z_r.at[d - 1], z_peers[d - 1])

    for kind in ("xt", "og"):
        for slot in (1, 2):
            ring_wait(kind, slot)
    for kind in ("pg", "ht"):
        ring_wait(kind, 0)
        ring_forward(kind, "r")
        pair_out(kind, 2)
        ring_wait(kind, 3)
        ring_forward(kind, "l")
        pair_out(kind, 5)
    for kind in ("pg", "ht"):
        ring_wait(kind, 1)
        pair_out(kind, 3)
        ring_wait(kind, 2)
        pair_out(kind, 4)
    for kind in ("xt", "og"):
        for slot in (4, 5, 6, 7):
            ring_wait(kind, slot)
    for slot in (4, 6, 5, 7):
        for kind in ("pg", "ht"):
            ring_wait(kind, slot)
            pair_out(kind, slot + 2)
    for kind in ("ht",):
        for slot in range(2):
            pair_wait(kind, slot)
    for slot in range(2, 10):
        for kind in ("pg", "ht"):
            pair_wait(kind, slot)

    def up_block(s):
        e = tab[6, s]
        f, h = e >> 6, e & 63
        left = jnp.concatenate([xt_own[f], xt_l[f], xt_r[f], xt_o[f]], axis=1)
        right = jnp.concatenate([pg_own[h], pg_l[h], pg_r[h], pg_o[h]], axis=0)
        return dot(left, right, NN)

    def dn_block(s):
        e = tab[7, s]
        f, h = e >> 6, e & 63
        left = jnp.concatenate([ht_own[h], ht_l[h], ht_r[h], ht_o[h]], axis=1)
        right = jnp.concatenate([og_own[f], og_l[f], og_r[f], og_o[f]], axis=0)
        return dot(left, right, NN)

    def up_base(d):
        return ((y + d) % SIDE) * (SIDE * SHARE) + x * SHARE

    def dn_base(d):
        return y * (SIDE * SHARE) + ((x + d) % SIDE) * SHARE

    half = SHARE // 2
    early, late = pl.ds(0, half), pl.ds(half, half)

    def fill(block, base, out, first, added=None):
        def body(i, carry):
            for j in range(9):
                at = first + i * 9 + j
                value = block(base + at)
                if added is not None:
                    value = value + added[i * 9 + j].astype(F32)
                out[at] = value.astype(out.dtype)
            return carry

        lax.fori_loop(0, half // 9, body, 0)

    sides = (
        (0, up_block, up_base, y_right, y_left, uf_s, ur_s, ul_s, ua_t, ub_t, ul_v, ur_v, u_acc, up_out),
        (1, dn_block, dn_base, x_right, x_left, df_s, dr_s, dl_s, da_t, db_t, dl_v, dr_v, d_acc, dn_out),
    )
    for n, block, base, to_right, to_left, f_s, r_s, l_s, a_t, b_t, l_v, r_v, acc, out in sides:
        fill(block, base(2), f_s, 0)
        send(f_s.at[early], a_t, rs_s.at[n, 0], rs_r.at[n, 0], to_right)
        fill(block, base(2), f_s, half)
        send(f_s.at[late], b_t, rs_s.at[n, 1], rs_r.at[n, 1], to_left)
    for n, block, base, to_right, to_left, f_s, r_s, l_s, a_t, b_t, l_v, r_v, acc, out in sides:
        fill(block, base(1), r_s, half)
        send(r_s.at[late], l_v.at[late], rs_s.at[n, 2], rs_r.at[n, 2], to_right)
        fill(block, base(3), l_s, 0)
        send(l_s.at[early], r_v.at[early], rs_s.at[n, 3], rs_r.at[n, 3], to_left)
    for n, block, base, to_right, to_left, f_s, r_s, l_s, a_t, b_t, l_v, r_v, acc, out in sides:
        arrived(a_t, rs_s.at[n, 0], rs_r.at[n, 0], to_left)
        fill(block, base(1), r_s, 0, a_t)
        send(r_s.at[early], l_v.at[early], rs_s.at[n, 4], rs_r.at[n, 4], to_right)
        arrived(b_t, rs_s.at[n, 1], rs_r.at[n, 1], to_right)
        fill(block, base(3), l_s, half, b_t)
        send(l_s.at[late], r_v.at[late], rs_s.at[n, 5], rs_r.at[n, 5], to_left)
    for n, block, base, to_right, to_left, f_s, r_s, l_s, a_t, b_t, l_v, r_v, acc, out in sides:
        fill(block, base(0), acc, 0)
        fill(block, base(0), acc, half)

    for d in range(1, SIDE):
        arrived(zin.at[d - 1], z_s.at[d - 1], z_r.at[d - 1], z_peers[d - 1])
    own_rows = pl.ds(pl.multiple_of(col * 32, 32), 32)
    dx_out[...] = (
        dxp[own_rows, :].astype(F32) + zin[0].astype(F32) + zin[1].astype(F32) + zin[2].astype(F32)
    ).astype(BF)
    for n, block, base, to_right, to_left, f_s, r_s, l_s, a_t, b_t, l_v, r_v, acc, out in sides:
        arrived(l_v.at[late], rs_s.at[n, 2], rs_r.at[n, 2], to_left)
        arrived(r_v.at[early], rs_s.at[n, 3], rs_r.at[n, 3], to_right)
        arrived(l_v.at[early], rs_s.at[n, 4], rs_r.at[n, 4], to_left)
        arrived(r_v.at[late], rs_s.at[n, 5], rs_r.at[n, 5], to_right)

        def total(i, carry, acc=acc, l_v=l_v, r_v=r_v, out=out):
            out[i] = (acc[i] + l_v[i].astype(F32) + r_v[i].astype(F32)).astype(BF)
            return carry

        lax.fori_loop(0, SHARE, total, 0)
    for copy in started:
        copy.wait_send()


def main(table, x, g, wu, wd):
    vmem = pl.BlockSpec(memory_space=pltpu.VMEM)
    far = pl.BlockSpec(memory_space=pl.ANY)

    def blocks(n, dtype=BF):
        return pltpu.VMEM((n, B, B), dtype)

    tokens = pltpu.VMEM((B, ROWS * B), BF)
    side = [blocks(SHARE)] * 3 + [blocks(SHARE // 2)] * 2 + [blocks(SHARE)] * 2 + [blocks(SHARE, F32)]
    dma = pltpu.SemaphoreType.DMA
    scratch = (
        [blocks(ROWS)] * 3 + [blocks(NBLK + 1), blocks(NBLK + 1), blocks(PAIRS + 1)]
        + [blocks(ROWS)] * 6
        + [blocks(COLS)] * 2
        + [blocks(ROWS)] * 3
        + [blocks(ROWS)] * 3
        + [blocks(COLS)] * 6
        + [tokens, pltpu.VMEM((3, 32, ROWS * B), BF)]
        + side
        + side
        + [dma((4,))] * 2
        + [dma((4, 8))] * 2
        + [dma((2, 10))] * 2
        + [dma((2, 6))] * 2
        + [dma((3,))] * 2
        + [dma((2,)), dma((2, ROWS))]
    )
    return pl.pallas_call(
        main_kernel,
        out_shape=[
            jax.ShapeDtypeStruct((32, ROWS * B), BF),
            jax.ShapeDtypeStruct((SHARE, B, B), BF),
            jax.ShapeDtypeStruct((SHARE, B, B), BF),
        ],
        in_specs=[pl.BlockSpec(memory_space=pltpu.SMEM)] + [far] * 4,
        out_specs=[vmem] * 3,
        scratch_shapes=scratch,
        compiler_params=pltpu.CompilerParams(
            collective_id=0, has_side_effects=True, vmem_limit_bytes=62 * 2**20
        ),
        name="backward",
    )(table, x, g, wu, wd)


def results_kernel(*refs):
    count = len(refs) // 2
    sems = refs[-1]
    copies = [pltpu.make_async_copy(refs[n], refs[count + n], sems.at[n]) for n in range(count)]
    for copy in copies:
        copy.start()
    for copy in copies:
        copy.wait()


def results(*values):
    far = pl.BlockSpec(memory_space=pl.ANY)
    return pl.pallas_call(
        results_kernel,
        out_shape=[jax.ShapeDtypeStruct(value.shape, value.dtype) for value in values],
        in_specs=[far] * len(values),
        out_specs=[far] * len(values),
        scratch_shapes=[pltpu.SemaphoreType.DMA((len(values),))],
        name="results",
    )(*values)


def shards(tokens_in, out_grad, up_weight, down_weight, up_blocks, down_blocks, owners):
    table = prepare(up_blocks[0], down_blocks[0], owners[0])
    input_grad, up_grad, down_grad = results(
        *main(table, tokens_in, out_grad, up_weight[0, 0], down_weight[0, 0])
    )
    return input_grad, up_grad[None, None], down_grad[None, None]


def solution(mesh):
    placed = (
        P("dp", "row"),
        P("dp", "row"),
        P("row", "col", None, None, None),
        P("row", "col", None, None, None),
        P("row", "col", None),
        P("row", "col", None),
        P("row", "col", None),
    )
    return jax.shard_map(
        shards,
        mesh=mesh,
        in_specs=placed,
        out_specs=(
            P(("dp", "col"), "row"),
            P("row", "col", "dp", None, None),
            P("row", "col", "dp", None, None),
        ),
        check_vma=False,
    )
```

```python
import functools

import jax
import jax.numpy as jnp
from jax import lax
from jax.experimental import pallas as pl
from jax.experimental.pallas import tpu as pltpu
from jax.sharding import PartitionSpec as P

BF = jnp.bfloat16
F32 = jnp.float32
B = 128
ROWS = 24
COLS = 48
NBLK = 288
SIDE = 4
SHARE = 18
CH = 12
PAIRS = 168
WIDE = 384
NN = (((1,), (0,)), ((), ()))
NT = (((1,), (1,)), ((), ()))
MESH = pl.DeviceIdType.MESH

root_two_pi = 0.7978845608028654
cubic_coef = 0.044715


def activate(pre_sum, back_sum):
    square = pre_sum * pre_sum
    inner_arg = root_two_pi * (pre_sum + cubic_coef * square * pre_sum)
    tanh_inner = jnp.tanh(inner_arg)
    half = 0.5 * (1.0 + tanh_inner)
    slope = half + 0.5 * pre_sum * (1.0 - tanh_inner * tanh_inner) * root_two_pi * (
        1.0 + 3.0 * cubic_coef * square
    )
    return pre_sum * half, back_sum * slope


def dot(left, right, dims):
    return lax.dot_general(left, right, dims, preferred_element_type=F32)


def prepare_kernel(up_ref, dn_ref, own_ref, out_ref):
    def iota(shape, axis):
        return lax.broadcasted_iota(jnp.int32, shape, axis)

    square = (NBLK, NBLK)
    sub, lane = iota(square, 0), iota(square, 1)
    wide = iota((NBLK, WIDE), 1)
    one, zero = jnp.float32(1), jnp.float32(0)

    def count(mask, axis):
        return jnp.sum(jnp.where(mask, one, zero), axis=axis, keepdims=True)

    def column(row):
        picked = jnp.where(sub == lane, jnp.broadcast_to(row, square).astype(F32), zero)
        return jnp.sum(picked, axis=1, keepdims=True).astype(jnp.int32)

    def pairs(e_row, e_col, split, segment, operand):
        seg_row, seg_col = segment(e_row), segment(e_col)
        same = seg_col == seg_row
        turn = count(same & (lane < sub), 1).astype(jnp.int32)
        even = (turn & 1) == 0
        turn_row = count(same & (sub < lane), 0).astype(jnp.int32)
        even_row = (turn_row & 1) == 0
        offset = count((seg_row < seg_col) & even_row, 1).astype(jnp.int32)
        place = 2 * (offset + (turn >> 1)) + (turn & 1)
        block = NBLK - iota((NBLK, 1), 0)
        value = block * 64 + operand(e_col) + jnp.where(turn >= 2, 65536, 0)
        table = jnp.sum(jnp.where(place == wide, value.astype(F32), zero), axis=0, keepdims=True)
        through = count((seg_col <= wide) & even, 0)
        here = count((seg_col == wide) & even, 0)
        last = jnp.where(here > zero, through - one, jnp.float32(PAIRS))
        return table.astype(jnp.int32), last.astype(jnp.int32)

    up_row, dn_row, owner_row = up_ref[...], dn_ref[...], own_ref[...]
    up_col, dn_col, owner_col = column(up_row), column(dn_row), column(owner_row)

    def owned(value):
        picked = jnp.where(owner_col == wide, value.astype(F32), zero)
        return jnp.sum(picked, axis=0, keepdims=True).astype(jnp.int32)

    def div(value, by):
        return (value.astype(F32) * jnp.float32(1.0 / by) + jnp.float32(0.5 / by)).astype(jnp.int32)

    def rem(value, by):
        return value - div(value, by) * by

    t0, l0 = pairs(up_row, up_col, COLS, lambda e: rem(e, COLS), lambda e: div(e, COLS))
    t1, l1 = pairs(dn_row, dn_col, ROWS, lambda e: div(e, ROWS), lambda e: rem(e, ROWS))
    t2, l2 = pairs(up_row, up_col, COLS, lambda e: div(e, COLS), lambda e: rem(e, COLS))
    rows = (
        t0, t1, t2, l0, l1, l2,
        owned(div(up_col, COLS) * 64 + rem(up_col, COLS)),
        owned(rem(dn_col, ROWS) * 64 + div(dn_col, ROWS)),
    )
    for n, value in enumerate(rows):
        out_ref[n : n + 1, :] = value


def prepare(up, down, owner):
    return pl.pallas_call(
        prepare_kernel,
        out_shape=jax.ShapeDtypeStruct((8, WIDE), jnp.int32),
        name="prepare",
    )(up, down, owner)


def main_kernel(*refs):
    tab, x_hbm, g_hbm, wu_hbm, wd_hbm = refs[:5]
    dx_out, up_out, dn_out = refs[5:8]
    (
        x_in, og_own, xt_own, wu, wd, runs,
        pre_ref, back_ref, pre_to, back_to, pre_in, back_in, pg_own, ht_own,
        xt_l, xt_r, xt_o, og_l, og_r, og_o,
        pg_l, pg_r, pg_o, ht_l, ht_r, ht_o,
        dxp, zin,
        uf_s, ur_s, ul_s, ua_t, ub_t, ul_v, ur_v, u_acc,
        df_s, dr_s, dl_s, da_t, db_t, dl_v, dr_v, d_acc,
        ex_s, ex_r, ag_s, ag_r, pa_s, pa_r, rs_s, rs_r, z_s, z_r, in_s, col_s, to_s, to_r, sh_s, sh_r,
    ) = refs[8:]
    dp, row, col = lax.axis_index("dp"), lax.axis_index("row"), lax.axis_index("col")
    y, x = dp // SIDE, dp % SIDE
    other = (dp, 1 - row, col)
    x_right = (y * SIDE + (x + 1) % SIDE, row, col)
    x_left = (y * SIDE + (x + 3) % SIDE, row, col)
    y_right = (((y + 1) % SIDE) * SIDE + x, row, col)
    y_left = (((y + 3) % SIDE) * SIDE + x, row, col)
    z_peers = [(dp, row, (col + d) % SIDE) for d in range(1, SIDE)]

    barrier = pltpu.get_barrier_semaphore()
    peers = [other, x_right, x_left, y_right, y_left] + z_peers
    for peer in peers:
        pl.semaphore_signal(barrier, inc=1, device_id=peer, device_id_type=MESH)

    def column_loads(src, dst, n):
        return [
            pltpu.make_async_copy(src.at[:, pl.ds(f * B, B)], dst.at[f], col_s.at[n, f]) for f in range(ROWS)
        ]

    loads = [
        column_loads(g_hbm, og_own, 0),
        column_loads(x_hbm, x_in, 1),
        [pltpu.make_async_copy(wu_hbm, wu.at[pl.ds(0, NBLK)], in_s.at[0])],
        [pltpu.make_async_copy(wd_hbm, wd.at[pl.ds(0, NBLK)], in_s.at[1])],
    ]

    def loaded(n):
        for load in loads[n]:
            load.wait()

    for group in loads:
        for load in group:
            load.start()
    wu[NBLK] = jnp.zeros((B, B), BF)
    wd[NBLK] = jnp.zeros((B, B), BF)
    runs[PAIRS] = jnp.zeros((B, B), BF)

    started = []

    def send(src, dst, send_sem, recv_sem, peer):
        copy = pltpu.make_async_remote_copy(
            src_ref=src, dst_ref=dst, send_sem=send_sem, recv_sem=recv_sem, device_id=peer, device_id_type=MESH
        )
        copy.start()
        started.append(copy)

    def arrived(dst, send_sem, recv_sem, peer):
        pltpu.make_async_remote_copy(
            src_ref=dst, dst_ref=dst, send_sem=send_sem, recv_sem=recv_sem, device_id=peer, device_id_type=MESH
        ).wait_recv()

    kinds = {
        "pg": (0, pg_own, pg_l, pg_r, pg_o, x_right, x_left),
        "ht": (1, ht_own, ht_l, ht_r, ht_o, y_right, y_left),
    }

    token_kinds = (
        (0, xt_own, (xt_l, xt_r, xt_o), x_right, x_left),
        (1, og_own, (og_l, og_r, og_o), y_right, y_left),
    )
    z_right, z_left = (dp, row, (col + 1) % SIDE), (dp, row, (col + 3) % SIDE)
    first, second = pl.ds(0, 4), pl.ds(4, 4)

    def share(step, offset=0, count=4):
        return pl.ds(8 + 4 * ((col + step) % SIDE) + offset, count)

    token_spots = (
        (0, share(0), share(0)), (0, first, first), (0, second, second),
        (1, share(0), share(0)), (1, first, first), (1, second, second),
        (2, share(0, 0, 2), 0), (2, first, 0), (2, share(0, 2, 2), 1), (2, second, 1),
    )

    def token_send(kind, slot):
        n, own, into, to_right, to_left = kind
        buffer, at, source = token_spots[slot]
        src = own if slot < 6 else into[source]
        peer = to_right if slot in (0, 1, 2, 6, 7) else to_left
        send(src.at[at], into[buffer].at[at], to_s.at[n, slot], to_r.at[n, slot], peer)

    def token_wait(kind, slot):
        n, _, into, to_right, _ = kind
        buffer, at, _ = token_spots[slot]
        arrived(into[buffer].at[at], to_s.at[n, slot], to_r.at[n, slot], to_right)

    def share_send(kind, source):
        n, _, into, _, _ = kind
        ref = into[source].at[share(0)]
        send(ref, ref, sh_s.at[n, source, 0], sh_r.at[n, source, 0], z_right)
        send(ref, ref, sh_s.at[n, source, 1], sh_r.at[n, source, 1], z_left)

    def share_wait(kind, source, way):
        n, _, into, _, _ = kind
        ref = into[source].at[share((3, 1, 2)[way])]
        arrived(ref, sh_s.at[n, source, way], sh_r.at[n, source, way], z_right)

    def share_forward(kind, source):
        n, _, into, _, _ = kind
        share_wait(kind, source, n)
        ref = into[source].at[share((3, 1)[n])]
        send(ref, ref, sh_s.at[n, source, 2], sh_r.at[n, source, 2], (z_right, z_left)[n])

    def part(c, whose=row):
        return pl.ds(whose * ROWS + c * CH, CH)

    def ring_out(kind, c, way):
        n, own, left, right, _, to_right, to_left = kinds[kind]
        at = part(c)
        if way == "r":
            send(own.at[at], left.at[at], ag_s.at[n, c], ag_r.at[n, c], to_right)
        else:
            send(own.at[at], right.at[at], ag_s.at[n, 2 + c], ag_r.at[n, 2 + c], to_left)

    def spot(kind, slot, whose=row):
        _, own, left, right, far, _, _ = kinds[kind]
        buffer = (own, own, left, left, right, right, far, far, far, far)[slot]
        if slot < 6:
            return buffer.at[part(slot % 2, whose)]
        return buffer.at[pl.ds(whose * ROWS + (slot - 6) * (CH // 2), CH // 2)]

    def ring_wait(kind, slot):
        n, to_right = kinds[kind][0], kinds[kind][5]
        arrived(spot(kind, slot + 2), ag_s.at[n, slot], ag_r.at[n, slot], to_right)

    def ring_forward(kind, way):
        n, _, left, right, far, to_right, to_left = kinds[kind]
        base = row * ROWS
        source, first, peer = (left, 4, to_right) if way == "r" else (right, 6, to_left)
        for slot in (first, first + 1):
            at = pl.ds(base + (slot - 4) * (CH // 2), CH // 2)
            send(source.at[at], far.at[at], ag_s.at[n, slot], ag_r.at[n, slot], peer)

    def pair_out(kind, slot):
        n = kinds[kind][0]
        ref = spot(kind, slot)
        send(ref, ref, pa_s.at[n, slot], pa_r.at[n, slot], other)

    def pair_wait(kind, slot):
        n = kinds[kind][0]
        ref = spot(kind, slot, 1 - row)
        arrived(ref, pa_s.at[n, slot], pa_r.at[n, slot], other)

    loaded(1)
    for f in range(ROWS):
        xt_own[f] = x_in[f].T

    def products(n, left, weights, axis, count, unroll):
        def body(i, total):
            parts = []
            for j in range(unroll):
                p = i * unroll + j
                first, second = tab[n, 2 * p], tab[n, 2 * p + 1]
                lhs = jnp.concatenate([left(first & 63), left(second & 63)], axis=1)
                rhs = jnp.concatenate(
                    [weights[NBLK - ((first >> 6) & 1023)], weights[NBLK - ((second >> 6) & 1023)]], axis=axis
                )
                parts.append(((first >> 16).astype(F32), dot(lhs, rhs, NT if axis else NN)))
            for j in range(unroll):
                total = total * parts[j][0] + parts[j][1]
                runs[i * unroll + j] = total.astype(BF)
            return total

        lax.fori_loop(0, count // unroll, body, jnp.zeros((B, B), F32))

    def exchange(n, to, mine, into):
        def pick(i, carry):
            for j in range(6):
                at = i * 6 + j
                to[at] = runs[tab[3 + n, (1 - row) * ROWS + at]]
            return carry

        def own(i, carry):
            for j in range(6):
                at = i * 6 + j
                mine[at] = runs[tab[3 + n, row * ROWS + at]]
            return carry

        for c in range(2):
            lax.fori_loop(2 * c, 2 * c + 2, pick, 0)
            here = pl.ds(c * CH, CH)
            send(to.at[here], into.at[here], ex_s.at[2 * n + c], ex_r.at[2 * n + c], other)
        lax.fori_loop(0, 4, own, 0)

    loaded(2)
    products(0, lambda f: x_in[f], wu, 0, PAIRS, 12)
    loaded(0)
    pl.semaphore_wait(barrier, len(peers))
    for slots in ((0, 3), (1, 5), (2, 4)):
        for kind in token_kinds:
            for slot in slots:
                token_send(kind, slot)
    exchange(0, pre_to, pre_ref, pre_in)
    loaded(3)
    products(1, lambda f: og_own[f], wd, 1, PAIRS, 12)
    exchange(1, back_to, back_ref, back_in)
    for kind in token_kinds:
        for slot, source, forward in ((0, 0, 6), (3, 1, 8)):
            token_wait(kind, slot)
            share_send(kind, source)
            token_send(kind, forward)
        for slot, forward in ((1, 7), (5, 9)):
            token_wait(kind, slot)
            token_send(kind, forward)

    for c in range(2):
        here = pl.ds(c * CH, CH)
        arrived(pre_in.at[here], ex_s.at[c], ex_r.at[c], other)
        arrived(back_in.at[here], ex_s.at[2 + c], ex_r.at[2 + c], other)

        def one(i, carry, c=c):
            mine = row * ROWS + c * CH + i
            pre = pre_ref[c * CH + i].astype(F32) + pre_in[c * CH + i].astype(F32)
            back = back_ref[c * CH + i].astype(F32) + back_in[c * CH + i].astype(F32)
            hidden, pre_grad = activate(pre, back)
            pg_own[mine] = pre_grad.astype(BF)
            ht_own[mine] = hidden.astype(BF).T
            return carry

        lax.fori_loop(0, CH, one, 0)
        for kind in ("pg", "ht"):
            ring_out(kind, c, "rl"[c])
            pair_out(kind, c)
    for kind in ("pg", "ht"):
        ring_out(kind, 1, "r")
        ring_out(kind, 0, "l")

    for kind in token_kinds:
        token_wait(kind, 6)
        token_wait(kind, 8)
        share_send(kind, 2)
        share_forward(kind, 0)
        share_forward(kind, 1)

    pair_wait("pg", 0)
    pair_wait("pg", 1)
    products(2, lambda h: pg_own[h], wu, 1, 156, 12)
    for f in range(ROWS):
        dxp[:, f * B : (f + 1) * B] = runs[tab[5, f]]
    for d in range(1, SIDE):
        theirs = pl.ds(pl.multiple_of(((col + d) % SIDE) * 32, 32), 32)
        send(dxp.at[theirs], zin.at[d - 1], z_s.at[d - 1], z_r.at[d - 1], z_peers[d - 1])

    for kind in token_kinds:
        share_forward(kind, 2)
    for kind in ("pg", "ht"):
        ring_wait(kind, 0)
        ring_forward(kind, "r")
        pair_out(kind, 2)
        ring_wait(kind, 3)
        ring_forward(kind, "l")
        pair_out(kind, 5)
    for kind in ("pg", "ht"):
        ring_wait(kind, 1)
        pair_out(kind, 3)
        ring_wait(kind, 2)
        pair_out(kind, 4)
    for kind in token_kinds:
        for slot in (2, 4, 7, 9):
            token_wait(kind, slot)
        for source in range(3):
            share_wait(kind, source, 1 - kind[0])
            share_wait(kind, source, 2)
    for slot in (4, 6, 5, 7):
        for kind in ("pg", "ht"):
            ring_wait(kind, slot)
            pair_out(kind, slot + 2)
    for kind in ("ht",):
        for slot in range(2):
            pair_wait(kind, slot)
    for slot in range(2, 10):
        for kind in ("pg", "ht"):
            pair_wait(kind, slot)

    def up_block(s):
        e = tab[6, s]
        f, h = e >> 6, e & 63
        left = jnp.concatenate([xt_own[f], xt_l[f], xt_r[f], xt_o[f]], axis=1)
        right = jnp.concatenate([pg_own[h], pg_l[h], pg_r[h], pg_o[h]], axis=0)
        return dot(left, right, NN)

    def dn_block(s):
        e = tab[7, s]
        f, h = e >> 6, e & 63
        left = jnp.concatenate([ht_own[h], ht_l[h], ht_r[h], ht_o[h]], axis=1)
        right = jnp.concatenate([og_own[f], og_l[f], og_r[f], og_o[f]], axis=0)
        return dot(left, right, NN)

    def up_base(d):
        return ((y + d) % SIDE) * (SIDE * SHARE) + x * SHARE

    def dn_base(d):
        return y * (SIDE * SHARE) + ((x + d) % SIDE) * SHARE

    half = SHARE // 2
    early, late = pl.ds(0, half), pl.ds(half, half)

    def fill(block, base, out, first, added=None):
        def body(i, carry):
            for j in range(9):
                at = first + i * 9 + j
                value = block(base + at)
                if added is not None:
                    value = value + added[i * 9 + j].astype(F32)
                out[at] = value.astype(out.dtype)
            return carry

        lax.fori_loop(0, half // 9, body, 0)

    sides = (
        (0, up_block, up_base, y_right, y_left, uf_s, ur_s, ul_s, ua_t, ub_t, ul_v, ur_v, u_acc, up_out),
        (1, dn_block, dn_base, x_right, x_left, df_s, dr_s, dl_s, da_t, db_t, dl_v, dr_v, d_acc, dn_out),
    )
    for n, block, base, to_right, to_left, f_s, r_s, l_s, a_t, b_t, l_v, r_v, acc, out in sides:
        fill(block, base(2), f_s, 0)
        send(f_s.at[early], a_t, rs_s.at[n, 0], rs_r.at[n, 0], to_right)
        fill(block, base(2), f_s, half)
        send(f_s.at[late], b_t, rs_s.at[n, 1], rs_r.at[n, 1], to_left)
    for n, block, base, to_right, to_left, f_s, r_s, l_s, a_t, b_t, l_v, r_v, acc, out in sides:
        fill(block, base(1), r_s, half)
        send(r_s.at[late], l_v.at[late], rs_s.at[n, 2], rs_r.at[n, 2], to_right)
        fill(block, base(3), l_s, 0)
        send(l_s.at[early], r_v.at[early], rs_s.at[n, 3], rs_r.at[n, 3], to_left)
    for n, block, base, to_right, to_left, f_s, r_s, l_s, a_t, b_t, l_v, r_v, acc, out in sides:
        arrived(a_t, rs_s.at[n, 0], rs_r.at[n, 0], to_left)
        fill(block, base(1), r_s, 0, a_t)
        send(r_s.at[early], l_v.at[early], rs_s.at[n, 4], rs_r.at[n, 4], to_right)
        arrived(b_t, rs_s.at[n, 1], rs_r.at[n, 1], to_right)
        fill(block, base(3), l_s, half, b_t)
        send(l_s.at[late], r_v.at[late], rs_s.at[n, 5], rs_r.at[n, 5], to_left)
    for n, block, base, to_right, to_left, f_s, r_s, l_s, a_t, b_t, l_v, r_v, acc, out in sides:
        fill(block, base(0), acc, 0)
        fill(block, base(0), acc, half)

    for d in range(1, SIDE):
        arrived(zin.at[d - 1], z_s.at[d - 1], z_r.at[d - 1], z_peers[d - 1])
    own_rows = pl.ds(pl.multiple_of(col * 32, 32), 32)
    dx_out[...] = (
        dxp[own_rows, :].astype(F32) + zin[0].astype(F32) + zin[1].astype(F32) + zin[2].astype(F32)
    ).astype(BF)
    for n, block, base, to_right, to_left, f_s, r_s, l_s, a_t, b_t, l_v, r_v, acc, out in sides:
        arrived(l_v.at[late], rs_s.at[n, 2], rs_r.at[n, 2], to_left)
        arrived(r_v.at[early], rs_s.at[n, 3], rs_r.at[n, 3], to_right)
        arrived(l_v.at[early], rs_s.at[n, 4], rs_r.at[n, 4], to_left)
        arrived(r_v.at[late], rs_s.at[n, 5], rs_r.at[n, 5], to_right)

        def total(i, carry, acc=acc, l_v=l_v, r_v=r_v, out=out):
            out[i] = (acc[i] + l_v[i].astype(F32) + r_v[i].astype(F32)).astype(BF)
            return carry

        lax.fori_loop(0, SHARE, total, 0)
    for copy in started:
        copy.wait_send()


def main(table, x, g, wu, wd):
    vmem = pl.BlockSpec(memory_space=pltpu.VMEM)
    far = pl.BlockSpec(memory_space=pl.ANY)

    def blocks(n, dtype=BF):
        return pltpu.VMEM((n, B, B), dtype)

    tokens = pltpu.VMEM((B, ROWS * B), BF)
    side = [blocks(SHARE)] * 3 + [blocks(SHARE // 2)] * 2 + [blocks(SHARE)] * 2 + [blocks(SHARE, F32)]
    dma = pltpu.SemaphoreType.DMA
    scratch = (
        [blocks(ROWS)] * 3 + [blocks(NBLK + 1), blocks(NBLK + 1), blocks(PAIRS + 1)]
        + [blocks(ROWS)] * 6
        + [blocks(COLS)] * 2
        + [blocks(ROWS)] * 3
        + [blocks(ROWS)] * 3
        + [blocks(COLS)] * 6
        + [tokens, pltpu.VMEM((3, 32, ROWS * B), BF)]
        + side
        + side
        + [dma((4,))] * 2
        + [dma((2, 8))] * 2
        + [dma((2, 10))] * 2
        + [dma((2, 6))] * 2
        + [dma((3,))] * 2
        + [dma((2,)), dma((2, ROWS))]
        + [dma((2, 10))] * 2
        + [dma((2, 3, 3))] * 2
    )
    return pl.pallas_call(
        main_kernel,
        out_shape=[
            jax.ShapeDtypeStruct((32, ROWS * B), BF),
            jax.ShapeDtypeStruct((SHARE, B, B), BF),
            jax.ShapeDtypeStruct((SHARE, B, B), BF),
        ],
        in_specs=[pl.BlockSpec(memory_space=pltpu.SMEM)] + [far] * 4,
        out_specs=[vmem] * 3,
        scratch_shapes=scratch,
        compiler_params=pltpu.CompilerParams(
            collective_id=0, has_side_effects=True, vmem_limit_bytes=62 * 2**20
        ),
        name="backward",
    )(table, x, g, wu, wd)


def results_kernel(*refs):
    count = len(refs) // 2
    for n in range(count):
        refs[count + n][...] = refs[n][...]


def results(*values):
    vmem = pl.BlockSpec(memory_space=pltpu.VMEM)
    return pl.pallas_call(
        results_kernel,
        out_shape=[jax.ShapeDtypeStruct(value.shape, value.dtype) for value in values],
        in_specs=[vmem] * len(values),
        out_specs=[vmem] * len(values),
        name="results",
    )(*values)


def shards(tokens_in, out_grad, up_weight, down_weight, up_blocks, down_blocks, owners):
    table = prepare(up_blocks[0], down_blocks[0], owners[0])
    input_grad, up_grad, down_grad = results(
        *main(table, tokens_in, out_grad, up_weight[0, 0], down_weight[0, 0])
    )
    return input_grad, up_grad[None, None], down_grad[None, None]


def solution(mesh):
    placed = (
        P("dp", "row"),
        P("dp", "row"),
        P("row", "col", None, None, None),
        P("row", "col", None, None, None),
        P("row", "col", None),
        P("row", "col", None),
        P("row", "col", None),
    )
    return jax.shard_map(
        shards,
        mesh=mesh,
        in_specs=placed,
        out_specs=(
            P(("dp", "col"), "row"),
            P("row", "col", "dp", None, None),
            P("row", "col", "dp", None, None),
        ),
        check_vma=False,
    )
```

```python
import functools

import jax
import jax.numpy as jnp
from jax import lax
from jax.experimental import pallas as pl
from jax.experimental.pallas import tpu as pltpu
from jax.sharding import PartitionSpec as P

BF = jnp.bfloat16
F32 = jnp.float32
B = 128
ROWS = 24
COLS = 48
NBLK = 288
SIDE = 4
SHARE = 18
CH = 12
PAIRS = 168
WIDE = 384
NN = (((1,), (0,)), ((), ()))
NT = (((1,), (1,)), ((), ()))
MESH = pl.DeviceIdType.MESH

root_two_pi = 0.7978845608028654
cubic_coef = 0.044715


def activate(pre_sum, back_sum):
    square = pre_sum * pre_sum
    inner_arg = root_two_pi * (pre_sum + cubic_coef * square * pre_sum)
    tanh_inner = jnp.tanh(inner_arg)
    half = 0.5 * (1.0 + tanh_inner)
    slope = half + 0.5 * pre_sum * (1.0 - tanh_inner * tanh_inner) * root_two_pi * (
        1.0 + 3.0 * cubic_coef * square
    )
    return pre_sum * half, back_sum * slope


def dot(left, right, dims):
    return lax.dot_general(left, right, dims, preferred_element_type=F32)


def prepare_kernel(up_ref, dn_ref, own_ref, out_ref):
    def iota(shape, axis):
        return lax.broadcasted_iota(jnp.int32, shape, axis)

    square = (NBLK, NBLK)
    sub, lane = iota(square, 0), iota(square, 1)
    wide = iota((NBLK, WIDE), 1)
    one, zero = jnp.float32(1), jnp.float32(0)

    def count(mask, axis):
        return jnp.sum(jnp.where(mask, one, zero), axis=axis, keepdims=True)

    def column(row):
        picked = jnp.where(sub == lane, jnp.broadcast_to(row, square).astype(F32), zero)
        return jnp.sum(picked, axis=1, keepdims=True).astype(jnp.int32)

    def pairs(e_row, e_col, split, segment, operand):
        seg_row, seg_col = segment(e_row), segment(e_col)
        same = seg_col == seg_row
        turn = count(same & (lane < sub), 1).astype(jnp.int32)
        even = (turn & 1) == 0
        turn_row = count(same & (sub < lane), 0).astype(jnp.int32)
        even_row = (turn_row & 1) == 0
        offset = count((seg_row < seg_col) & even_row, 1).astype(jnp.int32)
        place = 2 * (offset + (turn >> 1)) + (turn & 1)
        block = NBLK - iota((NBLK, 1), 0)
        value = block * 64 + operand(e_col) + jnp.where(turn >= 2, 65536, 0)
        table = jnp.sum(jnp.where(place == wide, value.astype(F32), zero), axis=0, keepdims=True)
        through = count((seg_col <= wide) & even, 0)
        here = count((seg_col == wide) & even, 0)
        last = jnp.where(here > zero, through - one, jnp.float32(PAIRS))
        return table.astype(jnp.int32), last.astype(jnp.int32)

    up_row, dn_row, owner_row = up_ref[...], dn_ref[...], own_ref[...]
    up_col, dn_col, owner_col = column(up_row), column(dn_row), column(owner_row)

    def owned(value):
        picked = jnp.where(owner_col == wide, value.astype(F32), zero)
        return jnp.sum(picked, axis=0, keepdims=True).astype(jnp.int32)

    def div(value, by):
        return (value.astype(F32) * jnp.float32(1.0 / by) + jnp.float32(0.5 / by)).astype(jnp.int32)

    def rem(value, by):
        return value - div(value, by) * by

    t0, l0 = pairs(up_row, up_col, COLS, lambda e: rem(e, COLS), lambda e: div(e, COLS))
    t1, l1 = pairs(dn_row, dn_col, ROWS, lambda e: div(e, ROWS), lambda e: rem(e, ROWS))
    t2, l2 = pairs(up_row, up_col, COLS, lambda e: div(e, COLS), lambda e: rem(e, COLS))
    rows = (
        t0, t1, t2, l0, l1, l2,
        owned(div(up_col, COLS) * 64 + rem(up_col, COLS)),
        owned(rem(dn_col, ROWS) * 64 + div(dn_col, ROWS)),
    )
    for n, value in enumerate(rows):
        out_ref[n : n + 1, :] = value


def prepare(up, down, owner):
    return pl.pallas_call(
        prepare_kernel,
        out_shape=jax.ShapeDtypeStruct((8, WIDE), jnp.int32),
        name="prepare",
    )(up, down, owner)


def main_kernel(*refs):
    tab, x_hbm, g_hbm, wu_hbm, wd_hbm = refs[:5]
    dx_out, up_out, dn_out = refs[5:8]
    (
        x_in, og_own, xt_own, wu, wd, runs,
        pre_ref, back_ref, pre_to, back_to, pre_in, back_in, pg_own, ht_own,
        xt_l, xt_r, xt_o, og_l, og_r, og_o,
        pg_l, pg_r, pg_o, ht_l, ht_r, ht_o,
        dxp, zin,
        uf_s, ur_s, ul_s, ua_t, ub_t, ul_v, ur_v, u_acc,
        df_s, dr_s, dl_s, da_t, db_t, dl_v, dr_v, d_acc,
        ex_s, ex_r, ag_s, ag_r, pa_s, pa_r, rs_s, rs_r, z_s, z_r, in_s, col_s, to_s, to_r, sh_s, sh_r,
    ) = refs[8:]
    dp, row, col = lax.axis_index("dp"), lax.axis_index("row"), lax.axis_index("col")
    y, x = dp // SIDE, dp % SIDE
    other = (dp, 1 - row, col)
    x_right = (y * SIDE + (x + 1) % SIDE, row, col)
    x_left = (y * SIDE + (x + 3) % SIDE, row, col)
    y_right = (((y + 1) % SIDE) * SIDE + x, row, col)
    y_left = (((y + 3) % SIDE) * SIDE + x, row, col)
    z_peers = [(dp, row, (col + d) % SIDE) for d in range(1, SIDE)]

    barrier = pltpu.get_barrier_semaphore()
    peers = [other, x_right, x_left, y_right, y_left] + z_peers
    for peer in peers:
        pl.semaphore_signal(barrier, inc=1, device_id=peer, device_id_type=MESH)

    def column_loads(src, dst, n):
        return [
            pltpu.make_async_copy(src.at[:, pl.ds(f * B, B)], dst.at[f], col_s.at[n, f]) for f in range(ROWS)
        ]

    loads = [
        column_loads(g_hbm, og_own, 0),
        column_loads(x_hbm, x_in, 1),
        [pltpu.make_async_copy(wu_hbm, wu.at[pl.ds(0, NBLK)], in_s.at[0])],
        [pltpu.make_async_copy(wd_hbm, wd.at[pl.ds(0, NBLK)], in_s.at[1])],
    ]

    def loaded(n):
        for load in loads[n]:
            load.wait()

    def begin(n):
        for load in loads[n]:
            load.start()

    for n in (1, 2, 0):
        begin(n)
    wu[NBLK] = jnp.zeros((B, B), BF)
    wd[NBLK] = jnp.zeros((B, B), BF)
    runs[PAIRS] = jnp.zeros((B, B), BF)

    started = []

    def send(src, dst, send_sem, recv_sem, peer):
        copy = pltpu.make_async_remote_copy(
            src_ref=src, dst_ref=dst, send_sem=send_sem, recv_sem=recv_sem, device_id=peer, device_id_type=MESH
        )
        copy.start()
        started.append(copy)

    def arrived(dst, send_sem, recv_sem, peer):
        pltpu.make_async_remote_copy(
            src_ref=dst, dst_ref=dst, send_sem=send_sem, recv_sem=recv_sem, device_id=peer, device_id_type=MESH
        ).wait_recv()

    kinds = {
        "pg": (0, pg_own, pg_l, pg_r, pg_o, x_right, x_left),
        "ht": (1, ht_own, ht_l, ht_r, ht_o, y_right, y_left),
    }

    token_kinds = (
        (0, xt_own, (xt_l, xt_r, xt_o), x_right, x_left),
        (1, og_own, (og_l, og_r, og_o), y_right, y_left),
    )
    z_right, z_left = (dp, row, (col + 1) % SIDE), (dp, row, (col + 3) % SIDE)
    first, second = pl.ds(0, 4), pl.ds(4, 4)

    def share(step, offset=0, count=4):
        return pl.ds(8 + 4 * ((col + step) % SIDE) + offset, count)

    token_spots = (
        (0, share(0), share(0)), (0, first, first), (0, second, second),
        (1, share(0), share(0)), (1, first, first), (1, second, second),
        (2, share(0, 0, 2), 0), (2, first, 0), (2, share(0, 2, 2), 1), (2, second, 1),
    )

    def token_send(kind, slot):
        n, own, into, to_right, to_left = kind
        buffer, at, source = token_spots[slot]
        src = own if slot < 6 else into[source]
        peer = to_right if slot in (0, 1, 2, 6, 7) else to_left
        send(src.at[at], into[buffer].at[at], to_s.at[n, slot], to_r.at[n, slot], peer)

    def token_wait(kind, slot):
        n, _, into, to_right, _ = kind
        buffer, at, _ = token_spots[slot]
        arrived(into[buffer].at[at], to_s.at[n, slot], to_r.at[n, slot], to_right)

    def share_send(kind, source):
        n, _, into, _, _ = kind
        ref = into[source].at[share(0)]
        send(ref, ref, sh_s.at[n, source, 0], sh_r.at[n, source, 0], z_right)
        send(ref, ref, sh_s.at[n, source, 1], sh_r.at[n, source, 1], z_left)

    def share_wait(kind, source, way):
        n, _, into, _, _ = kind
        ref = into[source].at[share((3, 1, 2)[way])]
        arrived(ref, sh_s.at[n, source, way], sh_r.at[n, source, way], z_right)

    def share_forward(kind, source):
        n, _, into, _, _ = kind
        share_wait(kind, source, n)
        ref = into[source].at[share((3, 1)[n])]
        send(ref, ref, sh_s.at[n, source, 2], sh_r.at[n, source, 2], (z_right, z_left)[n])

    def part(c, whose=row):
        return pl.ds(whose * ROWS + c * CH, CH)

    def ring_out(kind, c, way):
        n, own, left, right, _, to_right, to_left = kinds[kind]
        at = part(c)
        if way == "r":
            send(own.at[at], left.at[at], ag_s.at[n, c], ag_r.at[n, c], to_right)
        else:
            send(own.at[at], right.at[at], ag_s.at[n, 2 + c], ag_r.at[n, 2 + c], to_left)

    def spot(kind, slot, whose=row):
        _, own, left, right, far, _, _ = kinds[kind]
        buffer = (own, own, left, left, right, right, far, far, far, far)[slot]
        if slot < 6:
            return buffer.at[part(slot % 2, whose)]
        return buffer.at[pl.ds(whose * ROWS + (slot - 6) * (CH // 2), CH // 2)]

    def ring_wait(kind, slot):
        n, to_right = kinds[kind][0], kinds[kind][5]
        arrived(spot(kind, slot + 2), ag_s.at[n, slot], ag_r.at[n, slot], to_right)

    def ring_forward(kind, way):
        n, _, left, right, far, to_right, to_left = kinds[kind]
        base = row * ROWS
        source, first, peer = (left, 4, to_right) if way == "r" else (right, 6, to_left)
        for slot in (first, first + 1):
            at = pl.ds(base + (slot - 4) * (CH // 2), CH // 2)
            send(source.at[at], far.at[at], ag_s.at[n, slot], ag_r.at[n, slot], peer)

    def pair_out(kind, slot):
        n = kinds[kind][0]
        ref = spot(kind, slot)
        send(ref, ref, pa_s.at[n, slot], pa_r.at[n, slot], other)

    def pair_wait(kind, slot):
        n = kinds[kind][0]
        ref = spot(kind, slot, 1 - row)
        arrived(ref, pa_s.at[n, slot], pa_r.at[n, slot], other)

    loaded(1)
    for f in range(ROWS):
        xt_own[f] = x_in[f].T

    def products(n, left, weights, axis, start, stop, total=None):
        unroll = 12

        def body(i, total):
            parts = []
            for j in range(unroll):
                p = i * unroll + j
                first, second = tab[n, 2 * p], tab[n, 2 * p + 1]
                lhs = jnp.concatenate([left(first & 63), left(second & 63)], axis=1)
                rhs = jnp.concatenate(
                    [weights[NBLK - ((first >> 6) & 1023)], weights[NBLK - ((second >> 6) & 1023)]], axis=axis
                )
                parts.append(((first >> 16).astype(F32), dot(lhs, rhs, NT if axis else NN)))
            for j in range(unroll):
                total = total * parts[j][0] + parts[j][1]
                runs[i * unroll + j] = total.astype(BF)
            return total

        if total is None:
            total = jnp.zeros((B, B), F32)
        return lax.fori_loop(start, stop, body, total)

    def exchange(n, to, mine, into):
        def pick(i, carry):
            for j in range(6):
                at = i * 6 + j
                to[at] = runs[tab[3 + n, (1 - row) * ROWS + at]]
            return carry

        def own(i, carry):
            for j in range(6):
                at = i * 6 + j
                mine[at] = runs[tab[3 + n, row * ROWS + at]]
            return carry

        for c in range(2):
            lax.fori_loop(2 * c, 2 * c + 2, pick, 0)
            here = pl.ds(c * CH, CH)
            send(to.at[here], into.at[here], ex_s.at[2 * n + c], ex_r.at[2 * n + c], other)
        lax.fori_loop(0, 4, own, 0)

    loaded(2)
    begin(3)
    carried = products(0, lambda f: x_in[f], wu, 0, 0, 7)
    loaded(0)
    pl.semaphore_wait(barrier, len(peers))
    for slots in ((0, 3), (1, 5), (2, 4)):
        for kind in token_kinds:
            for slot in slots:
                token_send(kind, slot)
    products(0, lambda f: x_in[f], wu, 0, 7, 14, carried)
    exchange(0, pre_to, pre_ref, pre_in)
    for kind in token_kinds:
        for slot, source, forward in ((0, 0, 6), (3, 1, 8)):
            token_wait(kind, slot)
            share_send(kind, source)
            token_send(kind, forward)
    loaded(3)
    carried = products(1, lambda f: og_own[f], wd, 1, 0, 7)
    for kind in token_kinds:
        for slot, forward in ((1, 7), (5, 9)):
            token_wait(kind, slot)
            token_send(kind, forward)
    products(1, lambda f: og_own[f], wd, 1, 7, 14, carried)
    exchange(1, back_to, back_ref, back_in)
    for kind in token_kinds:
        token_wait(kind, 6)
        token_wait(kind, 8)
        share_send(kind, 2)
        share_forward(kind, 0)
        share_forward(kind, 1)

    for c in range(2):
        here = pl.ds(c * CH, CH)
        arrived(pre_in.at[here], ex_s.at[c], ex_r.at[c], other)
        arrived(back_in.at[here], ex_s.at[2 + c], ex_r.at[2 + c], other)

        def one(i, carry, c=c):
            mine = row * ROWS + c * CH + i
            pre = pre_ref[c * CH + i].astype(F32) + pre_in[c * CH + i].astype(F32)
            back = back_ref[c * CH + i].astype(F32) + back_in[c * CH + i].astype(F32)
            hidden, pre_grad = activate(pre, back)
            pg_own[mine] = pre_grad.astype(BF)
            ht_own[mine] = hidden.astype(BF).T
            return carry

        lax.fori_loop(0, CH, one, 0)
        for kind in ("pg", "ht"):
            ring_out(kind, c, "rl"[c])
            pair_out(kind, c)
    for kind in ("pg", "ht"):
        ring_out(kind, 1, "r")
        ring_out(kind, 0, "l")

    pair_wait("pg", 0)
    pair_wait("pg", 1)
    products(2, lambda h: pg_own[h], wu, 1, 0, 13)
    for f in range(ROWS):
        dxp[:, f * B : (f + 1) * B] = runs[tab[5, f]]
    for d in range(1, SIDE):
        theirs = pl.ds(pl.multiple_of(((col + d) % SIDE) * 32, 32), 32)
        send(dxp.at[theirs], zin.at[d - 1], z_s.at[d - 1], z_r.at[d - 1], z_peers[d - 1])

    for kind in token_kinds:
        share_forward(kind, 2)
    for kind in ("pg", "ht"):
        ring_wait(kind, 0)
        ring_forward(kind, "r")
        pair_out(kind, 2)
        ring_wait(kind, 3)
        ring_forward(kind, "l")
        pair_out(kind, 5)
    for kind in ("pg", "ht"):
        ring_wait(kind, 1)
        pair_out(kind, 3)
        ring_wait(kind, 2)
        pair_out(kind, 4)
    for kind in token_kinds:
        for slot in (2, 4, 7, 9):
            token_wait(kind, slot)
        for source in range(3):
            share_wait(kind, source, 1 - kind[0])
            share_wait(kind, source, 2)
    for slot in (4, 6, 5, 7):
        for kind in ("pg", "ht"):
            ring_wait(kind, slot)
            pair_out(kind, slot + 2)
    for kind in ("ht",):
        for slot in range(2):
            pair_wait(kind, slot)
    for slot in range(2, 10):
        for kind in ("pg", "ht"):
            pair_wait(kind, slot)

    def up_block(s):
        e = tab[6, s]
        f, h = e >> 6, e & 63
        left = jnp.concatenate([xt_own[f], xt_l[f], xt_r[f], xt_o[f]], axis=1)
        right = jnp.concatenate([pg_own[h], pg_l[h], pg_r[h], pg_o[h]], axis=0)
        return dot(left, right, NN)

    def dn_block(s):
        e = tab[7, s]
        f, h = e >> 6, e & 63
        left = jnp.concatenate([ht_own[h], ht_l[h], ht_r[h], ht_o[h]], axis=1)
        right = jnp.concatenate([og_own[f], og_l[f], og_r[f], og_o[f]], axis=0)
        return dot(left, right, NN)

    def up_base(d):
        return ((y + d) % SIDE) * (SIDE * SHARE) + x * SHARE

    def dn_base(d):
        return y * (SIDE * SHARE) + ((x + d) % SIDE) * SHARE

    half = SHARE // 2
    early, late = pl.ds(0, half), pl.ds(half, half)

    def fill(block, base, out, first, added=None):
        def body(i, carry):
            for j in range(9):
                at = first + i * 9 + j
                value = block(base + at)
                if added is not None:
                    value = value + added[i * 9 + j].astype(F32)
                out[at] = value.astype(out.dtype)
            return carry

        lax.fori_loop(0, half // 9, body, 0)

    sides = (
        (0, up_block, up_base, y_right, y_left, uf_s, ur_s, ul_s, ua_t, ub_t, ul_v, ur_v, u_acc, up_out),
        (1, dn_block, dn_base, x_right, x_left, df_s, dr_s, dl_s, da_t, db_t, dl_v, dr_v, d_acc, dn_out),
    )
    for n, block, base, to_right, to_left, f_s, r_s, l_s, a_t, b_t, l_v, r_v, acc, out in sides:
        fill(block, base(2), f_s, 0)
        send(f_s.at[early], a_t, rs_s.at[n, 0], rs_r.at[n, 0], to_right)
        fill(block, base(2), f_s, half)
        send(f_s.at[late], b_t, rs_s.at[n, 1], rs_r.at[n, 1], to_left)
    for n, block, base, to_right, to_left, f_s, r_s, l_s, a_t, b_t, l_v, r_v, acc, out in sides:
        fill(block, base(1), r_s, half)
        send(r_s.at[late], l_v.at[late], rs_s.at[n, 2], rs_r.at[n, 2], to_right)
        fill(block, base(3), l_s, 0)
        send(l_s.at[early], r_v.at[early], rs_s.at[n, 3], rs_r.at[n, 3], to_left)
    for n, block, base, to_right, to_left, f_s, r_s, l_s, a_t, b_t, l_v, r_v, acc, out in sides:
        arrived(a_t, rs_s.at[n, 0], rs_r.at[n, 0], to_left)
        fill(block, base(1), r_s, 0, a_t)
        send(r_s.at[early], l_v.at[early], rs_s.at[n, 4], rs_r.at[n, 4], to_right)
        arrived(b_t, rs_s.at[n, 1], rs_r.at[n, 1], to_right)
        fill(block, base(3), l_s, half, b_t)
        send(l_s.at[late], r_v.at[late], rs_s.at[n, 5], rs_r.at[n, 5], to_left)
    for n, block, base, to_right, to_left, f_s, r_s, l_s, a_t, b_t, l_v, r_v, acc, out in sides:
        fill(block, base(0), acc, 0)
        fill(block, base(0), acc, half)

    for d in range(1, SIDE):
        arrived(zin.at[d - 1], z_s.at[d - 1], z_r.at[d - 1], z_peers[d - 1])
    own_rows = pl.ds(pl.multiple_of(col * 32, 32), 32)
    dx_out[...] = (
        dxp[own_rows, :].astype(F32) + zin[0].astype(F32) + zin[1].astype(F32) + zin[2].astype(F32)
    ).astype(BF)
    for n, block, base, to_right, to_left, f_s, r_s, l_s, a_t, b_t, l_v, r_v, acc, out in sides:
        arrived(l_v.at[late], rs_s.at[n, 2], rs_r.at[n, 2], to_left)
        arrived(r_v.at[early], rs_s.at[n, 3], rs_r.at[n, 3], to_right)
        arrived(l_v.at[early], rs_s.at[n, 4], rs_r.at[n, 4], to_left)
        arrived(r_v.at[late], rs_s.at[n, 5], rs_r.at[n, 5], to_right)

        def total(i, carry, acc=acc, l_v=l_v, r_v=r_v, out=out):
            out[i] = (acc[i] + l_v[i].astype(F32) + r_v[i].astype(F32)).astype(BF)
            return carry

        lax.fori_loop(0, SHARE, total, 0)
    for copy in started:
        copy.wait_send()


def main(table, x, g, wu, wd):
    vmem = pl.BlockSpec(memory_space=pltpu.VMEM)
    far = pl.BlockSpec(memory_space=pl.ANY)

    def blocks(n, dtype=BF):
        return pltpu.VMEM((n, B, B), dtype)

    tokens = pltpu.VMEM((B, ROWS * B), BF)
    side = [blocks(SHARE)] * 3 + [blocks(SHARE // 2)] * 2 + [blocks(SHARE)] * 2 + [blocks(SHARE, F32)]
    dma = pltpu.SemaphoreType.DMA
    scratch = (
        [blocks(ROWS)] * 3 + [blocks(NBLK + 1), blocks(NBLK + 1), blocks(PAIRS + 1)]
        + [blocks(ROWS)] * 6
        + [blocks(COLS)] * 2
        + [blocks(ROWS)] * 3
        + [blocks(ROWS)] * 3
        + [blocks(COLS)] * 6
        + [tokens, pltpu.VMEM((3, 32, ROWS * B), BF)]
        + side
        + side
        + [dma((4,))] * 2
        + [dma((2, 8))] * 2
        + [dma((2, 10))] * 2
        + [dma((2, 6))] * 2
        + [dma((3,))] * 2
        + [dma((2,)), dma((2, ROWS))]
        + [dma((2, 10))] * 2
        + [dma((2, 3, 3))] * 2
    )
    return pl.pallas_call(
        main_kernel,
        out_shape=[
            jax.ShapeDtypeStruct((32, ROWS * B), BF),
            jax.ShapeDtypeStruct((SHARE, B, B), BF),
            jax.ShapeDtypeStruct((SHARE, B, B), BF),
        ],
        in_specs=[pl.BlockSpec(memory_space=pltpu.SMEM)] + [far] * 4,
        out_specs=[vmem] * 3,
        scratch_shapes=scratch,
        compiler_params=pltpu.CompilerParams(
            collective_id=0, has_side_effects=True, vmem_limit_bytes=62 * 2**20
        ),
        name="backward",
    )(table, x, g, wu, wd)


def results_kernel(*refs):
    count = len(refs) // 2
    for n in range(count):
        refs[count + n][...] = refs[n][...]


def results(*values):
    vmem = pl.BlockSpec(memory_space=pltpu.VMEM)
    return pl.pallas_call(
        results_kernel,
        out_shape=[jax.ShapeDtypeStruct(value.shape, value.dtype) for value in values],
        in_specs=[vmem] * len(values),
        out_specs=[vmem] * len(values),
        name="results",
    )(*values)


def shards(tokens_in, out_grad, up_weight, down_weight, up_blocks, down_blocks, owners):
    table = prepare(up_blocks[0], down_blocks[0], owners[0])
    input_grad, up_grad, down_grad = results(
        *main(table, tokens_in, out_grad, up_weight[0, 0], down_weight[0, 0])
    )
    return input_grad, up_grad[None, None], down_grad[None, None]


def solution(mesh):
    placed = (
        P("dp", "row"),
        P("dp", "row"),
        P("row", "col", None, None, None),
        P("row", "col", None, None, None),
        P("row", "col", None),
        P("row", "col", None),
        P("row", "col", None),
    )
    return jax.shard_map(
        shards,
        mesh=mesh,
        in_specs=placed,
        out_specs=(
            P(("dp", "col"), "row"),
            P("row", "col", "dp", None, None),
            P("row", "col", "dp", None, None),
        ),
        check_vma=False,
    )
```

```python
import functools

import jax
import jax.numpy as jnp
from jax import lax
from jax.experimental import pallas as pl
from jax.experimental.pallas import tpu as pltpu
from jax.sharding import PartitionSpec as P

BF = jnp.bfloat16
F32 = jnp.float32
B = 128
ROWS = 24
COLS = 48
NBLK = 288
SIDE = 4
SHARE = 18
CH = 12
PAIRS = 168
WIDE = 384
NN = (((1,), (0,)), ((), ()))
NT = (((1,), (1,)), ((), ()))
MESH = pl.DeviceIdType.MESH

root_two_pi = 0.7978845608028654
cubic_coef = 0.044715


def activate(pre_sum, back_sum):
    square = pre_sum * pre_sum
    inner_arg = root_two_pi * (pre_sum + cubic_coef * square * pre_sum)
    tanh_inner = jnp.tanh(inner_arg)
    half = 0.5 * (1.0 + tanh_inner)
    slope = half + 0.5 * pre_sum * (1.0 - tanh_inner * tanh_inner) * root_two_pi * (
        1.0 + 3.0 * cubic_coef * square
    )
    return pre_sum * half, back_sum * slope


def dot(left, right, dims):
    return lax.dot_general(left, right, dims, preferred_element_type=F32)


def prepare_kernel(up_ref, dn_ref, own_ref, out_ref):
    def iota(shape, axis):
        return lax.broadcasted_iota(jnp.int32, shape, axis)

    square = (NBLK, NBLK)
    sub, lane = iota(square, 0), iota(square, 1)
    wide = iota((NBLK, WIDE), 1)
    one, zero = jnp.float32(1), jnp.float32(0)

    def count(mask, axis):
        return jnp.sum(jnp.where(mask, one, zero), axis=axis, keepdims=True)

    def column(row):
        picked = jnp.where(sub == lane, jnp.broadcast_to(row, square).astype(F32), zero)
        return jnp.sum(picked, axis=1, keepdims=True).astype(jnp.int32)

    def pairs(e_row, e_col, split, segment, operand):
        seg_row, seg_col = segment(e_row), segment(e_col)
        same = seg_col == seg_row
        turn = count(same & (lane < sub), 1).astype(jnp.int32)
        even = (turn & 1) == 0
        turn_row = count(same & (sub < lane), 0).astype(jnp.int32)
        even_row = (turn_row & 1) == 0
        offset = count((seg_row < seg_col) & even_row, 1).astype(jnp.int32)
        place = 2 * (offset + (turn >> 1)) + (turn & 1)
        block = NBLK - iota((NBLK, 1), 0)
        value = block * 64 + operand(e_col) + jnp.where(turn >= 2, 65536, 0)
        table = jnp.sum(jnp.where(place == wide, value.astype(F32), zero), axis=0, keepdims=True)
        through = count((seg_col <= wide) & even, 0)
        here = count((seg_col == wide) & even, 0)
        last = jnp.where(here > zero, through - one, jnp.float32(PAIRS))
        return table.astype(jnp.int32), last.astype(jnp.int32)

    up_row, dn_row, owner_row = up_ref[...], dn_ref[...], own_ref[...]
    up_col, dn_col, owner_col = column(up_row), column(dn_row), column(owner_row)

    def owned(value):
        picked = jnp.where(owner_col == wide, value.astype(F32), zero)
        return jnp.sum(picked, axis=0, keepdims=True).astype(jnp.int32)

    def div(value, by):
        return (value.astype(F32) * jnp.float32(1.0 / by) + jnp.float32(0.5 / by)).astype(jnp.int32)

    def rem(value, by):
        return value - div(value, by) * by

    t0, l0 = pairs(up_row, up_col, COLS, lambda e: rem(e, COLS), lambda e: div(e, COLS))
    t1, l1 = pairs(dn_row, dn_col, ROWS, lambda e: div(e, ROWS), lambda e: rem(e, ROWS))
    t2, l2 = pairs(up_row, up_col, COLS, lambda e: div(e, COLS), lambda e: rem(e, COLS))
    rows = (
        t0, t1, t2, l0, l1, l2,
        owned(div(up_col, COLS) * 64 + rem(up_col, COLS)),
        owned(rem(dn_col, ROWS) * 64 + div(dn_col, ROWS)),
    )
    for n, value in enumerate(rows):
        out_ref[n : n + 1, :] = value


def prepare(up, down, owner):
    return pl.pallas_call(
        prepare_kernel,
        out_shape=jax.ShapeDtypeStruct((8, WIDE), jnp.int32),
        name="prepare",
    )(up, down, owner)


def main_kernel(*refs):
    tab, x_hbm, g_hbm, wu_hbm, wd_hbm = refs[:5]
    dx_out, up_out, dn_out = refs[5:8]
    (
        x_in, og_own, xt_own, wu, wd, runs,
        pre_ref, back_ref, pre_to, back_to, pre_in, back_in, pg_own, ht_own,
        xt_l, xt_r, xt_o, og_l, og_r, og_o,
        pg_l, pg_r, pg_o, ht_l, ht_r, ht_o,
        dxp, zin,
        uf_s, ur_s, ul_s, ua_t, ub_t, ul_v, ur_v, u_acc,
        df_s, dr_s, dl_s, da_t, db_t, dl_v, dr_v, d_acc,
        ex_s, ex_r, ag_s, ag_r, pa_s, pa_r, rs_s, rs_r, z_s, z_r, in_s, col_s, to_s, to_r, sh_s, sh_r,
    ) = refs[8:]
    dp, row, col = lax.axis_index("dp"), lax.axis_index("row"), lax.axis_index("col")
    y, x = dp // SIDE, dp % SIDE
    other = (dp, 1 - row, col)
    x_right = (y * SIDE + (x + 1) % SIDE, row, col)
    x_left = (y * SIDE + (x + 3) % SIDE, row, col)
    y_right = (((y + 1) % SIDE) * SIDE + x, row, col)
    y_left = (((y + 3) % SIDE) * SIDE + x, row, col)
    z_peers = [(dp, row, (col + d) % SIDE) for d in range(1, SIDE)]

    barrier = pltpu.get_barrier_semaphore()
    peers = [other, x_right, x_left, y_right, y_left] + z_peers
    for peer in peers:
        pl.semaphore_signal(barrier, inc=1, device_id=peer, device_id_type=MESH)

    def column_loads(src, dst, n):
        return [
            pltpu.make_async_copy(src.at[:, pl.ds(f * B, B)], dst.at[f], col_s.at[n, f]) for f in range(ROWS)
        ]

    loads = [
        column_loads(g_hbm, og_own, 0),
        column_loads(x_hbm, x_in, 1),
        [pltpu.make_async_copy(wu_hbm, wu.at[pl.ds(0, NBLK)], in_s.at[0])],
        [pltpu.make_async_copy(wd_hbm, wd.at[pl.ds(0, NBLK)], in_s.at[1])],
    ]

    def loaded(n):
        for load in loads[n]:
            load.wait()

    def begin(n):
        for load in loads[n]:
            load.start()

    for n in (1, 2, 0):
        begin(n)
    wu[NBLK] = jnp.zeros((B, B), BF)
    wd[NBLK] = jnp.zeros((B, B), BF)
    runs[PAIRS] = jnp.zeros((B, B), BF)

    started = []

    def send(src, dst, send_sem, recv_sem, peer):
        copy = pltpu.make_async_remote_copy(
            src_ref=src, dst_ref=dst, send_sem=send_sem, recv_sem=recv_sem, device_id=peer, device_id_type=MESH
        )
        copy.start()
        started.append(copy)

    def arrived(dst, send_sem, recv_sem, peer):
        pltpu.make_async_remote_copy(
            src_ref=dst, dst_ref=dst, send_sem=send_sem, recv_sem=recv_sem, device_id=peer, device_id_type=MESH
        ).wait_recv()

    kinds = {
        "pg": (0, pg_own, pg_l, pg_r, pg_o, x_right, x_left),
        "ht": (1, ht_own, ht_l, ht_r, ht_o, y_right, y_left),
    }

    token_kinds = (
        (0, xt_own, (xt_l, xt_r, xt_o), x_right, x_left),
        (1, og_own, (og_l, og_r, og_o), y_right, y_left),
    )
    z_right, z_left = (dp, row, (col + 1) % SIDE), (dp, row, (col + 3) % SIDE)
    first, second = pl.ds(0, 4), pl.ds(4, 4)

    def share(step, offset=0, count=4):
        return pl.ds(8 + 4 * ((col + step) % SIDE) + offset, count)

    token_spots = (
        (0, share(0), share(0)), (0, first, first), (0, second, second),
        (1, share(0), share(0)), (1, first, first), (1, second, second),
        (2, share(0, 0, 2), 0), (2, first, 0), (2, share(0, 2, 2), 1), (2, second, 1),
    )

    def token_send(kind, slot):
        n, own, into, to_right, to_left = kind
        buffer, at, source = token_spots[slot]
        src = own if slot < 6 else into[source]
        peer = to_right if slot in (0, 1, 2, 6, 7) else to_left
        send(src.at[at], into[buffer].at[at], to_s.at[n, slot], to_r.at[n, slot], peer)

    def token_wait(kind, slot):
        n, _, into, to_right, _ = kind
        buffer, at, _ = token_spots[slot]
        arrived(into[buffer].at[at], to_s.at[n, slot], to_r.at[n, slot], to_right)

    def share_send(kind, source):
        n, _, into, _, _ = kind
        ref = into[source].at[share(0)]
        send(ref, ref, sh_s.at[n, source, 0], sh_r.at[n, source, 0], z_right)
        send(ref, ref, sh_s.at[n, source, 1], sh_r.at[n, source, 1], z_left)

    def share_wait(kind, source, way):
        n, _, into, _, _ = kind
        ref = into[source].at[share((3, 1, 2)[way])]
        arrived(ref, sh_s.at[n, source, way], sh_r.at[n, source, way], z_right)

    def share_forward(kind, source):
        n, _, into, _, _ = kind
        share_wait(kind, source, n)
        ref = into[source].at[share((3, 1)[n])]
        send(ref, ref, sh_s.at[n, source, 2], sh_r.at[n, source, 2], (z_right, z_left)[n])

    def part(c, whose=row):
        return pl.ds(whose * ROWS + c * CH, CH)

    def ring_out(kind, c, way):
        n, own, left, right, _, to_right, to_left = kinds[kind]
        at = part(c)
        if way == "r":
            send(own.at[at], left.at[at], ag_s.at[n, c], ag_r.at[n, c], to_right)
        else:
            send(own.at[at], right.at[at], ag_s.at[n, 2 + c], ag_r.at[n, 2 + c], to_left)

    def spot(kind, slot, whose=row):
        _, own, left, right, far, _, _ = kinds[kind]
        buffer = (own, own, left, left, right, right, far, far, far, far)[slot]
        if slot < 6:
            return buffer.at[part(slot % 2, whose)]
        return buffer.at[pl.ds(whose * ROWS + (slot - 6) * (CH // 2), CH // 2)]

    def ring_wait(kind, slot):
        n, to_right = kinds[kind][0], kinds[kind][5]
        arrived(spot(kind, slot + 2), ag_s.at[n, slot], ag_r.at[n, slot], to_right)

    def ring_forward(kind, way):
        n, _, left, right, far, to_right, to_left = kinds[kind]
        base = row * ROWS
        source, first, peer = (left, 4, to_right) if way == "r" else (right, 6, to_left)
        for slot in (first, first + 1):
            at = pl.ds(base + (slot - 4) * (CH // 2), CH // 2)
            send(source.at[at], far.at[at], ag_s.at[n, slot], ag_r.at[n, slot], peer)

    def pair_out(kind, slot):
        n = kinds[kind][0]
        ref = spot(kind, slot)
        send(ref, ref, pa_s.at[n, slot], pa_r.at[n, slot], other)

    def pair_wait(kind, slot):
        n = kinds[kind][0]
        ref = spot(kind, slot, 1 - row)
        arrived(ref, pa_s.at[n, slot], pa_r.at[n, slot], other)

    loaded(1)
    for f in range(ROWS):
        xt_own[f] = x_in[f].T

    def products(n, left, weights, axis, start, stop, total=None):
        unroll = 12

        def body(i, total):
            parts = []
            for j in range(unroll):
                p = i * unroll + j
                first, second = tab[n, 2 * p], tab[n, 2 * p + 1]
                lhs = jnp.concatenate([left(first & 63), left(second & 63)], axis=1)
                rhs = jnp.concatenate(
                    [weights[NBLK - ((first >> 6) & 1023)], weights[NBLK - ((second >> 6) & 1023)]], axis=axis
                )
                parts.append(((first >> 16).astype(F32), dot(lhs, rhs, NT if axis else NN)))
            for j in range(unroll):
                total = total * parts[j][0] + parts[j][1]
                runs[i * unroll + j] = total.astype(BF)
            return total

        if total is None:
            total = jnp.zeros((B, B), F32)
        return lax.fori_loop(start, stop, body, total)

    def exchange(n, to, mine, into):
        def pick(i, carry):
            for j in range(6):
                at = i * 6 + j
                to[at] = runs[tab[3 + n, (1 - row) * ROWS + at]]
            return carry

        def own(i, carry):
            for j in range(6):
                at = i * 6 + j
                mine[at] = runs[tab[3 + n, row * ROWS + at]]
            return carry

        for c in range(2):
            lax.fori_loop(2 * c, 2 * c + 2, pick, 0)
            here = pl.ds(c * CH, CH)
            send(to.at[here], into.at[here], ex_s.at[2 * n + c], ex_r.at[2 * n + c], other)
        lax.fori_loop(0, 4, own, 0)

    loaded(2)
    begin(3)
    carried = products(0, lambda f: x_in[f], wu, 0, 0, 7)
    loaded(0)
    pl.semaphore_wait(barrier, len(peers))
    for slots in ((0, 3), (1, 5), (2, 4)):
        for kind in token_kinds:
            for slot in slots:
                token_send(kind, slot)
    products(0, lambda f: x_in[f], wu, 0, 7, 14, carried)
    exchange(0, pre_to, pre_ref, pre_in)
    for kind in token_kinds:
        for slot, source, forward in ((0, 0, 6), (3, 1, 8)):
            token_wait(kind, slot)
            share_send(kind, source)
            token_send(kind, forward)
    loaded(3)
    carried = products(1, lambda f: og_own[f], wd, 1, 0, 7)
    for kind in token_kinds:
        for slot, forward in ((1, 7), (5, 9)):
            token_wait(kind, slot)
            token_send(kind, forward)
    products(1, lambda f: og_own[f], wd, 1, 7, 14, carried)
    exchange(1, back_to, back_ref, back_in)
    for kind in token_kinds:
        token_wait(kind, 6)
        token_wait(kind, 8)
        share_send(kind, 2)

    for c in range(2):
        here = pl.ds(c * CH, CH)
        arrived(pre_in.at[here], ex_s.at[c], ex_r.at[c], other)
        arrived(back_in.at[here], ex_s.at[2 + c], ex_r.at[2 + c], other)

        def one(i, carry, c=c):
            mine = row * ROWS + c * CH + i
            pre = pre_ref[c * CH + i].astype(F32) + pre_in[c * CH + i].astype(F32)
            back = back_ref[c * CH + i].astype(F32) + back_in[c * CH + i].astype(F32)
            hidden, pre_grad = activate(pre, back)
            pg_own[mine] = pre_grad.astype(BF)
            ht_own[mine] = hidden.astype(BF).T
            return carry

        lax.fori_loop(0, CH, one, 0)
        for kind in ("pg", "ht"):
            ring_out(kind, c, "rl"[c])
            pair_out(kind, c)
    for kind in ("pg", "ht"):
        ring_out(kind, 1, "r")
        ring_out(kind, 0, "l")

    pair_wait("pg", 0)
    pair_wait("pg", 1)
    products(2, lambda h: pg_own[h], wu, 1, 0, 13)
    for f in range(ROWS):
        dxp[:, f * B : (f + 1) * B] = runs[tab[5, f]]
    for kind in token_kinds:
        share_forward(kind, 0)
        share_forward(kind, 1)
    for kind in ("pg", "ht"):
        ring_wait(kind, 0)
        ring_forward(kind, "r")
        pair_out(kind, 2)
        ring_wait(kind, 3)
        ring_forward(kind, "l")
        pair_out(kind, 5)
    for kind in token_kinds:
        share_forward(kind, 2)
    for d in range(1, SIDE):
        theirs = pl.ds(pl.multiple_of(((col + d) % SIDE) * 32, 32), 32)
        send(dxp.at[theirs], zin.at[d - 1], z_s.at[d - 1], z_r.at[d - 1], z_peers[d - 1])
    for kind in ("pg", "ht"):
        ring_wait(kind, 1)
        pair_out(kind, 3)
        ring_wait(kind, 2)
        pair_out(kind, 4)
    for kind in token_kinds:
        for slot in (2, 4, 7, 9):
            token_wait(kind, slot)
        for source in range(3):
            share_wait(kind, source, 1 - kind[0])
            share_wait(kind, source, 2)
    for slot in (4, 6, 5, 7):
        for kind in ("pg", "ht"):
            ring_wait(kind, slot)
            pair_out(kind, slot + 2)
    for kind in ("ht",):
        for slot in range(2):
            pair_wait(kind, slot)
    for slot in range(2, 10):
        for kind in ("pg", "ht"):
            pair_wait(kind, slot)

    def up_block(s):
        e = tab[6, s]
        f, h = e >> 6, e & 63
        left = jnp.concatenate([xt_own[f], xt_l[f], xt_r[f], xt_o[f]], axis=1)
        right = jnp.concatenate([pg_own[h], pg_l[h], pg_r[h], pg_o[h]], axis=0)
        return dot(left, right, NN)

    def dn_block(s):
        e = tab[7, s]
        f, h = e >> 6, e & 63
        left = jnp.concatenate([ht_own[h], ht_l[h], ht_r[h], ht_o[h]], axis=1)
        right = jnp.concatenate([og_own[f], og_l[f], og_r[f], og_o[f]], axis=0)
        return dot(left, right, NN)

    def up_base(d):
        return ((y + d) % SIDE) * (SIDE * SHARE) + x * SHARE

    def dn_base(d):
        return y * (SIDE * SHARE) + ((x + d) % SIDE) * SHARE

    half = SHARE // 2
    early, late = pl.ds(0, half), pl.ds(half, half)

    def fill(block, base, out, first, added=None):
        def body(i, carry):
            for j in range(9):
                at = first + i * 9 + j
                value = block(base + at)
                if added is not None:
                    value = value + added[i * 9 + j].astype(F32)
                out[at] = value.astype(out.dtype)
            return carry

        lax.fori_loop(0, half // 9, body, 0)

    sides = (
        (0, up_block, up_base, y_right, y_left, uf_s, ur_s, ul_s, ua_t, ub_t, ul_v, ur_v, u_acc, up_out),
        (1, dn_block, dn_base, x_right, x_left, df_s, dr_s, dl_s, da_t, db_t, dl_v, dr_v, d_acc, dn_out),
    )
    for n, block, base, to_right, to_left, f_s, r_s, l_s, a_t, b_t, l_v, r_v, acc, out in sides:
        fill(block, base(2), f_s, 0)
        send(f_s.at[early], a_t, rs_s.at[n, 0], rs_r.at[n, 0], to_right)
        fill(block, base(2), f_s, half)
        send(f_s.at[late], b_t, rs_s.at[n, 1], rs_r.at[n, 1], to_left)
    for n, block, base, to_right, to_left, f_s, r_s, l_s, a_t, b_t, l_v, r_v, acc, out in sides:
        fill(block, base(1), r_s, half)
        send(r_s.at[late], l_v.at[late], rs_s.at[n, 2], rs_r.at[n, 2], to_right)
        fill(block, base(3), l_s, 0)
        send(l_s.at[early], r_v.at[early], rs_s.at[n, 3], rs_r.at[n, 3], to_left)
    for n, block, base, to_right, to_left, f_s, r_s, l_s, a_t, b_t, l_v, r_v, acc, out in sides:
        arrived(a_t, rs_s.at[n, 0], rs_r.at[n, 0], to_left)
        fill(block, base(1), r_s, 0, a_t)
        send(r_s.at[early], l_v.at[early], rs_s.at[n, 4], rs_r.at[n, 4], to_right)
        arrived(b_t, rs_s.at[n, 1], rs_r.at[n, 1], to_right)
        fill(block, base(3), l_s, half, b_t)
        send(l_s.at[late], r_v.at[late], rs_s.at[n, 5], rs_r.at[n, 5], to_left)
    for n, block, base, to_right, to_left, f_s, r_s, l_s, a_t, b_t, l_v, r_v, acc, out in sides:
        fill(block, base(0), acc, 0)
        fill(block, base(0), acc, half)

    for d in range(1, SIDE):
        arrived(zin.at[d - 1], z_s.at[d - 1], z_r.at[d - 1], z_peers[d - 1])
    own_rows = pl.ds(pl.multiple_of(col * 32, 32), 32)
    dx_out[...] = (
        dxp[own_rows, :].astype(F32) + zin[0].astype(F32) + zin[1].astype(F32) + zin[2].astype(F32)
    ).astype(BF)
    for n, block, base, to_right, to_left, f_s, r_s, l_s, a_t, b_t, l_v, r_v, acc, out in sides:
        arrived(l_v.at[late], rs_s.at[n, 2], rs_r.at[n, 2], to_left)
        arrived(r_v.at[early], rs_s.at[n, 3], rs_r.at[n, 3], to_right)
        arrived(l_v.at[early], rs_s.at[n, 4], rs_r.at[n, 4], to_left)
        arrived(r_v.at[late], rs_s.at[n, 5], rs_r.at[n, 5], to_right)

        def total(i, carry, acc=acc, l_v=l_v, r_v=r_v, out=out):
            out[i] = (acc[i] + l_v[i].astype(F32) + r_v[i].astype(F32)).astype(BF)
            return carry

        lax.fori_loop(0, SHARE, total, 0)
    for copy in started:
        copy.wait_send()


def main(table, x, g, wu, wd):
    vmem = pl.BlockSpec(memory_space=pltpu.VMEM)
    far = pl.BlockSpec(memory_space=pl.ANY)

    def blocks(n, dtype=BF):
        return pltpu.VMEM((n, B, B), dtype)

    tokens = pltpu.VMEM((B, ROWS * B), BF)
    side = [blocks(SHARE)] * 3 + [blocks(SHARE // 2)] * 2 + [blocks(SHARE)] * 2 + [blocks(SHARE, F32)]
    dma = pltpu.SemaphoreType.DMA
    scratch = (
        [blocks(ROWS)] * 3 + [blocks(NBLK + 1), blocks(NBLK + 1), blocks(PAIRS + 1)]
        + [blocks(ROWS)] * 6
        + [blocks(COLS)] * 2
        + [blocks(ROWS)] * 3
        + [blocks(ROWS)] * 3
        + [blocks(COLS)] * 6
        + [tokens, pltpu.VMEM((3, 32, ROWS * B), BF)]
        + side
        + side
        + [dma((4,))] * 2
        + [dma((2, 8))] * 2
        + [dma((2, 10))] * 2
        + [dma((2, 6))] * 2
        + [dma((3,))] * 2
        + [dma((2,)), dma((2, ROWS))]
        + [dma((2, 10))] * 2
        + [dma((2, 3, 3))] * 2
    )
    return pl.pallas_call(
        main_kernel,
        out_shape=[
            jax.ShapeDtypeStruct((32, ROWS * B), BF),
            jax.ShapeDtypeStruct((SHARE, B, B), BF),
            jax.ShapeDtypeStruct((SHARE, B, B), BF),
        ],
        in_specs=[pl.BlockSpec(memory_space=pltpu.SMEM)] + [far] * 4,
        out_specs=[vmem] * 3,
        scratch_shapes=scratch,
        compiler_params=pltpu.CompilerParams(
            collective_id=0, has_side_effects=True, vmem_limit_bytes=62 * 2**20
        ),
        name="backward",
    )(table, x, g, wu, wd)


def results_kernel(*refs):
    count = len(refs) // 2
    for n in range(count):
        refs[count + n][...] = refs[n][...]


def results(*values):
    vmem = pl.BlockSpec(memory_space=pltpu.VMEM)
    return pl.pallas_call(
        results_kernel,
        out_shape=[jax.ShapeDtypeStruct(value.shape, value.dtype) for value in values],
        in_specs=[vmem] * len(values),
        out_specs=[vmem] * len(values),
        name="results",
    )(*values)


def shards(tokens_in, out_grad, up_weight, down_weight, up_blocks, down_blocks, owners):
    table = prepare(up_blocks[0], down_blocks[0], owners[0])
    input_grad, up_grad, down_grad = results(
        *main(table, tokens_in, out_grad, up_weight[0, 0], down_weight[0, 0])
    )
    return input_grad, up_grad[None, None], down_grad[None, None]


def solution(mesh):
    placed = (
        P("dp", "row"),
        P("dp", "row"),
        P("row", "col", None, None, None),
        P("row", "col", None, None, None),
        P("row", "col", None),
        P("row", "col", None),
        P("row", "col", None),
    )
    return jax.shard_map(
        shards,
        mesh=mesh,
        in_specs=placed,
        out_specs=(
            P(("dp", "col"), "row"),
            P("row", "col", "dp", None, None),
            P("row", "col", "dp", None, None),
        ),
        check_vma=False,
    )
```

```python
import functools

import jax
import jax.numpy as jnp
from jax import lax
from jax.experimental import pallas as pl
from jax.experimental.pallas import tpu as pltpu
from jax.sharding import PartitionSpec as P

BF = jnp.bfloat16
F32 = jnp.float32
B = 128
ROWS = 24
COLS = 48
NBLK = 288
SIDE = 4
SHARE = 18
CH = 12
PAIRS = 168
WIDE = 384
NN = (((1,), (0,)), ((), ()))
NT = (((1,), (1,)), ((), ()))
MESH = pl.DeviceIdType.MESH

root_two_pi = 0.7978845608028654
cubic_coef = 0.044715


def gelu(pre_sum):
    square = pre_sum * pre_sum
    tanh_inner = jnp.tanh(root_two_pi * (pre_sum + cubic_coef * square * pre_sum))
    half = 0.5 * (1.0 + tanh_inner)
    slope = half + 0.5 * pre_sum * (1.0 - tanh_inner * tanh_inner) * root_two_pi * (
        1.0 + 3.0 * cubic_coef * square
    )
    return pre_sum * half, slope


def dot(left, right, dims):
    return lax.dot_general(left, right, dims, preferred_element_type=F32)


def prepare_kernel(up_ref, dn_ref, own_ref, out_ref):
    def iota(shape, axis):
        return lax.broadcasted_iota(jnp.int32, shape, axis)

    square = (NBLK, NBLK)
    sub, lane = iota(square, 0), iota(square, 1)
    wide = iota((NBLK, WIDE), 1)
    one, zero = jnp.float32(1), jnp.float32(0)

    def count(mask, axis):
        return jnp.sum(jnp.where(mask, one, zero), axis=axis, keepdims=True)

    def column(row):
        picked = jnp.where(sub == lane, jnp.broadcast_to(row, square).astype(F32), zero)
        return jnp.sum(picked, axis=1, keepdims=True).astype(jnp.int32)

    def pairs(e_row, e_col, split, segment, operand):
        seg_row, seg_col = segment(e_row), segment(e_col)
        same = seg_col == seg_row
        turn = count(same & (lane < sub), 1).astype(jnp.int32)
        even = (turn & 1) == 0
        turn_row = count(same & (sub < lane), 0).astype(jnp.int32)
        even_row = (turn_row & 1) == 0
        offset = count((seg_row < seg_col) & even_row, 1).astype(jnp.int32)
        place = 2 * (offset + (turn >> 1)) + (turn & 1)
        block = NBLK - iota((NBLK, 1), 0)
        value = block * 64 + operand(e_col) + jnp.where(turn >= 2, 65536, 0)
        table = jnp.sum(jnp.where(place == wide, value.astype(F32), zero), axis=0, keepdims=True)
        through = count((seg_col <= wide) & even, 0)
        here = count((seg_col == wide) & even, 0)
        last = jnp.where(here > zero, through - one, jnp.float32(PAIRS))
        return table.astype(jnp.int32), last.astype(jnp.int32)

    up_row, dn_row, owner_row = up_ref[...], dn_ref[...], own_ref[...]
    up_col, dn_col, owner_col = column(up_row), column(dn_row), column(owner_row)

    def owned(value):
        picked = jnp.where(owner_col == wide, value.astype(F32), zero)
        return jnp.sum(picked, axis=0, keepdims=True).astype(jnp.int32)

    def div(value, by):
        return (value.astype(F32) * jnp.float32(1.0 / by) + jnp.float32(0.5 / by)).astype(jnp.int32)

    def rem(value, by):
        return value - div(value, by) * by

    t0, l0 = pairs(up_row, up_col, COLS, lambda e: rem(e, COLS), lambda e: div(e, COLS))
    t1, l1 = pairs(dn_row, dn_col, ROWS, lambda e: div(e, ROWS), lambda e: rem(e, ROWS))
    t2, l2 = pairs(up_row, up_col, COLS, lambda e: div(e, COLS), lambda e: rem(e, COLS))
    rows = (
        t0, t1, t2, l0, l1, l2,
        owned(div(up_col, COLS) * 64 + rem(up_col, COLS)),
        owned(rem(dn_col, ROWS) * 64 + div(dn_col, ROWS)),
    )
    for n, value in enumerate(rows):
        out_ref[n : n + 1, :] = value


def prepare(up, down, owner):
    return pl.pallas_call(
        prepare_kernel,
        out_shape=jax.ShapeDtypeStruct((8, WIDE), jnp.int32),
        name="prepare",
    )(up, down, owner)


def main_kernel(*refs):
    tab, x_hbm, g_hbm, wu_hbm, wd_hbm = refs[:5]
    dx_out, up_out, dn_out = refs[5:8]
    (
        x_in, og_own, xt_own, wu, wd, runs,
        pre_ref, back_ref, pre_to, back_to, pre_in, back_in, pg_own, ht_own,
        xt_l, xt_r, xt_o, og_l, og_r, og_o,
        pg_l, pg_r, pg_o, ht_l, ht_r, ht_o,
        dxp, zin,
        uf_s, ur_s, ul_s, ua_t, ub_t, ul_v, ur_v, u_acc,
        df_s, dr_s, dl_s, da_t, db_t, dl_v, dr_v, d_acc,
        ex_s, ex_r, ag_s, ag_r, pa_s, pa_r, rs_s, rs_r, z_s, z_r, in_s, col_s, to_s, to_r, sh_s, sh_r,
    ) = refs[8:]
    dp, row, col = lax.axis_index("dp"), lax.axis_index("row"), lax.axis_index("col")
    y, x = dp // SIDE, dp % SIDE
    other = (dp, 1 - row, col)
    x_right = (y * SIDE + (x + 1) % SIDE, row, col)
    x_left = (y * SIDE + (x + 3) % SIDE, row, col)
    y_right = (((y + 1) % SIDE) * SIDE + x, row, col)
    y_left = (((y + 3) % SIDE) * SIDE + x, row, col)
    z_peers = [(dp, row, (col + d) % SIDE) for d in range(1, SIDE)]

    barrier = pltpu.get_barrier_semaphore()
    peers = [other, x_right, x_left, y_right, y_left] + z_peers
    for peer in peers:
        pl.semaphore_signal(barrier, inc=1, device_id=peer, device_id_type=MESH)

    def column_loads(src, dst, n):
        return [
            pltpu.make_async_copy(src.at[:, pl.ds(f * B, B)], dst.at[f], col_s.at[n, f]) for f in range(ROWS)
        ]

    loads = [
        column_loads(g_hbm, og_own, 0),
        column_loads(x_hbm, x_in, 1),
        [pltpu.make_async_copy(wu_hbm, wu.at[pl.ds(0, NBLK)], in_s.at[0])],
        [pltpu.make_async_copy(wd_hbm, wd.at[pl.ds(0, NBLK)], in_s.at[1])],
    ]

    def loaded(n):
        for load in loads[n]:
            load.wait()

    def begin(n):
        for load in loads[n]:
            load.start()

    for n in (1, 2, 0):
        begin(n)
    wu[NBLK] = jnp.zeros((B, B), BF)
    wd[NBLK] = jnp.zeros((B, B), BF)
    runs[PAIRS] = jnp.zeros((B, B), BF)

    started = []

    def send(src, dst, send_sem, recv_sem, peer):
        copy = pltpu.make_async_remote_copy(
            src_ref=src, dst_ref=dst, send_sem=send_sem, recv_sem=recv_sem, device_id=peer, device_id_type=MESH
        )
        copy.start()
        started.append(copy)

    def arrived(dst, send_sem, recv_sem, peer):
        pltpu.make_async_remote_copy(
            src_ref=dst, dst_ref=dst, send_sem=send_sem, recv_sem=recv_sem, device_id=peer, device_id_type=MESH
        ).wait_recv()

    kinds = {
        "pg": (0, pg_own, pg_l, pg_r, pg_o, x_right, x_left),
        "ht": (1, ht_own, ht_l, ht_r, ht_o, y_right, y_left),
    }

    token_kinds = (
        (0, xt_own, (xt_l, xt_r, xt_o), x_right, x_left),
        (1, og_own, (og_l, og_r, og_o), y_right, y_left),
    )
    z_right, z_left = (dp, row, (col + 1) % SIDE), (dp, row, (col + 3) % SIDE)
    first, second = pl.ds(0, 4), pl.ds(4, 4)

    def share(step, offset=0, count=4):
        return pl.ds(8 + 4 * ((col + step) % SIDE) + offset, count)

    token_spots = (
        (0, share(0), share(0)), (0, first, first), (0, second, second),
        (1, share(0), share(0)), (1, first, first), (1, second, second),
        (2, share(0, 0, 2), 0), (2, first, 0), (2, share(0, 2, 2), 1), (2, second, 1),
    )

    def token_send(kind, slot):
        n, own, into, to_right, to_left = kind
        buffer, at, source = token_spots[slot]
        src = own if slot < 6 else into[source]
        peer = to_right if slot in (0, 1, 2, 6, 7) else to_left
        send(src.at[at], into[buffer].at[at], to_s.at[n, slot], to_r.at[n, slot], peer)

    def token_wait(kind, slot):
        n, _, into, to_right, _ = kind
        buffer, at, _ = token_spots[slot]
        arrived(into[buffer].at[at], to_s.at[n, slot], to_r.at[n, slot], to_right)

    def share_send(kind, source):
        n, _, into, _, _ = kind
        ref = into[source].at[share(0)]
        send(ref, ref, sh_s.at[n, source, 0], sh_r.at[n, source, 0], z_right)
        send(ref, ref, sh_s.at[n, source, 1], sh_r.at[n, source, 1], z_left)

    def share_wait(kind, source, way):
        n, _, into, _, _ = kind
        ref = into[source].at[share((3, 1, 2)[way])]
        arrived(ref, sh_s.at[n, source, way], sh_r.at[n, source, way], z_right)

    def share_forward(kind, source):
        n, _, into, _, _ = kind
        share_wait(kind, source, n)
        ref = into[source].at[share((3, 1)[n])]
        send(ref, ref, sh_s.at[n, source, 2], sh_r.at[n, source, 2], (z_right, z_left)[n])

    def part(c, whose=row):
        return pl.ds(whose * ROWS + c * CH, CH)

    def ring_out(kind, c, way):
        n, own, left, right, _, to_right, to_left = kinds[kind]
        at = part(c)
        if way == "r":
            send(own.at[at], left.at[at], ag_s.at[n, c], ag_r.at[n, c], to_right)
        else:
            send(own.at[at], right.at[at], ag_s.at[n, 2 + c], ag_r.at[n, 2 + c], to_left)

    def spot(kind, slot, whose=row):
        _, own, left, right, far, _, _ = kinds[kind]
        buffer = (own, own, left, left, right, right, far, far, far, far)[slot]
        if slot < 6:
            return buffer.at[part(slot % 2, whose)]
        return buffer.at[pl.ds(whose * ROWS + (slot - 6) * (CH // 2), CH // 2)]

    def ring_wait(kind, slot):
        n, to_right = kinds[kind][0], kinds[kind][5]
        arrived(spot(kind, slot + 2), ag_s.at[n, slot], ag_r.at[n, slot], to_right)

    def ring_forward(kind, way):
        n, _, left, right, far, to_right, to_left = kinds[kind]
        base = row * ROWS
        source, first, peer = (left, 4, to_right) if way == "r" else (right, 6, to_left)
        for slot in (first, first + 1):
            at = pl.ds(base + (slot - 4) * (CH // 2), CH // 2)
            send(source.at[at], far.at[at], ag_s.at[n, slot], ag_r.at[n, slot], peer)

    def pair_out(kind, slot):
        n = kinds[kind][0]
        ref = spot(kind, slot)
        send(ref, ref, pa_s.at[n, slot], pa_r.at[n, slot], other)

    def pair_wait(kind, slot):
        n = kinds[kind][0]
        ref = spot(kind, slot, 1 - row)
        arrived(ref, pa_s.at[n, slot], pa_r.at[n, slot], other)

    loaded(1)
    for f in range(ROWS):
        xt_own[f] = x_in[f].T

    def products(n, left, weights, axis, start, stop, total=None):
        unroll = 12

        def body(i, total):
            parts = []
            for j in range(unroll):
                p = i * unroll + j
                first, second = tab[n, 2 * p], tab[n, 2 * p + 1]
                lhs = jnp.concatenate([left(first & 63), left(second & 63)], axis=1)
                rhs = jnp.concatenate(
                    [weights[NBLK - ((first >> 6) & 1023)], weights[NBLK - ((second >> 6) & 1023)]], axis=axis
                )
                parts.append(((first >> 16).astype(F32), dot(lhs, rhs, NT if axis else NN)))
            for j in range(unroll):
                total = total * parts[j][0] + parts[j][1]
                runs[i * unroll + j] = total.astype(BF)
            return total

        if total is None:
            total = jnp.zeros((B, B), F32)
        return lax.fori_loop(start, stop, body, total)

    def exchange(n, to, mine, into):
        def pick(i, carry):
            for j in range(6):
                at = i * 6 + j
                to[at] = runs[tab[3 + n, (1 - row) * ROWS + at]]
            return carry

        def own(i, carry):
            for j in range(6):
                at = i * 6 + j
                mine[at] = runs[tab[3 + n, row * ROWS + at]]
            return carry

        for c in range(2):
            lax.fori_loop(2 * c, 2 * c + 2, pick, 0)
            here = pl.ds(c * CH, CH)
            send(to.at[here], into.at[here], ex_s.at[2 * n + c], ex_r.at[2 * n + c], other)
        lax.fori_loop(0, 4, own, 0)

    loaded(2)
    begin(3)
    carried = products(0, lambda f: x_in[f], wu, 0, 0, 7)
    loaded(0)
    pl.semaphore_wait(barrier, len(peers))
    for slots in ((0, 3), (1, 5), (2, 4)):
        for kind in token_kinds:
            for slot in slots:
                token_send(kind, slot)
    products(0, lambda f: x_in[f], wu, 0, 7, 14, carried)
    exchange(0, pre_to, pre_ref, pre_in)
    for kind in token_kinds:
        for slot, source, forward in ((0, 0, 6), (3, 1, 8)):
            token_wait(kind, slot)
            share_send(kind, source)
            token_send(kind, forward)
    loaded(3)
    carried = products(1, lambda f: og_own[f], wd, 1, 0, 7)
    for kind in token_kinds:
        for slot, forward in ((1, 7), (5, 9)):
            token_wait(kind, slot)
            token_send(kind, forward)

    for c in range(2):
        here = pl.ds(c * CH, CH)
        arrived(pre_in.at[here], ex_s.at[c], ex_r.at[c], other)

        def hidden_one(i, carry, c=c):
            pre = pre_ref[c * CH + i].astype(F32) + pre_in[c * CH + i].astype(F32)
            ht_own[row * ROWS + c * CH + i] = gelu(pre)[0].astype(BF).T
            return carry

        lax.fori_loop(0, CH, hidden_one, 0)
        ring_out("ht", c, "rl"[c])
        pair_out("ht", c)
    ring_out("ht", 1, "r")
    ring_out("ht", 0, "l")
    products(1, lambda f: og_own[f], wd, 1, 7, 14, carried)
    exchange(1, back_to, back_ref, back_in)
    for kind in token_kinds:
        token_wait(kind, 6)
        token_wait(kind, 8)
        share_send(kind, 2)

    for c in range(2):
        here = pl.ds(c * CH, CH)
        arrived(back_in.at[here], ex_s.at[2 + c], ex_r.at[2 + c], other)

        def grad_one(i, carry, c=c):
            pre = pre_ref[c * CH + i].astype(F32) + pre_in[c * CH + i].astype(F32)
            back = back_ref[c * CH + i].astype(F32) + back_in[c * CH + i].astype(F32)
            pg_own[row * ROWS + c * CH + i] = (back * gelu(pre)[1]).astype(BF)
            return carry

        lax.fori_loop(0, CH, grad_one, 0)
        ring_out("pg", c, "rl"[c])
        pair_out("pg", c)
    ring_out("pg", 1, "r")
    ring_out("pg", 0, "l")

    def pass_on(kind):
        ring_wait(kind, 0)
        ring_forward(kind, "r")
        pair_out(kind, 2)
        ring_wait(kind, 3)
        ring_forward(kind, "l")
        pair_out(kind, 5)

    def pass_rest(kind):
        ring_wait(kind, 1)
        pair_out(kind, 3)
        ring_wait(kind, 2)
        pair_out(kind, 4)

    def pass_far(kind):
        for slot in (4, 6, 5, 7):
            ring_wait(kind, slot)
            pair_out(kind, slot + 2)

    def tokens_in_place(kind):
        for slot in (2, 4, 7, 9):
            token_wait(kind, slot)
        for source in range(3):
            share_wait(kind, source, 1 - kind[0])
            share_wait(kind, source, 2)

    pass_on("ht")

    pair_wait("pg", 0)
    pair_wait("pg", 1)
    products(2, lambda h: pg_own[h], wu, 1, 0, 13)
    for f in range(ROWS):
        dxp[:, f * B : (f + 1) * B] = runs[tab[5, f]]
    for kind in token_kinds:
        share_forward(kind, 0)
        share_forward(kind, 1)
    pass_rest("ht")
    pass_on("pg")
    for kind in token_kinds:
        share_forward(kind, 2)
    for d in range(1, SIDE):
        theirs = pl.ds(pl.multiple_of(((col + d) % SIDE) * 32, 32), 32)
        send(dxp.at[theirs], zin.at[d - 1], z_s.at[d - 1], z_r.at[d - 1], z_peers[d - 1])
    pass_far("ht")
    pass_rest("pg")
    for slot in range(10):
        pair_wait("ht", slot)
    tokens_in_place(token_kinds[1])

    def up_block(s):
        e = tab[6, s]
        f, h = e >> 6, e & 63
        left = jnp.concatenate([xt_own[f], xt_l[f], xt_r[f], xt_o[f]], axis=1)
        right = jnp.concatenate([pg_own[h], pg_l[h], pg_r[h], pg_o[h]], axis=0)
        return dot(left, right, NN)

    def dn_block(s):
        e = tab[7, s]
        f, h = e >> 6, e & 63
        left = jnp.concatenate([ht_own[h], ht_l[h], ht_r[h], ht_o[h]], axis=1)
        right = jnp.concatenate([og_own[f], og_l[f], og_r[f], og_o[f]], axis=0)
        return dot(left, right, NN)

    def up_base(d):
        return ((y + d) % SIDE) * (SIDE * SHARE) + x * SHARE

    def dn_base(d):
        return y * (SIDE * SHARE) + ((x + d) % SIDE) * SHARE

    half = SHARE // 2
    early, late = pl.ds(0, half), pl.ds(half, half)

    def fill(block, base, out, first, added=None):
        def body(i, carry):
            for j in range(9):
                at = first + i * 9 + j
                value = block(base + at)
                if added is not None:
                    value = value + added[i * 9 + j].astype(F32)
                out[at] = value.astype(out.dtype)
            return carry

        lax.fori_loop(0, half // 9, body, 0)

    sides = (
        (0, up_block, up_base, y_right, y_left, uf_s, ur_s, ul_s, ua_t, ub_t, ul_v, ur_v, u_acc, up_out),
        (1, dn_block, dn_base, x_right, x_left, df_s, dr_s, dl_s, da_t, db_t, dl_v, dr_v, d_acc, dn_out),
    )
    def make(side, piece):
        _, block, base, _, _, f_s, r_s, l_s, _, _, _, _, acc, _ = side
        d, into, first = ((2, f_s, 0), (2, f_s, half), (1, r_s, half), (3, l_s, 0), (0, acc, 0), (0, acc, half))[piece]
        fill(block, base(d), into, first)

    def ship(side, piece):
        n, _, _, to_right, to_left, f_s, r_s, l_s, a_t, b_t, l_v, r_v, _, _ = side
        src, dst, peer = (
            (f_s.at[early], a_t, to_right),
            (f_s.at[late], b_t, to_left),
            (r_s.at[late], l_v.at[late], to_right),
            (l_s.at[early], r_v.at[early], to_left),
        )[piece]
        send(src, dst, rs_s.at[n, piece], rs_r.at[n, piece], peer)

    def finish(side):
        n, block, base, to_right, to_left, _, r_s, l_s, a_t, b_t, l_v, r_v, _, _ = side
        arrived(a_t, rs_s.at[n, 0], rs_r.at[n, 0], to_left)
        fill(block, base(1), r_s, 0, a_t)
        send(r_s.at[early], l_v.at[early], rs_s.at[n, 4], rs_r.at[n, 4], to_right)
        arrived(b_t, rs_s.at[n, 1], rs_r.at[n, 1], to_right)
        fill(block, base(3), l_s, half, b_t)
        send(l_s.at[late], r_v.at[late], rs_s.at[n, 5], rs_r.at[n, 5], to_left)

    up_side, dn_side = sides
    for piece in range(6):
        make(dn_side, piece)
    pass_far("pg")
    for piece in range(4):
        ship(dn_side, piece)
    tokens_in_place(token_kinds[0])
    for slot in range(2, 10):
        pair_wait("pg", slot)
    for piece in range(4):
        make(up_side, piece)
        ship(up_side, piece)
    finish(dn_side)
    finish(up_side)
    make(up_side, 4)
    make(up_side, 5)

    for d in range(1, SIDE):
        arrived(zin.at[d - 1], z_s.at[d - 1], z_r.at[d - 1], z_peers[d - 1])
    own_rows = pl.ds(pl.multiple_of(col * 32, 32), 32)
    dx_out[...] = (
        dxp[own_rows, :].astype(F32) + zin[0].astype(F32) + zin[1].astype(F32) + zin[2].astype(F32)
    ).astype(BF)
    for n, block, base, to_right, to_left, f_s, r_s, l_s, a_t, b_t, l_v, r_v, acc, out in sides:
        arrived(l_v.at[late], rs_s.at[n, 2], rs_r.at[n, 2], to_left)
        arrived(r_v.at[early], rs_s.at[n, 3], rs_r.at[n, 3], to_right)
        arrived(l_v.at[early], rs_s.at[n, 4], rs_r.at[n, 4], to_left)
        arrived(r_v.at[late], rs_s.at[n, 5], rs_r.at[n, 5], to_right)

        def total(i, carry, acc=acc, l_v=l_v, r_v=r_v, out=out):
            out[i] = (acc[i] + l_v[i].astype(F32) + r_v[i].astype(F32)).astype(BF)
            return carry

        lax.fori_loop(0, SHARE, total, 0)
    for copy in started:
        copy.wait_send()


def main(table, x, g, wu, wd):
    vmem = pl.BlockSpec(memory_space=pltpu.VMEM)
    far = pl.BlockSpec(memory_space=pl.ANY)

    def blocks(n, dtype=BF):
        return pltpu.VMEM((n, B, B), dtype)

    tokens = pltpu.VMEM((B, ROWS * B), BF)
    side = [blocks(SHARE)] * 3 + [blocks(SHARE // 2)] * 2 + [blocks(SHARE)] * 2 + [blocks(SHARE, F32)]
    dma = pltpu.SemaphoreType.DMA
    scratch = (
        [blocks(ROWS)] * 3 + [blocks(NBLK + 1), blocks(NBLK + 1), blocks(PAIRS + 1)]
        + [blocks(ROWS)] * 6
        + [blocks(COLS)] * 2
        + [blocks(ROWS)] * 3
        + [blocks(ROWS)] * 3
        + [blocks(COLS)] * 6
        + [tokens, pltpu.VMEM((3, 32, ROWS * B), BF)]
        + side
        + side
        + [dma((4,))] * 2
        + [dma((2, 8))] * 2
        + [dma((2, 10))] * 2
        + [dma((2, 6))] * 2
        + [dma((3,))] * 2
        + [dma((2,)), dma((2, ROWS))]
        + [dma((2, 10))] * 2
        + [dma((2, 3, 3))] * 2
    )
    return pl.pallas_call(
        main_kernel,
        out_shape=[
            jax.ShapeDtypeStruct((32, ROWS * B), BF),
            jax.ShapeDtypeStruct((SHARE, B, B), BF),
            jax.ShapeDtypeStruct((SHARE, B, B), BF),
        ],
        in_specs=[pl.BlockSpec(memory_space=pltpu.SMEM)] + [far] * 4,
        out_specs=[vmem] * 3,
        scratch_shapes=scratch,
        compiler_params=pltpu.CompilerParams(
            collective_id=0, has_side_effects=True, vmem_limit_bytes=62 * 2**20
        ),
        name="backward",
    )(table, x, g, wu, wd)


def results_kernel(*refs):
    count = len(refs) // 2
    for n in range(count):
        refs[count + n][...] = refs[n][...]


def results(*values):
    vmem = pl.BlockSpec(memory_space=pltpu.VMEM)
    return pl.pallas_call(
        results_kernel,
        out_shape=[jax.ShapeDtypeStruct(value.shape, value.dtype) for value in values],
        in_specs=[vmem] * len(values),
        out_specs=[vmem] * len(values),
        name="results",
    )(*values)


def shards(tokens_in, out_grad, up_weight, down_weight, up_blocks, down_blocks, owners):
    table = prepare(up_blocks[0], down_blocks[0], owners[0])
    input_grad, up_grad, down_grad = results(
        *main(table, tokens_in, out_grad, up_weight[0, 0], down_weight[0, 0])
    )
    return input_grad, up_grad[None, None], down_grad[None, None]


def solution(mesh):
    placed = (
        P("dp", "row"),
        P("dp", "row"),
        P("row", "col", None, None, None),
        P("row", "col", None, None, None),
        P("row", "col", None),
        P("row", "col", None),
        P("row", "col", None),
    )
    return jax.shard_map(
        shards,
        mesh=mesh,
        in_specs=placed,
        out_specs=(
            P(("dp", "col"), "row"),
            P("row", "col", "dp", None, None),
            P("row", "col", "dp", None, None),
        ),
        check_vma=False,
    )
```

```python
import functools

import jax
import jax.numpy as jnp
from jax import lax
from jax.experimental import pallas as pl
from jax.experimental.pallas import tpu as pltpu
from jax.sharding import PartitionSpec as P

BF = jnp.bfloat16
F32 = jnp.float32
B = 128
ROWS = 24
COLS = 48
NBLK = 288
SIDE = 4
SHARE = 18
CH = 12
PAIRS = 168
WIDE = 384
NN = (((1,), (0,)), ((), ()))
NT = (((1,), (1,)), ((), ()))
MESH = pl.DeviceIdType.MESH

root_two_pi = 0.7978845608028654
cubic_coef = 0.044715


def gelu(pre_sum):
    square = pre_sum * pre_sum
    tanh_inner = jnp.tanh(root_two_pi * (pre_sum + cubic_coef * square * pre_sum))
    half = 0.5 * (1.0 + tanh_inner)
    slope = half + 0.5 * pre_sum * (1.0 - tanh_inner * tanh_inner) * root_two_pi * (
        1.0 + 3.0 * cubic_coef * square
    )
    return pre_sum * half, slope


def dot(left, right, dims):
    return lax.dot_general(left, right, dims, preferred_element_type=F32)


def make_tables(up_ref, dn_ref, own_ref, out_ref):
    def iota(shape, axis):
        return lax.broadcasted_iota(jnp.int32, shape, axis)

    square = (NBLK, NBLK)
    sub, lane = iota(square, 0), iota(square, 1)
    wide = iota((NBLK, WIDE), 1)

    def total(values, axis):
        return jnp.sum(values, axis=axis, keepdims=True)

    def count(mask, axis):
        return total(jnp.where(mask, 1, 0), axis)

    def column(row):
        return total(jnp.where(sub == lane, jnp.broadcast_to(row, square), 0), 1)

    def pairs(e_row, e_col, segment, operand):
        seg_row, seg_col = segment(e_row), segment(e_col)
        same = seg_col == seg_row
        turn = count(same & (lane < sub), 1)
        even = (turn & 1) == 0
        even_row = (count(same & (sub < lane), 0) & 1) == 0
        offset = count((seg_row < seg_col) & even_row, 1)
        place = 2 * (offset + (turn >> 1)) + (turn & 1)
        block = NBLK - iota((NBLK, 1), 0)
        value = block * 64 + operand(e_col) + jnp.where(turn >= 2, 65536, 0)
        table = total(jnp.where(place == wide, value, 0), 0)
        through = count((seg_col <= wide) & even, 0)
        here = count((seg_col == wide) & even, 0)
        return table, jnp.where(here > 0, through - 1, PAIRS)

    up_row, dn_row, owner_row = up_ref[...], dn_ref[...], own_ref[...]
    up_col, dn_col, owner_col = column(up_row), column(dn_row), column(owner_row)

    def owned(value):
        return total(jnp.where(owner_col == wide, value, 0), 0)

    def by_cols(value):
        return (value * 1366) >> 16

    def by_rows(value):
        return (value * 2731) >> 16

    def in_cols(value):
        return value - by_cols(value) * COLS

    def in_rows(value):
        return value - by_rows(value) * ROWS

    t0, l0 = pairs(up_row, up_col, in_cols, by_cols)
    t1, l1 = pairs(dn_row, dn_col, by_rows, in_rows)
    t2, l2 = pairs(up_row, up_col, by_cols, in_cols)
    rows = (
        t0, t1, t2, l0, l1, l2,
        owned(by_cols(up_col) * 64 + in_cols(up_col)),
        owned(in_rows(dn_col) * 64 + by_rows(dn_col)),
    )
    for n, value in enumerate(rows):
        out_ref[n : n + 1, :] = value


def main_kernel(*refs):
    up_ref, dn_ref, own_ref, x_hbm, g_hbm, wu_hbm, wd_hbm = refs[:7]
    dx_out, up_out, dn_out = refs[7:10]
    (
        x_in, og_own, xt_own, wu, wd, runs,
        pre_ref, back_ref, pre_to, back_to, pre_in, back_in, pg_own, ht_own,
        xt_l, xt_r, xt_o, og_l, og_r, og_o,
        pg_l, pg_r, pg_o, ht_l, ht_r, ht_o,
        dxp, zin,
        uf_s, ur_s, ul_s, ua_t, ub_t, ul_v, ur_v, u_acc,
        df_s, dr_s, dl_s, da_t, db_t, dl_v, dr_v, d_acc,
        ex_s, ex_r, ag_s, ag_r, pa_s, pa_r, rs_s, rs_r, z_s, z_r, in_s, col_s, to_s, to_r, sh_s, sh_r,
        made, tab, tab_s,
    ) = refs[10:]
    dp, row, col = lax.axis_index("dp"), lax.axis_index("row"), lax.axis_index("col")
    y, x = dp // SIDE, dp % SIDE
    other = (dp, 1 - row, col)
    x_right = (y * SIDE + (x + 1) % SIDE, row, col)
    x_left = (y * SIDE + (x + 3) % SIDE, row, col)
    y_right = (((y + 1) % SIDE) * SIDE + x, row, col)
    y_left = (((y + 3) % SIDE) * SIDE + x, row, col)
    z_peers = [(dp, row, (col + d) % SIDE) for d in range(1, SIDE)]

    barrier = pltpu.get_barrier_semaphore()
    peers = [other, x_right, x_left, y_right, y_left] + z_peers
    for peer in peers:
        pl.semaphore_signal(barrier, inc=1, device_id=peer, device_id_type=MESH)

    def column_loads(src, dst, n):
        return [
            pltpu.make_async_copy(src.at[:, pl.ds(f * B, B)], dst.at[f], col_s.at[n, f]) for f in range(ROWS)
        ]

    loads = [
        column_loads(g_hbm, og_own, 0),
        column_loads(x_hbm, x_in, 1),
        [pltpu.make_async_copy(wu_hbm, wu.at[pl.ds(0, NBLK)], in_s.at[0])],
        [pltpu.make_async_copy(wd_hbm, wd.at[pl.ds(0, NBLK)], in_s.at[1])],
    ]

    def loaded(n):
        for load in loads[n]:
            load.wait()

    def begin(n):
        for load in loads[n]:
            load.start()

    for n in (1, 2, 0):
        begin(n)
    make_tables(up_ref, dn_ref, own_ref, made)
    tables = pltpu.make_async_copy(made, tab, tab_s)
    tables.start()
    wu[NBLK] = jnp.zeros((B, B), BF)
    wd[NBLK] = jnp.zeros((B, B), BF)
    runs[PAIRS] = jnp.zeros((B, B), BF)

    started = []

    def send(src, dst, send_sem, recv_sem, peer):
        copy = pltpu.make_async_remote_copy(
            src_ref=src, dst_ref=dst, send_sem=send_sem, recv_sem=recv_sem, device_id=peer, device_id_type=MESH
        )
        copy.start()
        started.append(copy)

    def arrived(dst, send_sem, recv_sem, peer):
        pltpu.make_async_remote_copy(
            src_ref=dst, dst_ref=dst, send_sem=send_sem, recv_sem=recv_sem, device_id=peer, device_id_type=MESH
        ).wait_recv()

    kinds = {
        "pg": (0, pg_own, pg_l, pg_r, pg_o, x_right, x_left),
        "ht": (1, ht_own, ht_l, ht_r, ht_o, y_right, y_left),
    }

    token_kinds = (
        (0, xt_own, (xt_l, xt_r, xt_o), x_right, x_left),
        (1, og_own, (og_l, og_r, og_o), y_right, y_left),
    )
    z_right, z_left = (dp, row, (col + 1) % SIDE), (dp, row, (col + 3) % SIDE)
    first, second = pl.ds(0, 4), pl.ds(4, 4)

    def share(step, offset=0, count=4):
        return pl.ds(8 + 4 * ((col + step) % SIDE) + offset, count)

    token_spots = (
        (0, share(0), share(0)), (0, first, first), (0, second, second),
        (1, share(0), share(0)), (1, first, first), (1, second, second),
        (2, share(0, 0, 2), 0), (2, first, 0), (2, share(0, 2, 2), 1), (2, second, 1),
    )

    def token_send(kind, slot):
        n, own, into, to_right, to_left = kind
        buffer, at, source = token_spots[slot]
        src = own if slot < 6 else into[source]
        peer = to_right if slot in (0, 1, 2, 6, 7) else to_left
        send(src.at[at], into[buffer].at[at], to_s.at[n, slot], to_r.at[n, slot], peer)

    def token_wait(kind, slot):
        n, _, into, to_right, _ = kind
        buffer, at, _ = token_spots[slot]
        arrived(into[buffer].at[at], to_s.at[n, slot], to_r.at[n, slot], to_right)

    def share_send(kind, source):
        n, _, into, _, _ = kind
        ref = into[source].at[share(0)]
        send(ref, ref, sh_s.at[n, source, 0], sh_r.at[n, source, 0], z_right)
        send(ref, ref, sh_s.at[n, source, 1], sh_r.at[n, source, 1], z_left)

    def share_wait(kind, source, way):
        n, _, into, _, _ = kind
        ref = into[source].at[share((3, 1, 2)[way])]
        arrived(ref, sh_s.at[n, source, way], sh_r.at[n, source, way], z_right)

    def share_forward(kind, source):
        n, _, into, _, _ = kind
        share_wait(kind, source, n)
        ref = into[source].at[share((3, 1)[n])]
        send(ref, ref, sh_s.at[n, source, 2], sh_r.at[n, source, 2], (z_right, z_left)[n])

    def part(c, whose=row):
        return pl.ds(whose * ROWS + c * CH, CH)

    def ring_out(kind, c, way):
        n, own, left, right, _, to_right, to_left = kinds[kind]
        at = part(c)
        if way == "r":
            send(own.at[at], left.at[at], ag_s.at[n, c], ag_r.at[n, c], to_right)
        else:
            send(own.at[at], right.at[at], ag_s.at[n, 2 + c], ag_r.at[n, 2 + c], to_left)

    def spot(kind, slot, whose=row):
        _, own, left, right, far, _, _ = kinds[kind]
        buffer = (own, own, left, left, right, right, far, far, far, far)[slot]
        if slot < 6:
            return buffer.at[part(slot % 2, whose)]
        return buffer.at[pl.ds(whose * ROWS + (slot - 6) * (CH // 2), CH // 2)]

    def ring_wait(kind, slot):
        n, to_right = kinds[kind][0], kinds[kind][5]
        arrived(spot(kind, slot + 2), ag_s.at[n, slot], ag_r.at[n, slot], to_right)

    def ring_forward(kind, way):
        n, _, left, right, far, to_right, to_left = kinds[kind]
        base = row * ROWS
        source, first, peer = (left, 4, to_right) if way == "r" else (right, 6, to_left)
        for slot in (first, first + 1):
            at = pl.ds(base + (slot - 4) * (CH // 2), CH // 2)
            send(source.at[at], far.at[at], ag_s.at[n, slot], ag_r.at[n, slot], peer)

    def pair_out(kind, slot):
        n = kinds[kind][0]
        ref = spot(kind, slot)
        send(ref, ref, pa_s.at[n, slot], pa_r.at[n, slot], other)

    def pair_wait(kind, slot):
        n = kinds[kind][0]
        ref = spot(kind, slot, 1 - row)
        arrived(ref, pa_s.at[n, slot], pa_r.at[n, slot], other)

    loaded(1)
    for f in range(ROWS):
        xt_own[f] = x_in[f].T

    def products(n, left, weights, axis, start, stop, total=None):
        unroll = 28

        def body(i, total):
            parts = []
            for j in range(unroll):
                p = i * unroll + j
                first, second = tab[n, 2 * p], tab[n, 2 * p + 1]
                lhs = jnp.concatenate([left(first & 63), left(second & 63)], axis=1)
                rhs = jnp.concatenate(
                    [weights[NBLK - ((first >> 6) & 1023)], weights[NBLK - ((second >> 6) & 1023)]], axis=axis
                )
                parts.append(((first >> 16).astype(F32), dot(lhs, rhs, NT if axis else NN)))
            for j in range(unroll):
                total = total * parts[j][0] + parts[j][1]
                runs[i * unroll + j] = total.astype(BF)
            return total

        if total is None:
            total = jnp.zeros((B, B), F32)
        return lax.fori_loop(start, stop, body, total)

    def exchange(n, to, mine, into):
        def pick(i, carry):
            for j in range(6):
                at = i * 6 + j
                to[at] = runs[tab[3 + n, (1 - row) * ROWS + at]]
            return carry

        def own(i, carry):
            for j in range(6):
                at = i * 6 + j
                mine[at] = runs[tab[3 + n, row * ROWS + at]]
            return carry

        for c in range(2):
            lax.fori_loop(2 * c, 2 * c + 2, pick, 0)
            here = pl.ds(c * CH, CH)
            send(to.at[here], into.at[here], ex_s.at[2 * n + c], ex_r.at[2 * n + c], other)
        lax.fori_loop(0, 4, own, 0)

    tables.wait()
    loaded(2)
    begin(3)
    carried = products(0, lambda f: x_in[f], wu, 0, 0, 3)
    loaded(0)
    pl.semaphore_wait(barrier, len(peers))
    for slots in ((0, 3), (1, 5), (2, 4)):
        for kind in token_kinds:
            for slot in slots:
                token_send(kind, slot)
    products(0, lambda f: x_in[f], wu, 0, 3, 6, carried)
    exchange(0, pre_to, pre_ref, pre_in)
    for kind in token_kinds:
        for slot, source, forward in ((0, 0, 6), (3, 1, 8)):
            token_wait(kind, slot)
            share_send(kind, source)
            token_send(kind, forward)
    loaded(3)
    carried = products(1, lambda f: og_own[f], wd, 1, 0, 3)
    for kind in token_kinds:
        for slot, forward in ((1, 7), (5, 9)):
            token_wait(kind, slot)
            token_send(kind, forward)

    for c in range(2):
        here = pl.ds(c * CH, CH)
        arrived(pre_in.at[here], ex_s.at[c], ex_r.at[c], other)

        def hidden_one(i, carry, c=c):
            pre = pre_ref[c * CH + i].astype(F32) + pre_in[c * CH + i].astype(F32)
            ht_own[row * ROWS + c * CH + i] = gelu(pre)[0].astype(BF).T
            return carry

        lax.fori_loop(0, CH, hidden_one, 0)
        ring_out("ht", c, "rl"[c])
        pair_out("ht", c)
    ring_out("ht", 1, "r")
    ring_out("ht", 0, "l")
    products(1, lambda f: og_own[f], wd, 1, 3, 6, carried)
    exchange(1, back_to, back_ref, back_in)
    for kind in token_kinds:
        token_wait(kind, 6)
        token_wait(kind, 8)
        share_send(kind, 2)

    for c in range(2):
        here = pl.ds(c * CH, CH)
        arrived(back_in.at[here], ex_s.at[2 + c], ex_r.at[2 + c], other)

        def grad_one(i, carry, c=c):
            pre = pre_ref[c * CH + i].astype(F32) + pre_in[c * CH + i].astype(F32)
            back = back_ref[c * CH + i].astype(F32) + back_in[c * CH + i].astype(F32)
            pg_own[row * ROWS + c * CH + i] = (back * gelu(pre)[1]).astype(BF)
            return carry

        lax.fori_loop(0, CH, grad_one, 0)
        ring_out("pg", c, "rl"[c])
        pair_out("pg", c)
    ring_out("pg", 1, "r")
    ring_out("pg", 0, "l")

    def pass_on(kind):
        ring_wait(kind, 0)
        ring_forward(kind, "r")
        pair_out(kind, 2)
        ring_wait(kind, 3)
        ring_forward(kind, "l")
        pair_out(kind, 5)

    def pass_rest(kind):
        ring_wait(kind, 1)
        pair_out(kind, 3)
        ring_wait(kind, 2)
        pair_out(kind, 4)

    def pass_far(kind):
        for slot in (4, 6, 5, 7):
            ring_wait(kind, slot)
            pair_out(kind, slot + 2)

    def tokens_in_place(kind):
        for slot in (2, 4, 7, 9):
            token_wait(kind, slot)
        for source in range(3):
            share_wait(kind, source, 1 - kind[0])
            share_wait(kind, source, 2)

    pass_on("ht")

    pair_wait("pg", 0)
    pair_wait("pg", 1)
    products(2, lambda h: pg_own[h], wu, 1, 0, 6)
    for f in range(ROWS):
        dxp[:, f * B : (f + 1) * B] = runs[tab[5, f]]
    for kind in token_kinds:
        share_forward(kind, 0)
        share_forward(kind, 1)
    pass_rest("ht")
    pass_on("pg")
    for kind in token_kinds:
        share_forward(kind, 2)
    for d in range(1, SIDE):
        theirs = pl.ds(pl.multiple_of(((col + d) % SIDE) * 32, 32), 32)
        send(dxp.at[theirs], zin.at[d - 1], z_s.at[d - 1], z_r.at[d - 1], z_peers[d - 1])
    pass_far("ht")
    pass_rest("pg")
    for slot in range(10):
        pair_wait("ht", slot)
    tokens_in_place(token_kinds[1])

    def up_block(s):
        e = tab[6, s]
        f, h = e >> 6, e & 63
        left = jnp.concatenate([xt_own[f], xt_l[f], xt_r[f], xt_o[f]], axis=1)
        right = jnp.concatenate([pg_own[h], pg_l[h], pg_r[h], pg_o[h]], axis=0)
        return dot(left, right, NN)

    def dn_block(s):
        e = tab[7, s]
        f, h = e >> 6, e & 63
        left = jnp.concatenate([ht_own[h], ht_l[h], ht_r[h], ht_o[h]], axis=1)
        right = jnp.concatenate([og_own[f], og_l[f], og_r[f], og_o[f]], axis=0)
        return dot(left, right, NN)

    def up_base(d):
        return ((y + d) % SIDE) * (SIDE * SHARE) + x * SHARE

    def dn_base(d):
        return y * (SIDE * SHARE) + ((x + d) % SIDE) * SHARE

    half = SHARE // 2
    early, late = pl.ds(0, half), pl.ds(half, half)

    def fill(block, base, out, first, added=None):
        def body(i, carry):
            for j in range(9):
                at = first + i * 9 + j
                value = block(base + at)
                if added is not None:
                    value = value + added[i * 9 + j].astype(F32)
                out[at] = value.astype(out.dtype)
            return carry

        lax.fori_loop(0, half // 9, body, 0)

    sides = (
        (0, up_block, up_base, y_right, y_left, uf_s, ur_s, ul_s, ua_t, ub_t, ul_v, ur_v, u_acc, up_out),
        (1, dn_block, dn_base, x_right, x_left, df_s, dr_s, dl_s, da_t, db_t, dl_v, dr_v, d_acc, dn_out),
    )
    def make(side, piece):
        _, block, base, _, _, f_s, r_s, l_s, _, _, _, _, acc, _ = side
        d, into, first = ((2, f_s, 0), (2, f_s, half), (1, r_s, half), (3, l_s, 0), (0, acc, 0), (0, acc, half))[piece]
        fill(block, base(d), into, first)

    def ship(side, piece):
        n, _, _, to_right, to_left, f_s, r_s, l_s, a_t, b_t, l_v, r_v, _, _ = side
        src, dst, peer = (
            (f_s.at[early], a_t, to_right),
            (f_s.at[late], b_t, to_left),
            (r_s.at[late], l_v.at[late], to_right),
            (l_s.at[early], r_v.at[early], to_left),
        )[piece]
        send(src, dst, rs_s.at[n, piece], rs_r.at[n, piece], peer)

    def finish(side):
        n, block, base, to_right, to_left, _, r_s, l_s, a_t, b_t, l_v, r_v, _, _ = side
        arrived(a_t, rs_s.at[n, 0], rs_r.at[n, 0], to_left)
        fill(block, base(1), r_s, 0, a_t)
        send(r_s.at[early], l_v.at[early], rs_s.at[n, 4], rs_r.at[n, 4], to_right)
        arrived(b_t, rs_s.at[n, 1], rs_r.at[n, 1], to_right)
        fill(block, base(3), l_s, half, b_t)
        send(l_s.at[late], r_v.at[late], rs_s.at[n, 5], rs_r.at[n, 5], to_left)

    up_side, dn_side = sides
    for piece in range(6):
        make(dn_side, piece)
    pass_far("pg")
    for piece in range(4):
        ship(dn_side, piece)
    tokens_in_place(token_kinds[0])
    for slot in range(2, 10):
        pair_wait("pg", slot)
    for piece in range(4):
        make(up_side, piece)
        ship(up_side, piece)
    finish(dn_side)
    finish(up_side)
    make(up_side, 4)
    make(up_side, 5)

    for d in range(1, SIDE):
        arrived(zin.at[d - 1], z_s.at[d - 1], z_r.at[d - 1], z_peers[d - 1])
    own_rows = pl.ds(pl.multiple_of(col * 32, 32), 32)
    dx_out[...] = (
        dxp[own_rows, :].astype(F32) + zin[0].astype(F32) + zin[1].astype(F32) + zin[2].astype(F32)
    ).astype(BF)
    for n, block, base, to_right, to_left, f_s, r_s, l_s, a_t, b_t, l_v, r_v, acc, out in sides:
        arrived(l_v.at[late], rs_s.at[n, 2], rs_r.at[n, 2], to_left)
        arrived(r_v.at[early], rs_s.at[n, 3], rs_r.at[n, 3], to_right)
        arrived(l_v.at[early], rs_s.at[n, 4], rs_r.at[n, 4], to_left)
        arrived(r_v.at[late], rs_s.at[n, 5], rs_r.at[n, 5], to_right)

        def total(i, carry, acc=acc, l_v=l_v, r_v=r_v, out=out):
            out[i] = (acc[i] + l_v[i].astype(F32) + r_v[i].astype(F32)).astype(BF)
            return carry

        lax.fori_loop(0, SHARE, total, 0)
    for copy in started:
        copy.wait_send()


def main(up, dn, owner, x, g, wu, wd):
    vmem = pl.BlockSpec(memory_space=pltpu.VMEM)
    far = pl.BlockSpec(memory_space=pl.ANY)

    def blocks(n, dtype=BF):
        return pltpu.VMEM((n, B, B), dtype)

    tokens = pltpu.VMEM((B, ROWS * B), BF)
    side = [blocks(SHARE)] * 3 + [blocks(SHARE // 2)] * 2 + [blocks(SHARE)] * 2 + [blocks(SHARE, F32)]
    dma = pltpu.SemaphoreType.DMA
    scratch = (
        [blocks(ROWS)] * 3 + [blocks(NBLK + 1), blocks(NBLK + 1), blocks(PAIRS + 1)]
        + [blocks(ROWS)] * 6
        + [blocks(COLS)] * 2
        + [blocks(ROWS)] * 3
        + [blocks(ROWS)] * 3
        + [blocks(COLS)] * 6
        + [tokens, pltpu.VMEM((3, 32, ROWS * B), BF)]
        + side
        + side
        + [dma((4,))] * 2
        + [dma((2, 8))] * 2
        + [dma((2, 10))] * 2
        + [dma((2, 6))] * 2
        + [dma((3,))] * 2
        + [dma((2,)), dma((2, ROWS))]
        + [dma((2, 10))] * 2
        + [dma((2, 3, 3))] * 2
        + [pltpu.VMEM((8, WIDE), jnp.int32), pltpu.SMEM((8, WIDE), jnp.int32), dma(())]
    )
    return pl.pallas_call(
        main_kernel,
        out_shape=[
            jax.ShapeDtypeStruct((32, ROWS * B), BF),
            jax.ShapeDtypeStruct((SHARE, B, B), BF),
            jax.ShapeDtypeStruct((SHARE, B, B), BF),
        ],
        in_specs=[vmem] * 3 + [far] * 4,
        out_specs=[vmem] * 3,
        scratch_shapes=scratch,
        compiler_params=pltpu.CompilerParams(
            collective_id=0, has_side_effects=True, vmem_limit_bytes=62 * 2**20
        ),
        name="backward",
    )(up, dn, owner, x, g, wu, wd)


def results_kernel(*refs):
    count = len(refs) // 2
    for n in range(count):
        refs[count + n][...] = refs[n][...]


def results(*values):
    vmem = pl.BlockSpec(memory_space=pltpu.VMEM)
    return pl.pallas_call(
        results_kernel,
        out_shape=[jax.ShapeDtypeStruct(value.shape, value.dtype) for value in values],
        in_specs=[vmem] * len(values),
        out_specs=[vmem] * len(values),
        name="results",
    )(*values)


def shards(tokens_in, out_grad, up_weight, down_weight, up_blocks, down_blocks, owners):
    input_grad, up_grad, down_grad = results(
        *main(
            up_blocks[0], down_blocks[0], owners[0], tokens_in, out_grad, up_weight[0, 0], down_weight[0, 0]
        )
    )
    return input_grad, up_grad[None, None], down_grad[None, None]


def solution(mesh):
    placed = (
        P("dp", "row"),
        P("dp", "row"),
        P("row", "col", None, None, None),
        P("row", "col", None, None, None),
        P("row", "col", None),
        P("row", "col", None),
        P("row", "col", None),
    )
    return jax.shard_map(
        shards,
        mesh=mesh,
        in_specs=placed,
        out_specs=(
            P(("dp", "col"), "row"),
            P("row", "col", "dp", None, None),
            P("row", "col", "dp", None, None),
        ),
        check_vma=False,
    )
```

```python
import functools

import jax
import jax.numpy as jnp
from jax import lax
from jax.experimental import pallas as pl
from jax.experimental.pallas import tpu as pltpu
from jax.sharding import PartitionSpec as P

BF = jnp.bfloat16
F32 = jnp.float32
B = 128
ROWS = 24
COLS = 48
NBLK = 288
SIDE = 4
SHARE = 18
CH = 12
PAIRS = 168
WIDE = 384
NN = (((1,), (0,)), ((), ()))
NT = (((1,), (1,)), ((), ()))
MESH = pl.DeviceIdType.MESH

root_two_pi = 0.7978845608028654
cubic_coef = 0.044715


def gelu(pre_sum):
    square = pre_sum * pre_sum
    tanh_inner = jnp.tanh(root_two_pi * (pre_sum + cubic_coef * square * pre_sum))
    half = 0.5 * (1.0 + tanh_inner)
    slope = half + 0.5 * pre_sum * (1.0 - tanh_inner * tanh_inner) * root_two_pi * (
        1.0 + 3.0 * cubic_coef * square
    )
    return pre_sum * half, slope


def dot(left, right, dims):
    return lax.dot_general(left, right, dims, preferred_element_type=F32)


def make_tables(up_ref, dn_ref, own_ref, out_ref):
    def iota(shape, axis):
        return lax.broadcasted_iota(jnp.int32, shape, axis)

    square = (NBLK, NBLK)
    sub, lane = iota(square, 0), iota(square, 1)
    wide = iota((NBLK, WIDE), 1)

    def total(values, axis):
        return jnp.sum(values, axis=axis, keepdims=True)

    def count(mask, axis):
        return total(jnp.where(mask, 1, 0), axis)

    def column(row):
        return total(jnp.where(sub == lane, jnp.broadcast_to(row, square), 0), 1)

    def pairs(e_row, e_col, segment, operand):
        seg_row, seg_col = segment(e_row), segment(e_col)
        same = seg_col == seg_row
        turn = count(same & (lane < sub), 1)
        even = (turn & 1) == 0
        even_row = (count(same & (sub < lane), 0) & 1) == 0
        offset = count((seg_row < seg_col) & even_row, 1)
        place = 2 * (offset + (turn >> 1)) + (turn & 1)
        block = NBLK - iota((NBLK, 1), 0)
        value = block * 64 + operand(e_col) + jnp.where(turn >= 2, 65536, 0)
        table = total(jnp.where(place == wide, value, 0), 0)
        through = count((seg_col <= wide) & even, 0)
        here = count((seg_col == wide) & even, 0)
        return table, jnp.where(here > 0, through - 1, PAIRS)

    up_row, dn_row, owner_row = up_ref[...], dn_ref[...], own_ref[...]
    up_col, dn_col, owner_col = column(up_row), column(dn_row), column(owner_row)

    def owned(value):
        return total(jnp.where(owner_col == wide, value, 0), 0)

    def by_cols(value):
        return (value * 1366) >> 16

    def by_rows(value):
        return (value * 2731) >> 16

    def in_cols(value):
        return value - by_cols(value) * COLS

    def in_rows(value):
        return value - by_rows(value) * ROWS

    t0, l0 = pairs(up_row, up_col, in_cols, by_cols)
    t1, l1 = pairs(dn_row, dn_col, by_rows, in_rows)
    t2, l2 = pairs(up_row, up_col, by_cols, in_cols)
    rows = (
        t0, t1, t2, l0, l1, l2,
        owned(by_cols(up_col) * 64 + in_cols(up_col)),
        owned(in_rows(dn_col) * 64 + by_rows(dn_col)),
    )
    for n, value in enumerate(rows):
        out_ref[n : n + 1, :] = value


def main_kernel(*refs):
    up_ref, dn_ref, own_ref, x_hbm, g_hbm, wu_hbm, wd_hbm = refs[:7]
    dx_out, up_out, dn_out = refs[7:10]
    (
        x_in, og_own, xt_own, wu, wd, runs,
        pre_ref, back_ref, pre_to, back_to, pre_in, back_in, pg_own, ht_own,
        xt_l, xt_r, xt_o, og_l, og_r, og_o,
        pg_l, pg_r, pg_o, ht_l, ht_r, ht_o,
        dxp, zin,
        uf_s, ur_s, ul_s, ua_t, ub_t, ul_v, ur_v, u_acc,
        df_s, dr_s, dl_s, da_t, db_t, dl_v, dr_v, d_acc,
        ex_s, ex_r, ag_s, ag_r, pa_s, pa_r, rs_s, rs_r, z_s, z_r, in_s, col_s, to_s, to_r, sh_s, sh_r,
        made, tab, tab_s,
    ) = refs[10:]
    dp, row, col = lax.axis_index("dp"), lax.axis_index("row"), lax.axis_index("col")
    y, x = dp // SIDE, dp % SIDE
    other = (dp, 1 - row, col)
    x_right = (y * SIDE + (x + 1) % SIDE, row, col)
    x_left = (y * SIDE + (x + 3) % SIDE, row, col)
    y_right = (((y + 1) % SIDE) * SIDE + x, row, col)
    y_left = (((y + 3) % SIDE) * SIDE + x, row, col)
    z_peers = [(dp, row, (col + d) % SIDE) for d in range(1, SIDE)]

    barrier = pltpu.get_barrier_semaphore()
    peers = [other, x_right, x_left, y_right, y_left] + z_peers
    for peer in peers:
        pl.semaphore_signal(barrier, inc=1, device_id=peer, device_id_type=MESH)

    def column_loads(src, dst, n):
        return [
            pltpu.make_async_copy(src.at[:, pl.ds(f * B, B)], dst.at[f], col_s.at[n, f]) for f in range(ROWS)
        ]

    loads = [
        column_loads(g_hbm, og_own, 0),
        column_loads(x_hbm, x_in, 1),
        [pltpu.make_async_copy(wu_hbm, wu.at[pl.ds(0, NBLK)], in_s.at[0])],
        [pltpu.make_async_copy(wd_hbm, wd.at[pl.ds(0, NBLK)], in_s.at[1])],
    ]

    def loaded(n):
        for load in loads[n]:
            load.wait()

    def begin(n):
        for load in loads[n]:
            load.start()

    for n in (1, 2, 0):
        begin(n)
    make_tables(up_ref, dn_ref, own_ref, made)
    tables = pltpu.make_async_copy(made, tab, tab_s)
    tables.start()
    wu[NBLK] = jnp.zeros((B, B), BF)
    wd[NBLK] = jnp.zeros((B, B), BF)
    runs[PAIRS] = jnp.zeros((B, B), BF)

    started = []

    def send(src, dst, send_sem, recv_sem, peer):
        copy = pltpu.make_async_remote_copy(
            src_ref=src, dst_ref=dst, send_sem=send_sem, recv_sem=recv_sem, device_id=peer, device_id_type=MESH
        )
        copy.start()
        started.append(copy)

    def arrived(dst, send_sem, recv_sem, peer):
        pltpu.make_async_remote_copy(
            src_ref=dst, dst_ref=dst, send_sem=send_sem, recv_sem=recv_sem, device_id=peer, device_id_type=MESH
        ).wait_recv()

    kinds = {
        "pg": (0, pg_own, pg_l, pg_r, pg_o, x_right, x_left),
        "ht": (1, ht_own, ht_l, ht_r, ht_o, y_right, y_left),
    }

    token_kinds = (
        (0, xt_own, (xt_l, xt_r, xt_o), x_right, x_left),
        (1, og_own, (og_l, og_r, og_o), y_right, y_left),
    )
    z_right, z_left = (dp, row, (col + 1) % SIDE), (dp, row, (col + 3) % SIDE)
    first, second = pl.ds(0, 4), pl.ds(4, 4)

    def share(step, offset=0, count=4):
        return pl.ds(8 + 4 * ((col + step) % SIDE) + offset, count)

    token_spots = (
        (0, share(0), share(0)), (0, first, first), (0, second, second),
        (1, share(0), share(0)), (1, first, first), (1, second, second),
        (2, share(0, 0, 2), 0), (2, first, 0), (2, share(0, 2, 2), 1), (2, second, 1),
    )

    def token_send(kind, slot):
        n, own, into, to_right, to_left = kind
        buffer, at, source = token_spots[slot]
        src = own if slot < 6 else into[source]
        peer = to_right if slot in (0, 1, 2, 6, 7) else to_left
        send(src.at[at], into[buffer].at[at], to_s.at[n, slot], to_r.at[n, slot], peer)

    def token_wait(kind, slot):
        n, _, into, to_right, _ = kind
        buffer, at, _ = token_spots[slot]
        arrived(into[buffer].at[at], to_s.at[n, slot], to_r.at[n, slot], to_right)

    def share_send(kind, source):
        n, _, into, _, _ = kind
        ref = into[source].at[share(0)]
        send(ref, ref, sh_s.at[n, source, 0], sh_r.at[n, source, 0], z_right)
        send(ref, ref, sh_s.at[n, source, 1], sh_r.at[n, source, 1], z_left)

    def share_wait(kind, source, way):
        n, _, into, _, _ = kind
        ref = into[source].at[share((3, 1, 2)[way])]
        arrived(ref, sh_s.at[n, source, way], sh_r.at[n, source, way], z_right)

    def share_forward(kind, source):
        n, _, into, _, _ = kind
        share_wait(kind, source, n)
        ref = into[source].at[share((3, 1)[n])]
        send(ref, ref, sh_s.at[n, source, 2], sh_r.at[n, source, 2], (z_right, z_left)[n])

    def part(c, whose=row):
        return pl.ds(whose * ROWS + c * CH, CH)

    def ring_out(kind, c, way):
        n, own, left, right, _, to_right, to_left = kinds[kind]
        at = part(c)
        if way == "r":
            send(own.at[at], left.at[at], ag_s.at[n, c], ag_r.at[n, c], to_right)
        else:
            send(own.at[at], right.at[at], ag_s.at[n, 2 + c], ag_r.at[n, 2 + c], to_left)

    def spot(kind, slot, whose=row):
        _, own, left, right, far, _, _ = kinds[kind]
        buffer = (own, own, left, left, right, right, far, far, far, far)[slot]
        if slot < 6:
            return buffer.at[part(slot % 2, whose)]
        return buffer.at[pl.ds(whose * ROWS + (slot - 6) * (CH // 2), CH // 2)]

    def ring_wait(kind, slot):
        n, to_right = kinds[kind][0], kinds[kind][5]
        arrived(spot(kind, slot + 2), ag_s.at[n, slot], ag_r.at[n, slot], to_right)

    def ring_forward(kind, way):
        n, _, left, right, far, to_right, to_left = kinds[kind]
        base = row * ROWS
        source, first, peer = (left, 4, to_right) if way == "r" else (right, 6, to_left)
        for slot in (first, first + 1):
            at = pl.ds(base + (slot - 4) * (CH // 2), CH // 2)
            send(source.at[at], far.at[at], ag_s.at[n, slot], ag_r.at[n, slot], peer)

    def pair_out(kind, slot):
        n = kinds[kind][0]
        ref = spot(kind, slot)
        send(ref, ref, pa_s.at[n, slot], pa_r.at[n, slot], other)

    def pair_wait(kind, slot):
        n = kinds[kind][0]
        ref = spot(kind, slot, 1 - row)
        arrived(ref, pa_s.at[n, slot], pa_r.at[n, slot], other)

    loaded(1)
    for f in range(ROWS):
        xt_own[f] = x_in[f].T

    def products(n, left, weights, axis, start, stop, total=None):
        unroll = 28

        def body(i, total):
            parts = []
            for j in range(unroll):
                p = i * unroll + j
                first, second = tab[n, 2 * p], tab[n, 2 * p + 1]
                lhs = jnp.concatenate([left(first & 63), left(second & 63)], axis=1)
                rhs = jnp.concatenate(
                    [weights[NBLK - ((first >> 6) & 1023)], weights[NBLK - ((second >> 6) & 1023)]], axis=axis
                )
                parts.append(((first >> 16).astype(F32), dot(lhs, rhs, NT if axis else NN)))
            for j in range(unroll):
                total = total * parts[j][0] + parts[j][1]
                runs[i * unroll + j] = total.astype(BF)
            return total

        if total is None:
            total = jnp.zeros((B, B), F32)
        return lax.fori_loop(start, stop, body, total)

    def exchange(n, to, mine, into):
        def pick(i, carry):
            for j in range(6):
                at = i * 6 + j
                to[at] = runs[tab[3 + n, (1 - row) * ROWS + at]]
            return carry

        def own(i, carry):
            for j in range(6):
                at = i * 6 + j
                mine[at] = runs[tab[3 + n, row * ROWS + at]]
            return carry

        for c in range(2):
            lax.fori_loop(2 * c, 2 * c + 2, pick, 0)
            here = pl.ds(c * CH, CH)
            send(to.at[here], into.at[here], ex_s.at[2 * n + c], ex_r.at[2 * n + c], other)
        lax.fori_loop(0, 4, own, 0)

    tables.wait()
    loaded(2)
    begin(3)
    products(0, lambda f: x_in[f], wu, 0, 0, 6)
    loaded(0)
    pl.semaphore_wait(barrier, len(peers))
    exchange(0, pre_to, pre_ref, pre_in)
    for slots in ((0, 3), (1, 5), (2, 4)):
        for kind in token_kinds:
            for slot in slots:
                token_send(kind, slot)
    loaded(3)
    carried = products(1, lambda f: og_own[f], wd, 1, 0, 3)
    for kind in token_kinds:
        for slot, source, forward in ((0, 0, 6), (3, 1, 8)):
            token_wait(kind, slot)
            share_send(kind, source)
            token_send(kind, forward)

    for c in range(2):
        here = pl.ds(c * CH, CH)
        arrived(pre_in.at[here], ex_s.at[c], ex_r.at[c], other)

        def hidden_one(i, carry, c=c):
            pre = pre_ref[c * CH + i].astype(F32) + pre_in[c * CH + i].astype(F32)
            ht_own[row * ROWS + c * CH + i] = gelu(pre)[0].astype(BF).T
            return carry

        lax.fori_loop(0, CH, hidden_one, 0)
        ring_out("ht", c, "rl"[c])
        pair_out("ht", c)
    ring_out("ht", 1, "r")
    ring_out("ht", 0, "l")
    for kind in token_kinds:
        for slot, forward in ((1, 7), (5, 9)):
            token_wait(kind, slot)
            token_send(kind, forward)
    products(1, lambda f: og_own[f], wd, 1, 3, 6, carried)
    exchange(1, back_to, back_ref, back_in)

    for c in range(2):
        here = pl.ds(c * CH, CH)
        arrived(back_in.at[here], ex_s.at[2 + c], ex_r.at[2 + c], other)

        def grad_one(i, carry, c=c):
            pre = pre_ref[c * CH + i].astype(F32) + pre_in[c * CH + i].astype(F32)
            back = back_ref[c * CH + i].astype(F32) + back_in[c * CH + i].astype(F32)
            pg_own[row * ROWS + c * CH + i] = (back * gelu(pre)[1]).astype(BF)
            return carry

        lax.fori_loop(0, CH, grad_one, 0)
        ring_out("pg", c, "rl"[c])
        pair_out("pg", c)
    ring_out("pg", 1, "r")
    ring_out("pg", 0, "l")

    def pass_on(kind):
        ring_wait(kind, 0)
        ring_forward(kind, "r")
        pair_out(kind, 2)
        ring_wait(kind, 3)
        ring_forward(kind, "l")
        pair_out(kind, 5)

    def pass_rest(kind):
        ring_wait(kind, 1)
        pair_out(kind, 3)
        ring_wait(kind, 2)
        pair_out(kind, 4)

    def pass_far(kind):
        for slot in (4, 6, 5, 7):
            ring_wait(kind, slot)
            pair_out(kind, slot + 2)

    def tokens_in_place(kind):
        for slot in (2, 4, 7, 9):
            token_wait(kind, slot)
        for source in range(3):
            share_wait(kind, source, 1 - kind[0])
            share_wait(kind, source, 2)

    for kind in token_kinds:
        token_wait(kind, 6)
        token_wait(kind, 8)
        share_send(kind, 2)
    pass_on("ht")

    pair_wait("pg", 0)
    pair_wait("pg", 1)
    products(2, lambda h: pg_own[h], wu, 1, 0, 6)
    for f in range(ROWS):
        dxp[:, f * B : (f + 1) * B] = runs[tab[5, f]]
    for kind in token_kinds:
        share_forward(kind, 0)
        share_forward(kind, 1)
    pass_rest("ht")
    pass_on("pg")
    for kind in token_kinds:
        share_forward(kind, 2)
    for d in range(1, SIDE):
        theirs = pl.ds(pl.multiple_of(((col + d) % SIDE) * 32, 32), 32)
        send(dxp.at[theirs], zin.at[d - 1], z_s.at[d - 1], z_r.at[d - 1], z_peers[d - 1])
    pass_far("ht")
    pass_rest("pg")
    for slot in range(10):
        pair_wait("ht", slot)
    tokens_in_place(token_kinds[1])

    def up_block(s):
        e = tab[6, s]
        f, h = e >> 6, e & 63
        left = jnp.concatenate([xt_own[f], xt_l[f], xt_r[f], xt_o[f]], axis=1)
        right = jnp.concatenate([pg_own[h], pg_l[h], pg_r[h], pg_o[h]], axis=0)
        return dot(left, right, NN)

    def dn_block(s):
        e = tab[7, s]
        f, h = e >> 6, e & 63
        left = jnp.concatenate([ht_own[h], ht_l[h], ht_r[h], ht_o[h]], axis=1)
        right = jnp.concatenate([og_own[f], og_l[f], og_r[f], og_o[f]], axis=0)
        return dot(left, right, NN)

    def up_base(d):
        return ((y + d) % SIDE) * (SIDE * SHARE) + x * SHARE

    def dn_base(d):
        return y * (SIDE * SHARE) + ((x + d) % SIDE) * SHARE

    half = SHARE // 2
    early, late = pl.ds(0, half), pl.ds(half, half)

    def fill(block, base, out, first, added=None):
        def body(i, carry):
            for j in range(9):
                at = first + i * 9 + j
                value = block(base + at)
                if added is not None:
                    value = value + added[i * 9 + j].astype(F32)
                out[at] = value.astype(out.dtype)
            return carry

        lax.fori_loop(0, half // 9, body, 0)

    sides = (
        (0, up_block, up_base, y_right, y_left, uf_s, ur_s, ul_s, ua_t, ub_t, ul_v, ur_v, u_acc, up_out),
        (1, dn_block, dn_base, x_right, x_left, df_s, dr_s, dl_s, da_t, db_t, dl_v, dr_v, d_acc, dn_out),
    )
    def make(side, piece):
        _, block, base, _, _, f_s, r_s, l_s, _, _, _, _, acc, _ = side
        d, into, first = ((2, f_s, 0), (2, f_s, half), (1, r_s, half), (3, l_s, 0), (0, acc, 0), (0, acc, half))[piece]
        fill(block, base(d), into, first)

    def ship(side, piece):
        n, _, _, to_right, to_left, f_s, r_s, l_s, a_t, b_t, l_v, r_v, _, _ = side
        src, dst, peer = (
            (f_s.at[early], a_t, to_right),
            (f_s.at[late], b_t, to_left),
            (r_s.at[late], l_v.at[late], to_right),
            (l_s.at[early], r_v.at[early], to_left),
        )[piece]
        send(src, dst, rs_s.at[n, piece], rs_r.at[n, piece], peer)

    def finish(side):
        n, block, base, to_right, to_left, _, r_s, l_s, a_t, b_t, l_v, r_v, _, _ = side
        arrived(a_t, rs_s.at[n, 0], rs_r.at[n, 0], to_left)
        fill(block, base(1), r_s, 0, a_t)
        send(r_s.at[early], l_v.at[early], rs_s.at[n, 4], rs_r.at[n, 4], to_right)
        arrived(b_t, rs_s.at[n, 1], rs_r.at[n, 1], to_right)
        fill(block, base(3), l_s, half, b_t)
        send(l_s.at[late], r_v.at[late], rs_s.at[n, 5], rs_r.at[n, 5], to_left)

    up_side, dn_side = sides
    for piece in range(6):
        make(dn_side, piece)
    pass_far("pg")
    for piece in range(4):
        ship(dn_side, piece)
    tokens_in_place(token_kinds[0])
    for slot in range(2, 10):
        pair_wait("pg", slot)
    for piece in range(4):
        make(up_side, piece)
        ship(up_side, piece)
    finish(dn_side)
    finish(up_side)
    make(up_side, 4)
    make(up_side, 5)

    for d in range(1, SIDE):
        arrived(zin.at[d - 1], z_s.at[d - 1], z_r.at[d - 1], z_peers[d - 1])
    own_rows = pl.ds(pl.multiple_of(col * 32, 32), 32)
    dx_out[...] = (
        dxp[own_rows, :].astype(F32) + zin[0].astype(F32) + zin[1].astype(F32) + zin[2].astype(F32)
    ).astype(BF)
    for n, block, base, to_right, to_left, f_s, r_s, l_s, a_t, b_t, l_v, r_v, acc, out in sides:
        arrived(l_v.at[late], rs_s.at[n, 2], rs_r.at[n, 2], to_left)
        arrived(r_v.at[early], rs_s.at[n, 3], rs_r.at[n, 3], to_right)

        def partial(i, carry, acc=acc, l_v=l_v, r_v=r_v):
            for j in range(3):
                at = 3 * i + j
                acc[at] = acc[at] + r_v[at].astype(F32)
                acc[half + at] = acc[half + at] + l_v[half + at].astype(F32)
            return carry

        lax.fori_loop(0, half // 3, partial, 0)
    for n, block, base, to_right, to_left, f_s, r_s, l_s, a_t, b_t, l_v, r_v, acc, out in sides:
        arrived(l_v.at[early], rs_s.at[n, 4], rs_r.at[n, 4], to_left)
        arrived(r_v.at[late], rs_s.at[n, 5], rs_r.at[n, 5], to_right)

        def final(i, carry, acc=acc, l_v=l_v, r_v=r_v, out=out):
            for j in range(3):
                at = 3 * i + j
                out[at] = (acc[at] + l_v[at].astype(F32)).astype(BF)
                out[half + at] = (acc[half + at] + r_v[half + at].astype(F32)).astype(BF)
            return carry

        lax.fori_loop(0, half // 3, final, 0)
    for copy in started:
        copy.wait_send()


def main(up, dn, owner, x, g, wu, wd):
    vmem = pl.BlockSpec(memory_space=pltpu.VMEM)
    far = pl.BlockSpec(memory_space=pl.ANY)

    def blocks(n, dtype=BF):
        return pltpu.VMEM((n, B, B), dtype)

    tokens = pltpu.VMEM((B, ROWS * B), BF)
    side = [blocks(SHARE)] * 3 + [blocks(SHARE // 2)] * 2 + [blocks(SHARE)] * 2 + [blocks(SHARE, F32)]
    dma = pltpu.SemaphoreType.DMA
    scratch = (
        [blocks(ROWS)] * 3 + [blocks(NBLK + 1), blocks(NBLK + 1), blocks(PAIRS + 1)]
        + [blocks(ROWS)] * 6
        + [blocks(COLS)] * 2
        + [blocks(ROWS)] * 3
        + [blocks(ROWS)] * 3
        + [blocks(COLS)] * 6
        + [tokens, pltpu.VMEM((3, 32, ROWS * B), BF)]
        + side
        + side
        + [dma((4,))] * 2
        + [dma((2, 8))] * 2
        + [dma((2, 10))] * 2
        + [dma((2, 6))] * 2
        + [dma((3,))] * 2
        + [dma((2,)), dma((2, ROWS))]
        + [dma((2, 10))] * 2
        + [dma((2, 3, 3))] * 2
        + [pltpu.VMEM((8, WIDE), jnp.int32), pltpu.SMEM((8, WIDE), jnp.int32), dma(())]
    )
    return pl.pallas_call(
        main_kernel,
        out_shape=[
            jax.ShapeDtypeStruct((32, ROWS * B), BF),
            jax.ShapeDtypeStruct((SHARE, B, B), BF),
            jax.ShapeDtypeStruct((SHARE, B, B), BF),
        ],
        in_specs=[vmem] * 3 + [far] * 4,
        out_specs=[vmem] * 3,
        scratch_shapes=scratch,
        compiler_params=pltpu.CompilerParams(
            collective_id=0, has_side_effects=True, vmem_limit_bytes=62 * 2**20
        ),
        name="backward",
    )(up, dn, owner, x, g, wu, wd)


def results_kernel(*refs):
    count = (len(refs) - 2) // 3
    in_sem, out_sem = refs[-2:]
    ins = [pltpu.make_async_copy(refs[n], refs[2 * count + n], in_sem.at[n]) for n in range(count)]
    outs = [pltpu.make_async_copy(refs[2 * count + n], refs[count + n], out_sem.at[n]) for n in range(count)]
    for copy in ins:
        copy.start()
    for n in range(count):
        ins[n].wait()
        outs[n].start()
    for copy in outs:
        copy.wait()


def results(*values):
    far = pl.BlockSpec(memory_space=pl.ANY)
    return pl.pallas_call(
        results_kernel,
        out_shape=[jax.ShapeDtypeStruct(value.shape, value.dtype) for value in values],
        in_specs=[far] * len(values),
        out_specs=[far] * len(values),
        scratch_shapes=[pltpu.VMEM(value.shape, value.dtype) for value in values]
        + [pltpu.SemaphoreType.DMA((len(values),))] * 2,
        name="results",
    )(*values)


def shards(tokens_in, out_grad, up_weight, down_weight, up_blocks, down_blocks, owners):
    input_grad, up_grad, down_grad = results(
        *main(
            up_blocks[0], down_blocks[0], owners[0], tokens_in, out_grad, up_weight[0, 0], down_weight[0, 0]
        )
    )
    return input_grad, up_grad[None, None], down_grad[None, None]


def solution(mesh):
    placed = (
        P("dp", "row"),
        P("dp", "row"),
        P("row", "col", None, None, None),
        P("row", "col", None, None, None),
        P("row", "col", None),
        P("row", "col", None),
        P("row", "col", None),
    )
    return jax.shard_map(
        shards,
        mesh=mesh,
        in_specs=placed,
        out_specs=(
            P(("dp", "col"), "row"),
            P("row", "col", "dp", None, None),
            P("row", "col", "dp", None, None),
        ),
        check_vma=False,
    )
```

```python
import functools

import jax
import jax.numpy as jnp
from jax import lax
from jax.experimental import pallas as pl
from jax.experimental.pallas import tpu as pltpu
from jax.sharding import PartitionSpec as P

BF = jnp.bfloat16
F32 = jnp.float32
B = 128
ROWS = 24
COLS = 48
NBLK = 288
SIDE = 4
SHARE = 18
CH = 12
PAIRS = 168
WIDE = 384
NN = (((1,), (0,)), ((), ()))
NT = (((1,), (1,)), ((), ()))
MESH = pl.DeviceIdType.MESH

root_two_pi = 0.7978845608028654
cubic_coef = 0.044715


def gelu(pre_sum):
    square = pre_sum * pre_sum
    tanh_inner = jnp.tanh(root_two_pi * (pre_sum + cubic_coef * square * pre_sum))
    half = 0.5 * (1.0 + tanh_inner)
    slope = half + 0.5 * pre_sum * (1.0 - tanh_inner * tanh_inner) * root_two_pi * (
        1.0 + 3.0 * cubic_coef * square
    )
    return pre_sum * half, slope


def dot(left, right, dims):
    return lax.dot_general(left, right, dims, preferred_element_type=F32)


def make_tables(up_ref, dn_ref, own_ref, out_ref):
    def iota(shape, axis):
        return lax.broadcasted_iota(jnp.int32, shape, axis)

    square = (NBLK, NBLK)
    sub, lane = iota(square, 0), iota(square, 1)
    wide = iota((NBLK, WIDE), 1)

    def total(values, axis):
        return jnp.sum(values, axis=axis, keepdims=True)

    def count(mask, axis):
        return total(jnp.where(mask, 1, 0), axis)

    def column(row):
        return total(jnp.where(sub == lane, jnp.broadcast_to(row, square), 0), 1)

    def pairs(e_row, e_col, segment, operand):
        seg_row, seg_col = segment(e_row), segment(e_col)
        same = seg_col == seg_row
        turn = count(same & (lane < sub), 1)
        even = (turn & 1) == 0
        even_row = (count(same & (sub < lane), 0) & 1) == 0
        offset = count((seg_row < seg_col) & even_row, 1)
        place = 2 * (offset + (turn >> 1)) + (turn & 1)
        block = NBLK - iota((NBLK, 1), 0)
        value = block * 64 + operand(e_col) + jnp.where(turn >= 2, 65536, 0)
        table = total(jnp.where(place == wide, value, 0), 0)
        through = count((seg_col <= wide) & even, 0)
        here = count((seg_col == wide) & even, 0)
        return table, jnp.where(here > 0, through - 1, PAIRS)

    up_row, dn_row, owner_row = up_ref[...], dn_ref[...], own_ref[...]
    up_col, dn_col, owner_col = column(up_row), column(dn_row), column(owner_row)

    def owned(value):
        return total(jnp.where(owner_col == wide, value, 0), 0)

    def by_cols(value):
        return (value * 1366) >> 16

    def by_rows(value):
        return (value * 2731) >> 16

    def in_cols(value):
        return value - by_cols(value) * COLS

    def in_rows(value):
        return value - by_rows(value) * ROWS

    t0, l0 = pairs(up_row, up_col, in_cols, by_cols)
    t1, l1 = pairs(dn_row, dn_col, by_rows, in_rows)
    t2, l2 = pairs(up_row, up_col, by_cols, in_cols)
    rows = (
        t0, t1, t2, l0, l1, l2,
        owned(by_cols(up_col) * 64 + in_cols(up_col)),
        owned(in_rows(dn_col) * 64 + by_rows(dn_col)),
    )
    for n, value in enumerate(rows):
        out_ref[n : n + 1, :] = value


def main_kernel(*refs):
    up_ref, dn_ref, own_ref, x_hbm, g_hbm, wu_hbm, wd_hbm = refs[:7]
    dx_out, up_out, dn_out = refs[7:10]
    (
        x_in, og_own, xt_own, wu, wd, runs,
        pre_ref, back_ref, pre_to, back_to, pre_in, back_in, pg_own, ht_own,
        xt_l, xt_r, xt_o, og_l, og_r, og_o,
        pg_l, pg_r, pg_o, ht_l, ht_r, ht_o,
        dxp, zin,
        uf_s, ur_s, ul_s, ua_t, ub_t, ul_v, ur_v, u_acc,
        df_s, dr_s, dl_s, da_t, db_t, dl_v, dr_v, d_acc,
        ex_s, ex_r, ag_s, ag_r, pa_s, pa_r, rs_s, rs_r, z_s, z_r, in_s, col_s, to_s, to_r, sh_s, sh_r,
        made, tab, tab_s,
    ) = refs[10:]
    dp, row, col = lax.axis_index("dp"), lax.axis_index("row"), lax.axis_index("col")
    y, x = dp // SIDE, dp % SIDE
    other = (dp, 1 - row, col)
    x_right = (y * SIDE + (x + 1) % SIDE, row, col)
    x_left = (y * SIDE + (x + 3) % SIDE, row, col)
    y_right = (((y + 1) % SIDE) * SIDE + x, row, col)
    y_left = (((y + 3) % SIDE) * SIDE + x, row, col)
    z_peers = [(dp, row, (col + d) % SIDE) for d in range(1, SIDE)]

    barrier = pltpu.get_barrier_semaphore()
    peers = [other, x_right, x_left, y_right, y_left] + z_peers
    for peer in peers:
        pl.semaphore_signal(barrier, inc=1, device_id=peer, device_id_type=MESH)

    def column_loads(src, dst, n):
        return [
            pltpu.make_async_copy(src.at[:, pl.ds(f * B, B)], dst.at[f], col_s.at[n, f]) for f in range(ROWS)
        ]

    loads = [
        column_loads(g_hbm, og_own, 0),
        column_loads(x_hbm, x_in, 1),
        [pltpu.make_async_copy(wu_hbm, wu.at[pl.ds(0, NBLK)], in_s.at[0])],
        [pltpu.make_async_copy(wd_hbm, wd.at[pl.ds(0, NBLK)], in_s.at[1])],
    ]

    def loaded(n):
        for load in loads[n]:
            load.wait()

    def begin(n):
        for load in loads[n]:
            load.start()

    for n in (1, 2, 0):
        begin(n)
    make_tables(up_ref, dn_ref, own_ref, made)
    tables = pltpu.make_async_copy(made, tab, tab_s)
    tables.start()
    wu[NBLK] = jnp.zeros((B, B), BF)
    wd[NBLK] = jnp.zeros((B, B), BF)
    runs[PAIRS] = jnp.zeros((B, B), BF)

    started = []

    def send(src, dst, send_sem, recv_sem, peer):
        copy = pltpu.make_async_remote_copy(
            src_ref=src, dst_ref=dst, send_sem=send_sem, recv_sem=recv_sem, device_id=peer, device_id_type=MESH
        )
        copy.start()
        started.append(copy)

    def arrived(dst, send_sem, recv_sem, peer):
        pltpu.make_async_remote_copy(
            src_ref=dst, dst_ref=dst, send_sem=send_sem, recv_sem=recv_sem, device_id=peer, device_id_type=MESH
        ).wait_recv()

    kinds = {
        "pg": (0, pg_own, pg_l, pg_r, pg_o, x_right, x_left),
        "ht": (1, ht_own, ht_l, ht_r, ht_o, y_right, y_left),
    }

    token_kinds = (
        (0, xt_own, (xt_l, xt_r, xt_o), x_right, x_left),
        (1, og_own, (og_l, og_r, og_o), y_right, y_left),
    )
    z_right, z_left = (dp, row, (col + 1) % SIDE), (dp, row, (col + 3) % SIDE)
    first, second = pl.ds(0, 4), pl.ds(4, 4)

    def share(step, offset=0, count=4):
        return pl.ds(8 + 4 * ((col + step) % SIDE) + offset, count)

    token_spots = (
        (0, share(0), share(0)), (0, first, first), (0, second, second),
        (1, share(0), share(0)), (1, first, first), (1, second, second),
        (2, share(0, 0, 2), 0), (2, first, 0), (2, share(0, 2, 2), 1), (2, second, 1),
    )

    def token_send(kind, slot):
        n, own, into, to_right, to_left = kind
        buffer, at, source = token_spots[slot]
        src = own if slot < 6 else into[source]
        peer = to_right if slot in (0, 1, 2, 6, 7) else to_left
        send(src.at[at], into[buffer].at[at], to_s.at[n, slot], to_r.at[n, slot], peer)

    def token_wait(kind, slot):
        n, _, into, to_right, _ = kind
        buffer, at, _ = token_spots[slot]
        arrived(into[buffer].at[at], to_s.at[n, slot], to_r.at[n, slot], to_right)

    def share_send(kind, source):
        n, _, into, _, _ = kind
        ref = into[source].at[share(0)]
        send(ref, ref, sh_s.at[n, source, 0], sh_r.at[n, source, 0], z_right)
        send(ref, ref, sh_s.at[n, source, 1], sh_r.at[n, source, 1], z_left)

    def share_wait(kind, source, way):
        n, _, into, _, _ = kind
        ref = into[source].at[share((3, 1, 2)[way])]
        arrived(ref, sh_s.at[n, source, way], sh_r.at[n, source, way], z_right)

    def share_forward(kind, source):
        n, _, into, _, _ = kind
        share_wait(kind, source, n)
        ref = into[source].at[share((3, 1)[n])]
        send(ref, ref, sh_s.at[n, source, 2], sh_r.at[n, source, 2], (z_right, z_left)[n])

    def part(c, whose=row):
        return pl.ds(whose * ROWS + c * CH, CH)

    def ring_out(kind, c, way):
        n, own, left, right, _, to_right, to_left = kinds[kind]
        at = part(c)
        if way == "r":
            send(own.at[at], left.at[at], ag_s.at[n, c], ag_r.at[n, c], to_right)
        else:
            send(own.at[at], right.at[at], ag_s.at[n, 2 + c], ag_r.at[n, 2 + c], to_left)

    def spot(kind, slot, whose=row):
        _, own, left, right, far, _, _ = kinds[kind]
        buffer = (own, own, left, left, right, right, far, far, far, far)[slot]
        if slot < 6:
            return buffer.at[part(slot % 2, whose)]
        return buffer.at[pl.ds(whose * ROWS + (slot - 6) * (CH // 2), CH // 2)]

    def ring_wait(kind, slot):
        n, to_right = kinds[kind][0], kinds[kind][5]
        arrived(spot(kind, slot + 2), ag_s.at[n, slot], ag_r.at[n, slot], to_right)

    def ring_forward(kind, way):
        n, _, left, right, far, to_right, to_left = kinds[kind]
        base = row * ROWS
        source, first, peer = (left, 4, to_right) if way == "r" else (right, 6, to_left)
        for slot in (first, first + 1):
            at = pl.ds(base + (slot - 4) * (CH // 2), CH // 2)
            send(source.at[at], far.at[at], ag_s.at[n, slot], ag_r.at[n, slot], peer)

    def pair_out(kind, slot):
        n = kinds[kind][0]
        ref = spot(kind, slot)
        send(ref, ref, pa_s.at[n, slot], pa_r.at[n, slot], other)

    def pair_wait(kind, slot):
        n = kinds[kind][0]
        ref = spot(kind, slot, 1 - row)
        arrived(ref, pa_s.at[n, slot], pa_r.at[n, slot], other)

    loaded(1)
    for f in range(ROWS):
        xt_own[f] = x_in[f].T

    def products(n, left, weights, axis, start, stop, total=None):
        unroll = 28

        def body(i, total):
            parts = []
            for j in range(unroll):
                p = i * unroll + j
                first, second = tab[n, 2 * p], tab[n, 2 * p + 1]
                lhs = jnp.concatenate([left(first & 63), left(second & 63)], axis=1)
                rhs = jnp.concatenate(
                    [weights[NBLK - ((first >> 6) & 1023)], weights[NBLK - ((second >> 6) & 1023)]], axis=axis
                )
                parts.append(((first >> 16).astype(F32), dot(lhs, rhs, NT if axis else NN)))
            for j in range(unroll):
                total = total * parts[j][0] + parts[j][1]
                runs[i * unroll + j] = total.astype(BF)
            return total

        if total is None:
            total = jnp.zeros((B, B), F32)
        return lax.fori_loop(start, stop, body, total)

    def exchange(n, to, mine, into):
        def pick(i, carry):
            for j in range(6):
                at = i * 6 + j
                to[at] = runs[tab[3 + n, (1 - row) * ROWS + at]]
            return carry

        def own(i, carry):
            for j in range(6):
                at = i * 6 + j
                mine[at] = runs[tab[3 + n, row * ROWS + at]]
            return carry

        for c in range(2):
            lax.fori_loop(2 * c, 2 * c + 2, pick, 0)
            here = pl.ds(c * CH, CH)
            send(to.at[here], into.at[here], ex_s.at[2 * n + c], ex_r.at[2 * n + c], other)
        lax.fori_loop(0, 4, own, 0)

    tables.wait()
    loaded(2)
    begin(3)
    loaded(0)
    pl.semaphore_wait(barrier, len(peers))
    for slots in ((0, 3), (1, 5), (2, 4)):
        for kind in token_kinds:
            for slot in slots:
                token_send(kind, slot)
    carried = products(0, lambda f: x_in[f], wu, 0, 0, 3)
    products(0, lambda f: x_in[f], wu, 0, 3, 6, carried)
    exchange(0, pre_to, pre_ref, pre_in)
    for kind in token_kinds:
        for slot, source, forward in ((0, 0, 6), (3, 1, 8)):
            token_wait(kind, slot)
            share_send(kind, source)
            token_send(kind, forward)
    loaded(3)
    carried = products(1, lambda f: og_own[f], wd, 1, 0, 3)
    for kind in token_kinds:
        for slot, forward in ((1, 7), (5, 9)):
            token_wait(kind, slot)
            token_send(kind, forward)

    for c in range(2):
        here = pl.ds(c * CH, CH)
        arrived(pre_in.at[here], ex_s.at[c], ex_r.at[c], other)

        def hidden_one(i, carry, c=c):
            pre = pre_ref[c * CH + i].astype(F32) + pre_in[c * CH + i].astype(F32)
            ht_own[row * ROWS + c * CH + i] = gelu(pre)[0].astype(BF).T
            return carry

        lax.fori_loop(0, CH, hidden_one, 0)
        ring_out("ht", c, "rl"[c])
        pair_out("ht", c)
    ring_out("ht", 1, "r")
    ring_out("ht", 0, "l")
    products(1, lambda f: og_own[f], wd, 1, 3, 6, carried)
    exchange(1, back_to, back_ref, back_in)
    for kind in token_kinds:
        token_wait(kind, 6)
        token_wait(kind, 8)
        share_send(kind, 2)

    for c in range(2):
        here = pl.ds(c * CH, CH)
        arrived(back_in.at[here], ex_s.at[2 + c], ex_r.at[2 + c], other)

        def grad_one(i, carry, c=c):
            pre = pre_ref[c * CH + i].astype(F32) + pre_in[c * CH + i].astype(F32)
            back = back_ref[c * CH + i].astype(F32) + back_in[c * CH + i].astype(F32)
            pg_own[row * ROWS + c * CH + i] = (back * gelu(pre)[1]).astype(BF)
            return carry

        lax.fori_loop(0, CH, grad_one, 0)
        ring_out("pg", c, "rl"[c])
        pair_out("pg", c)
    ring_out("pg", 1, "r")
    ring_out("pg", 0, "l")

    def pass_on(kind):
        ring_wait(kind, 0)
        ring_forward(kind, "r")
        pair_out(kind, 2)
        ring_wait(kind, 3)
        ring_forward(kind, "l")
        pair_out(kind, 5)

    def pass_rest(kind):
        ring_wait(kind, 1)
        pair_out(kind, 3)
        ring_wait(kind, 2)
        pair_out(kind, 4)

    def pass_far(kind):
        for slot in (4, 6, 5, 7):
            ring_wait(kind, slot)
            pair_out(kind, slot + 2)

    def tokens_in_place(kind):
        for slot in (2, 4, 7, 9):
            token_wait(kind, slot)
        for source in range(3):
            share_wait(kind, source, 1 - kind[0])
            share_wait(kind, source, 2)

    pass_on("ht")

    pair_wait("pg", 0)
    pair_wait("pg", 1)
    products(2, lambda h: pg_own[h], wu, 1, 0, 6)
    for f in range(ROWS):
        dxp[:, f * B : (f + 1) * B] = runs[tab[5, f]]
    for kind in token_kinds:
        share_forward(kind, 0)
        share_forward(kind, 1)
    pass_rest("ht")
    pass_on("pg")
    for kind in token_kinds:
        share_forward(kind, 2)
    for d in range(1, SIDE):
        theirs = pl.ds(pl.multiple_of(((col + d) % SIDE) * 32, 32), 32)
        send(dxp.at[theirs], zin.at[d - 1], z_s.at[d - 1], z_r.at[d - 1], z_peers[d - 1])
    pass_far("ht")
    pass_rest("pg")
    for slot in range(10):
        pair_wait("ht", slot)
    tokens_in_place(token_kinds[1])

    def up_block(s):
        e = tab[6, s]
        f, h = e >> 6, e & 63
        left = jnp.concatenate([xt_own[f], xt_l[f], xt_r[f], xt_o[f]], axis=1)
        right = jnp.concatenate([pg_own[h], pg_l[h], pg_r[h], pg_o[h]], axis=0)
        return dot(left, right, NN)

    def dn_block(s):
        e = tab[7, s]
        f, h = e >> 6, e & 63
        left = jnp.concatenate([ht_own[h], ht_l[h], ht_r[h], ht_o[h]], axis=1)
        right = jnp.concatenate([og_own[f], og_l[f], og_r[f], og_o[f]], axis=0)
        return dot(left, right, NN)

    def up_base(d):
        return ((y + d) % SIDE) * (SIDE * SHARE) + x * SHARE

    def dn_base(d):
        return y * (SIDE * SHARE) + ((x + d) % SIDE) * SHARE

    half = SHARE // 2
    early, late = pl.ds(0, half), pl.ds(half, half)

    def fill(block, base, out, first, added=None):
        def body(i, carry):
            for j in range(9):
                at = first + i * 9 + j
                value = block(base + at)
                if added is not None:
                    value = value + added[i * 9 + j].astype(F32)
                out[at] = value.astype(out.dtype)
            return carry

        lax.fori_loop(0, half // 9, body, 0)

    sides = (
        (0, up_block, up_base, y_right, y_left, uf_s, ur_s, ul_s, ua_t, ub_t, ul_v, ur_v, u_acc, up_out),
        (1, dn_block, dn_base, x_right, x_left, df_s, dr_s, dl_s, da_t, db_t, dl_v, dr_v, d_acc, dn_out),
    )
    def make(side, piece):
        _, block, base, _, _, f_s, r_s, l_s, _, _, _, _, acc, _ = side
        d, into, first = ((2, f_s, 0), (2, f_s, half), (1, r_s, half), (3, l_s, 0), (0, acc, 0), (0, acc, half))[piece]
        fill(block, base(d), into, first)

    def ship(side, piece):
        n, _, _, to_right, to_left, f_s, r_s, l_s, a_t, b_t, l_v, r_v, _, _ = side
        src, dst, peer = (
            (f_s.at[early], a_t, to_right),
            (f_s.at[late], b_t, to_left),
            (r_s.at[late], l_v.at[late], to_right),
            (l_s.at[early], r_v.at[early], to_left),
        )[piece]
        send(src, dst, rs_s.at[n, piece], rs_r.at[n, piece], peer)

    def finish(side):
        n, block, base, to_right, to_left, _, r_s, l_s, a_t, b_t, l_v, r_v, _, _ = side
        arrived(a_t, rs_s.at[n, 0], rs_r.at[n, 0], to_left)
        fill(block, base(1), r_s, 0, a_t)
        send(r_s.at[early], l_v.at[early], rs_s.at[n, 4], rs_r.at[n, 4], to_right)
        arrived(b_t, rs_s.at[n, 1], rs_r.at[n, 1], to_right)
        fill(block, base(3), l_s, half, b_t)
        send(l_s.at[late], r_v.at[late], rs_s.at[n, 5], rs_r.at[n, 5], to_left)

    up_side, dn_side = sides
    for piece in range(6):
        make(dn_side, piece)
    pass_far("pg")
    for piece in range(4):
        ship(dn_side, piece)
    tokens_in_place(token_kinds[0])
    for slot in range(2, 10):
        pair_wait("pg", slot)
    for piece in range(4):
        make(up_side, piece)
        ship(up_side, piece)
    finish(dn_side)
    finish(up_side)
    make(up_side, 4)
    make(up_side, 5)

    for d in range(1, SIDE):
        arrived(zin.at[d - 1], z_s.at[d - 1], z_r.at[d - 1], z_peers[d - 1])
    own_rows = pl.ds(pl.multiple_of(col * 32, 32), 32)
    dx_out[...] = (
        dxp[own_rows, :].astype(F32) + zin[0].astype(F32) + zin[1].astype(F32) + zin[2].astype(F32)
    ).astype(BF)
    for n, block, base, to_right, to_left, f_s, r_s, l_s, a_t, b_t, l_v, r_v, acc, out in sides:
        arrived(l_v.at[late], rs_s.at[n, 2], rs_r.at[n, 2], to_left)
        arrived(r_v.at[early], rs_s.at[n, 3], rs_r.at[n, 3], to_right)

        def partial(i, carry, acc=acc, l_v=l_v, r_v=r_v):
            for j in range(3):
                at = 3 * i + j
                acc[at] = acc[at] + r_v[at].astype(F32)
                acc[half + at] = acc[half + at] + l_v[half + at].astype(F32)
            return carry

        lax.fori_loop(0, half // 3, partial, 0)
    for n, block, base, to_right, to_left, f_s, r_s, l_s, a_t, b_t, l_v, r_v, acc, out in sides:
        arrived(l_v.at[early], rs_s.at[n, 4], rs_r.at[n, 4], to_left)
        arrived(r_v.at[late], rs_s.at[n, 5], rs_r.at[n, 5], to_right)

        def final(i, carry, acc=acc, l_v=l_v, r_v=r_v, out=out):
            for j in range(3):
                at = 3 * i + j
                out[at] = (acc[at] + l_v[at].astype(F32)).astype(BF)
                out[half + at] = (acc[half + at] + r_v[half + at].astype(F32)).astype(BF)
            return carry

        lax.fori_loop(0, half // 3, final, 0)
    for copy in started:
        copy.wait_send()


def main(up, dn, owner, x, g, wu, wd):
    vmem = pl.BlockSpec(memory_space=pltpu.VMEM)
    far = pl.BlockSpec(memory_space=pl.ANY)

    def blocks(n, dtype=BF):
        return pltpu.VMEM((n, B, B), dtype)

    tokens = pltpu.VMEM((B, ROWS * B), BF)
    side = [blocks(SHARE)] * 3 + [blocks(SHARE // 2)] * 2 + [blocks(SHARE)] * 2 + [blocks(SHARE, F32)]
    dma = pltpu.SemaphoreType.DMA
    scratch = (
        [blocks(ROWS)] * 3 + [blocks(NBLK + 1), blocks(NBLK + 1), blocks(PAIRS + 1)]
        + [blocks(ROWS)] * 6
        + [blocks(COLS)] * 2
        + [blocks(ROWS)] * 3
        + [blocks(ROWS)] * 3
        + [blocks(COLS)] * 6
        + [tokens, pltpu.VMEM((3, 32, ROWS * B), BF)]
        + side
        + side
        + [dma((4,))] * 2
        + [dma((2, 8))] * 2
        + [dma((2, 10))] * 2
        + [dma((2, 6))] * 2
        + [dma((3,))] * 2
        + [dma((2,)), dma((2, ROWS))]
        + [dma((2, 10))] * 2
        + [dma((2, 3, 3))] * 2
        + [pltpu.VMEM((8, WIDE), jnp.int32), pltpu.SMEM((8, WIDE), jnp.int32), dma(())]
    )
    return pl.pallas_call(
        main_kernel,
        out_shape=[
            jax.ShapeDtypeStruct((32, ROWS * B), BF),
            jax.ShapeDtypeStruct((SHARE, B, B), BF),
            jax.ShapeDtypeStruct((SHARE, B, B), BF),
        ],
        in_specs=[vmem] * 3 + [far] * 4,
        out_specs=[vmem] * 3,
        scratch_shapes=scratch,
        compiler_params=pltpu.CompilerParams(
            collective_id=0, has_side_effects=True, vmem_limit_bytes=62 * 2**20
        ),
        name="backward",
    )(up, dn, owner, x, g, wu, wd)


def results_kernel(*refs):
    count = (len(refs) - 2) // 3
    in_sem, out_sem = refs[-2:]
    ins = [pltpu.make_async_copy(refs[n], refs[2 * count + n], in_sem.at[n]) for n in range(count)]
    outs = [pltpu.make_async_copy(refs[2 * count + n], refs[count + n], out_sem.at[n]) for n in range(count)]
    for copy in ins:
        copy.start()
    for n in range(count):
        ins[n].wait()
        outs[n].start()
    for copy in outs:
        copy.wait()


def results(*values):
    far = pl.BlockSpec(memory_space=pl.ANY)
    return pl.pallas_call(
        results_kernel,
        out_shape=[jax.ShapeDtypeStruct(value.shape, value.dtype) for value in values],
        in_specs=[far] * len(values),
        out_specs=[far] * len(values),
        scratch_shapes=[pltpu.VMEM(value.shape, value.dtype) for value in values]
        + [pltpu.SemaphoreType.DMA((len(values),))] * 2,
        name="results",
    )(*values)


def shards(tokens_in, out_grad, up_weight, down_weight, up_blocks, down_blocks, owners):
    input_grad, up_grad, down_grad = results(
        *main(
            up_blocks[0], down_blocks[0], owners[0], tokens_in, out_grad, up_weight[0, 0], down_weight[0, 0]
        )
    )
    return input_grad, up_grad[None, None], down_grad[None, None]


def solution(mesh):
    placed = (
        P("dp", "row"),
        P("dp", "row"),
        P("row", "col", None, None, None),
        P("row", "col", None, None, None),
        P("row", "col", None),
        P("row", "col", None),
        P("row", "col", None),
    )
    return jax.shard_map(
        shards,
        mesh=mesh,
        in_specs=placed,
        out_specs=(
            P(("dp", "col"), "row"),
            P("row", "col", "dp", None, None),
            P("row", "col", "dp", None, None),
        ),
        check_vma=False,
    )
```

```python
import functools

import jax
import jax.numpy as jnp
from jax import lax
from jax.experimental import pallas as pl
from jax.experimental.pallas import tpu as pltpu
from jax.sharding import PartitionSpec as P

BF = jnp.bfloat16
F32 = jnp.float32
B = 128
ROWS = 24
COLS = 48
NBLK = 288
SIDE = 4
SHARE = 18
CH = 12
PAIRS = 168
WIDE = 384
NN = (((1,), (0,)), ((), ()))
NT = (((1,), (1,)), ((), ()))
MESH = pl.DeviceIdType.MESH

root_two_pi = 0.7978845608028654
cubic_coef = 0.044715


def gelu(pre_sum):
    square = pre_sum * pre_sum
    tanh_inner = jnp.tanh(root_two_pi * (pre_sum + cubic_coef * square * pre_sum))
    half = 0.5 * (1.0 + tanh_inner)
    slope = half + 0.5 * pre_sum * (1.0 - tanh_inner * tanh_inner) * root_two_pi * (
        1.0 + 3.0 * cubic_coef * square
    )
    return pre_sum * half, slope


def dot(left, right, dims):
    return lax.dot_general(left, right, dims, preferred_element_type=F32)


def make_tables(up_ref, dn_ref, own_ref, out_ref):
    def iota(shape, axis):
        return lax.broadcasted_iota(jnp.int32, shape, axis)

    square = (NBLK, NBLK)
    sub, lane = iota(square, 0), iota(square, 1)
    wide = iota((NBLK, WIDE), 1)

    def total(values, axis):
        return jnp.sum(values, axis=axis, keepdims=True)

    def count(mask, axis):
        return total(jnp.where(mask, 1, 0), axis)

    def column(row):
        return total(jnp.where(sub == lane, jnp.broadcast_to(row, square), 0), 1)

    def pairs(e_row, e_col, segment, operand):
        seg_row, seg_col = segment(e_row), segment(e_col)
        same = seg_col == seg_row
        turn = count(same & (lane < sub), 1)
        even = (turn & 1) == 0
        even_row = (count(same & (sub < lane), 0) & 1) == 0
        offset = count((seg_row < seg_col) & even_row, 1)
        place = 2 * (offset + (turn >> 1)) + (turn & 1)
        block = NBLK - iota((NBLK, 1), 0)
        value = block * 64 + operand(e_col) + jnp.where(turn >= 2, 65536, 0)
        table = total(jnp.where(place == wide, value, 0), 0)
        through = count((seg_col <= wide) & even, 0)
        here = count((seg_col == wide) & even, 0)
        return table, jnp.where(here > 0, through - 1, PAIRS)

    up_row, dn_row, owner_row = up_ref[...], dn_ref[...], own_ref[...]
    up_col, dn_col, owner_col = column(up_row), column(dn_row), column(owner_row)

    def owned(value):
        return total(jnp.where(owner_col == wide, value, 0), 0)

    def by_cols(value):
        return (value * 1366) >> 16

    def by_rows(value):
        return (value * 2731) >> 16

    def in_cols(value):
        return value - by_cols(value) * COLS

    def in_rows(value):
        return value - by_rows(value) * ROWS

    t0, l0 = pairs(up_row, up_col, in_cols, by_cols)
    t1, l1 = pairs(dn_row, dn_col, by_rows, in_rows)
    t2, l2 = pairs(up_row, up_col, by_cols, in_cols)
    rows = (
        t0, t1, t2, l0, l1, l2,
        owned(by_cols(up_col) * 64 + in_cols(up_col)),
        owned(in_rows(dn_col) * 64 + by_rows(dn_col)),
    )
    for n, value in enumerate(rows):
        out_ref[n : n + 1, :] = value


def main_kernel(*refs):
    up_ref, dn_ref, own_ref, x_hbm, g_hbm, wu_hbm, wd_hbm = refs[:7]
    dx_out, up_out, dn_out = refs[7:10]
    (
        x_in, og_own, xt_own, wu, wd, runs,
        pre_ref, back_ref, pre_to, back_to, pre_in, back_in, pg_own, ht_own,
        xt_l, xt_r, xt_o, og_l, og_r, og_o,
        pg_l, pg_r, pg_o, ht_l, ht_r, ht_o,
        dxp, zin,
        uf_s, ur_s, ul_s, ua_t, ub_t, ul_v, ur_v, u_acc,
        df_s, dr_s, dl_s, da_t, db_t, dl_v, dr_v, d_acc,
        ex_s, ex_r, ag_s, ag_r, pa_s, pa_r, rs_s, rs_r, z_s, z_r, in_s, col_s, to_s, to_r, sh_s, sh_r,
        made, tab, tab_s,
    ) = refs[10:]
    dp, row, col = lax.axis_index("dp"), lax.axis_index("row"), lax.axis_index("col")
    y, x = dp // SIDE, dp % SIDE
    other = (dp, 1 - row, col)
    x_right = (y * SIDE + (x + 1) % SIDE, row, col)
    x_left = (y * SIDE + (x + 3) % SIDE, row, col)
    y_right = (((y + 1) % SIDE) * SIDE + x, row, col)
    y_left = (((y + 3) % SIDE) * SIDE + x, row, col)
    z_peers = [(dp, row, (col + d) % SIDE) for d in range(1, SIDE)]

    barrier = pltpu.get_barrier_semaphore()
    peers = [other, x_right, x_left, y_right, y_left] + z_peers
    for peer in peers:
        pl.semaphore_signal(barrier, inc=1, device_id=peer, device_id_type=MESH)

    def column_loads(src, dst, n):
        return [
            pltpu.make_async_copy(src.at[:, pl.ds(f * B, B)], dst.at[f], col_s.at[n, f]) for f in range(ROWS)
        ]

    loads = [
        column_loads(g_hbm, og_own, 0),
        column_loads(x_hbm, x_in, 1),
        [pltpu.make_async_copy(wu_hbm, wu.at[pl.ds(0, NBLK)], in_s.at[0])],
        [pltpu.make_async_copy(wd_hbm, wd.at[pl.ds(0, NBLK)], in_s.at[1])],
    ]

    def loaded(n):
        for load in loads[n]:
            load.wait()

    def begin(n):
        for load in loads[n]:
            load.start()

    for n in (1, 2, 0):
        begin(n)
    make_tables(up_ref, dn_ref, own_ref, made)
    tables = pltpu.make_async_copy(made, tab, tab_s)
    tables.start()
    wu[NBLK] = jnp.zeros((B, B), BF)
    wd[NBLK] = jnp.zeros((B, B), BF)
    runs[PAIRS] = jnp.zeros((B, B), BF)

    started = []

    def send(src, dst, send_sem, recv_sem, peer):
        copy = pltpu.make_async_remote_copy(
            src_ref=src, dst_ref=dst, send_sem=send_sem, recv_sem=recv_sem, device_id=peer, device_id_type=MESH
        )
        copy.start()
        started.append(copy)

    def arrived(dst, send_sem, recv_sem, peer):
        pltpu.make_async_remote_copy(
            src_ref=dst, dst_ref=dst, send_sem=send_sem, recv_sem=recv_sem, device_id=peer, device_id_type=MESH
        ).wait_recv()

    kinds = {
        "pg": (0, pg_own, pg_l, pg_r, pg_o, x_right, x_left),
        "ht": (1, ht_own, ht_l, ht_r, ht_o, y_right, y_left),
    }

    token_kinds = (
        (0, xt_own, (xt_l, xt_r, xt_o), x_right, x_left),
        (1, og_own, (og_l, og_r, og_o), y_right, y_left),
    )
    z_right, z_left = (dp, row, (col + 1) % SIDE), (dp, row, (col + 3) % SIDE)
    first, second = pl.ds(0, 4), pl.ds(4, 4)

    def share(step, offset=0, count=4):
        return pl.ds(8 + 4 * ((col + step) % SIDE) + offset, count)

    token_spots = (
        (0, share(0), share(0)), (0, first, first), (0, second, second),
        (1, share(0), share(0)), (1, first, first), (1, second, second),
        (2, share(0, 0, 2), 0), (2, first, 0), (2, share(0, 2, 2), 1), (2, second, 1),
    )

    def token_send(kind, slot):
        n, own, into, to_right, to_left = kind
        buffer, at, source = token_spots[slot]
        src = own if slot < 6 else into[source]
        peer = to_right if slot in (0, 1, 2, 6, 7) else to_left
        send(src.at[at], into[buffer].at[at], to_s.at[n, slot], to_r.at[n, slot], peer)

    def token_wait(kind, slot):
        n, _, into, to_right, _ = kind
        buffer, at, _ = token_spots[slot]
        arrived(into[buffer].at[at], to_s.at[n, slot], to_r.at[n, slot], to_right)

    def share_send(kind, source):
        n, _, into, _, _ = kind
        ref = into[source].at[share(0)]
        send(ref, ref, sh_s.at[n, source, 0], sh_r.at[n, source, 0], z_right)
        send(ref, ref, sh_s.at[n, source, 1], sh_r.at[n, source, 1], z_left)

    def share_wait(kind, source, way):
        n, _, into, _, _ = kind
        ref = into[source].at[share((3, 1, 2)[way])]
        arrived(ref, sh_s.at[n, source, way], sh_r.at[n, source, way], z_right)

    def share_forward(kind, source):
        n, _, into, _, _ = kind
        share_wait(kind, source, n)
        ref = into[source].at[share((3, 1)[n])]
        send(ref, ref, sh_s.at[n, source, 2], sh_r.at[n, source, 2], (z_right, z_left)[n])

    def part(c, whose=row):
        return pl.ds(whose * ROWS + c * CH, CH)

    def ring_out(kind, c, way):
        n, own, left, right, _, to_right, to_left = kinds[kind]
        at = part(c)
        if way == "r":
            send(own.at[at], left.at[at], ag_s.at[n, c], ag_r.at[n, c], to_right)
        else:
            send(own.at[at], right.at[at], ag_s.at[n, 2 + c], ag_r.at[n, 2 + c], to_left)

    def spot(kind, slot, whose=row):
        _, own, left, right, far, _, _ = kinds[kind]
        buffer = (own, own, left, left, right, right, far, far, far, far)[slot]
        if slot < 6:
            return buffer.at[part(slot % 2, whose)]
        return buffer.at[pl.ds(whose * ROWS + (slot - 6) * (CH // 2), CH // 2)]

    def ring_wait(kind, slot):
        n, to_right = kinds[kind][0], kinds[kind][5]
        arrived(spot(kind, slot + 2), ag_s.at[n, slot], ag_r.at[n, slot], to_right)

    def ring_forward(kind, way):
        n, _, left, right, far, to_right, to_left = kinds[kind]
        base = row * ROWS
        source, first, peer = (left, 4, to_right) if way == "r" else (right, 6, to_left)
        for slot in (first, first + 1):
            at = pl.ds(base + (slot - 4) * (CH // 2), CH // 2)
            send(source.at[at], far.at[at], ag_s.at[n, slot], ag_r.at[n, slot], peer)

    def pair_out(kind, slot):
        n = kinds[kind][0]
        ref = spot(kind, slot)
        send(ref, ref, pa_s.at[n, slot], pa_r.at[n, slot], other)

    def pair_wait(kind, slot):
        n = kinds[kind][0]
        ref = spot(kind, slot, 1 - row)
        arrived(ref, pa_s.at[n, slot], pa_r.at[n, slot], other)

    loaded(1)
    for f in range(ROWS):
        xt_own[f] = x_in[f].T
    loaded(0)
    pl.semaphore_wait(barrier, len(peers))
    for slots in ((0, 3), (1, 5), (2, 4)):
        for kind in token_kinds:
            for slot in slots:
                token_send(kind, slot)

    def products(n, left, weights, axis, start, stop, total=None):
        unroll = 28

        def body(i, total):
            parts = []
            for j in range(unroll):
                p = i * unroll + j
                first, second = tab[n, 2 * p], tab[n, 2 * p + 1]
                lhs = jnp.concatenate([left(first & 63), left(second & 63)], axis=1)
                rhs = jnp.concatenate(
                    [weights[NBLK - ((first >> 6) & 1023)], weights[NBLK - ((second >> 6) & 1023)]], axis=axis
                )
                parts.append(((first >> 16).astype(F32), dot(lhs, rhs, NT if axis else NN)))
            for j in range(unroll):
                total = total * parts[j][0] + parts[j][1]
                runs[i * unroll + j] = total.astype(BF)
            return total

        if total is None:
            total = jnp.zeros((B, B), F32)
        return lax.fori_loop(start, stop, body, total)

    def exchange(n, to, mine, into):
        def pick(i, carry):
            for j in range(6):
                at = i * 6 + j
                to[at] = runs[tab[3 + n, (1 - row) * ROWS + at]]
            return carry

        def own(i, carry):
            for j in range(6):
                at = i * 6 + j
                mine[at] = runs[tab[3 + n, row * ROWS + at]]
            return carry

        for c in range(2):
            lax.fori_loop(2 * c, 2 * c + 2, pick, 0)
            here = pl.ds(c * CH, CH)
            send(to.at[here], into.at[here], ex_s.at[2 * n + c], ex_r.at[2 * n + c], other)
        lax.fori_loop(0, 4, own, 0)

    tables.wait()
    loaded(2)
    begin(3)
    carried = products(0, lambda f: x_in[f], wu, 0, 0, 3)
    products(0, lambda f: x_in[f], wu, 0, 3, 6, carried)
    exchange(0, pre_to, pre_ref, pre_in)
    for kind in token_kinds:
        for slot, source, forward in ((0, 0, 6), (3, 1, 8)):
            token_wait(kind, slot)
            share_send(kind, source)
            token_send(kind, forward)
    loaded(3)
    carried = products(1, lambda f: og_own[f], wd, 1, 0, 3)
    for kind in token_kinds:
        for slot, forward in ((1, 7), (5, 9)):
            token_wait(kind, slot)
            token_send(kind, forward)

    for c in range(2):
        here = pl.ds(c * CH, CH)
        arrived(pre_in.at[here], ex_s.at[c], ex_r.at[c], other)

        def hidden_one(i, carry, c=c):
            pre = pre_ref[c * CH + i].astype(F32) + pre_in[c * CH + i].astype(F32)
            ht_own[row * ROWS + c * CH + i] = gelu(pre)[0].astype(BF).T
            return carry

        lax.fori_loop(0, CH, hidden_one, 0)
        ring_out("ht", c, "rl"[c])
        pair_out("ht", c)
    ring_out("ht", 1, "r")
    ring_out("ht", 0, "l")
    products(1, lambda f: og_own[f], wd, 1, 3, 6, carried)
    exchange(1, back_to, back_ref, back_in)
    for kind in token_kinds:
        token_wait(kind, 6)
        token_wait(kind, 8)
        share_send(kind, 2)

    for c in range(2):
        here = pl.ds(c * CH, CH)
        arrived(back_in.at[here], ex_s.at[2 + c], ex_r.at[2 + c], other)

        def grad_one(i, carry, c=c):
            pre = pre_ref[c * CH + i].astype(F32) + pre_in[c * CH + i].astype(F32)
            back = back_ref[c * CH + i].astype(F32) + back_in[c * CH + i].astype(F32)
            pg_own[row * ROWS + c * CH + i] = (back * gelu(pre)[1]).astype(BF)
            return carry

        lax.fori_loop(0, CH, grad_one, 0)
        ring_out("pg", c, "rl"[c])
        pair_out("pg", c)
    ring_out("pg", 1, "r")
    ring_out("pg", 0, "l")

    def pass_on(kind):
        ring_wait(kind, 0)
        ring_forward(kind, "r")
        pair_out(kind, 2)
        ring_wait(kind, 3)
        ring_forward(kind, "l")
        pair_out(kind, 5)

    def pass_rest(kind):
        ring_wait(kind, 1)
        pair_out(kind, 3)
        ring_wait(kind, 2)
        pair_out(kind, 4)

    def pass_far(kind):
        for slot in (4, 6, 5, 7):
            ring_wait(kind, slot)
            pair_out(kind, slot + 2)

    def tokens_in_place(kind):
        for slot in (2, 4, 7, 9):
            token_wait(kind, slot)
        for source in range(3):
            share_wait(kind, source, 1 - kind[0])
            share_wait(kind, source, 2)

    pass_on("ht")

    pair_wait("pg", 0)
    pair_wait("pg", 1)
    products(2, lambda h: pg_own[h], wu, 1, 0, 6)
    for f in range(ROWS):
        dxp[:, f * B : (f + 1) * B] = runs[tab[5, f]]
    for kind in token_kinds:
        share_forward(kind, 0)
        share_forward(kind, 1)
    pass_rest("ht")
    pass_on("pg")
    for kind in token_kinds:
        share_forward(kind, 2)
    for d in range(1, SIDE):
        theirs = pl.ds(pl.multiple_of(((col + d) % SIDE) * 32, 32), 32)
        send(dxp.at[theirs], zin.at[d - 1], z_s.at[d - 1], z_r.at[d - 1], z_peers[d - 1])
    pass_far("ht")
    pass_rest("pg")
    for slot in range(10):
        pair_wait("ht", slot)
    tokens_in_place(token_kinds[1])

    def up_block(s):
        e = tab[6, s]
        f, h = e >> 6, e & 63
        left = jnp.concatenate([xt_own[f], xt_l[f], xt_r[f], xt_o[f]], axis=1)
        right = jnp.concatenate([pg_own[h], pg_l[h], pg_r[h], pg_o[h]], axis=0)
        return dot(left, right, NN)

    def dn_block(s):
        e = tab[7, s]
        f, h = e >> 6, e & 63
        left = jnp.concatenate([ht_own[h], ht_l[h], ht_r[h], ht_o[h]], axis=1)
        right = jnp.concatenate([og_own[f], og_l[f], og_r[f], og_o[f]], axis=0)
        return dot(left, right, NN)

    def up_base(d):
        return ((y + d) % SIDE) * (SIDE * SHARE) + x * SHARE

    def dn_base(d):
        return y * (SIDE * SHARE) + ((x + d) % SIDE) * SHARE

    half = SHARE // 2
    early, late = pl.ds(0, half), pl.ds(half, half)

    def fill(block, base, out, first, added=None):
        def body(i, carry):
            for j in range(9):
                at = first + i * 9 + j
                value = block(base + at)
                if added is not None:
                    value = value + added[i * 9 + j].astype(F32)
                out[at] = value.astype(out.dtype)
            return carry

        lax.fori_loop(0, half // 9, body, 0)

    sides = (
        (0, up_block, up_base, y_right, y_left, uf_s, ur_s, ul_s, ua_t, ub_t, ul_v, ur_v, u_acc, up_out),
        (1, dn_block, dn_base, x_right, x_left, df_s, dr_s, dl_s, da_t, db_t, dl_v, dr_v, d_acc, dn_out),
    )
    def make(side, piece):
        _, block, base, _, _, f_s, r_s, l_s, _, _, _, _, acc, _ = side
        d, into, first = ((2, f_s, 0), (2, f_s, half), (1, r_s, half), (3, l_s, 0), (0, acc, 0), (0, acc, half))[piece]
        fill(block, base(d), into, first)

    def ship(side, piece):
        n, _, _, to_right, to_left, f_s, r_s, l_s, a_t, b_t, l_v, r_v, _, _ = side
        src, dst, peer = (
            (f_s.at[early], a_t, to_right),
            (f_s.at[late], b_t, to_left),
            (r_s.at[late], l_v.at[late], to_right),
            (l_s.at[early], r_v.at[early], to_left),
        )[piece]
        send(src, dst, rs_s.at[n, piece], rs_r.at[n, piece], peer)

    def finish(side):
        n, block, base, to_right, to_left, _, r_s, l_s, a_t, b_t, l_v, r_v, _, _ = side
        arrived(a_t, rs_s.at[n, 0], rs_r.at[n, 0], to_left)
        fill(block, base(1), r_s, 0, a_t)
        send(r_s.at[early], l_v.at[early], rs_s.at[n, 4], rs_r.at[n, 4], to_right)
        arrived(b_t, rs_s.at[n, 1], rs_r.at[n, 1], to_right)
        fill(block, base(3), l_s, half, b_t)
        send(l_s.at[late], r_v.at[late], rs_s.at[n, 5], rs_r.at[n, 5], to_left)

    up_side, dn_side = sides
    for piece in range(6):
        make(dn_side, piece)
    pass_far("pg")
    for piece in range(4):
        ship(dn_side, piece)
    tokens_in_place(token_kinds[0])
    for slot in range(2, 10):
        pair_wait("pg", slot)
    for piece in range(4):
        make(up_side, piece)
        ship(up_side, piece)
    finish(dn_side)
    finish(up_side)
    make(up_side, 4)
    make(up_side, 5)

    for d in range(1, SIDE):
        arrived(zin.at[d - 1], z_s.at[d - 1], z_r.at[d - 1], z_peers[d - 1])
    own_rows = pl.ds(pl.multiple_of(col * 32, 32), 32)
    dx_out[...] = (
        dxp[own_rows, :].astype(F32) + zin[0].astype(F32) + zin[1].astype(F32) + zin[2].astype(F32)
    ).astype(BF)
    for n, block, base, to_right, to_left, f_s, r_s, l_s, a_t, b_t, l_v, r_v, acc, out in sides:
        arrived(l_v.at[late], rs_s.at[n, 2], rs_r.at[n, 2], to_left)
        arrived(r_v.at[early], rs_s.at[n, 3], rs_r.at[n, 3], to_right)

        def partial(i, carry, acc=acc, l_v=l_v, r_v=r_v):
            for j in range(3):
                at = 3 * i + j
                acc[at] = acc[at] + r_v[at].astype(F32)
                acc[half + at] = acc[half + at] + l_v[half + at].astype(F32)
            return carry

        lax.fori_loop(0, half // 3, partial, 0)
    for n, block, base, to_right, to_left, f_s, r_s, l_s, a_t, b_t, l_v, r_v, acc, out in sides:
        arrived(l_v.at[early], rs_s.at[n, 4], rs_r.at[n, 4], to_left)
        arrived(r_v.at[late], rs_s.at[n, 5], rs_r.at[n, 5], to_right)

        def final(i, carry, acc=acc, l_v=l_v, r_v=r_v, out=out):
            for j in range(3):
                at = 3 * i + j
                out[at] = (acc[at] + l_v[at].astype(F32)).astype(BF)
                out[half + at] = (acc[half + at] + r_v[half + at].astype(F32)).astype(BF)
            return carry

        lax.fori_loop(0, half // 3, final, 0)
    for copy in started:
        copy.wait_send()


def main(up, dn, owner, x, g, wu, wd):
    vmem = pl.BlockSpec(memory_space=pltpu.VMEM)
    far = pl.BlockSpec(memory_space=pl.ANY)

    def blocks(n, dtype=BF):
        return pltpu.VMEM((n, B, B), dtype)

    tokens = pltpu.VMEM((B, ROWS * B), BF)
    side = [blocks(SHARE)] * 3 + [blocks(SHARE // 2)] * 2 + [blocks(SHARE)] * 2 + [blocks(SHARE, F32)]
    dma = pltpu.SemaphoreType.DMA
    scratch = (
        [blocks(ROWS)] * 3 + [blocks(NBLK + 1), blocks(NBLK + 1), blocks(PAIRS + 1)]
        + [blocks(ROWS)] * 6
        + [blocks(COLS)] * 2
        + [blocks(ROWS)] * 3
        + [blocks(ROWS)] * 3
        + [blocks(COLS)] * 6
        + [tokens, pltpu.VMEM((3, 32, ROWS * B), BF)]
        + side
        + side
        + [dma((4,))] * 2
        + [dma((2, 8))] * 2
        + [dma((2, 10))] * 2
        + [dma((2, 6))] * 2
        + [dma((3,))] * 2
        + [dma((2,)), dma((2, ROWS))]
        + [dma((2, 10))] * 2
        + [dma((2, 3, 3))] * 2
        + [pltpu.VMEM((8, WIDE), jnp.int32), pltpu.SMEM((8, WIDE), jnp.int32), dma(())]
    )
    return pl.pallas_call(
        main_kernel,
        out_shape=[
            jax.ShapeDtypeStruct((32, ROWS * B), BF),
            jax.ShapeDtypeStruct((SHARE, B, B), BF),
            jax.ShapeDtypeStruct((SHARE, B, B), BF),
        ],
        in_specs=[vmem] * 3 + [far] * 4,
        out_specs=[vmem] * 3,
        scratch_shapes=scratch,
        compiler_params=pltpu.CompilerParams(
            collective_id=0, has_side_effects=True, vmem_limit_bytes=62 * 2**20
        ),
        name="backward",
    )(up, dn, owner, x, g, wu, wd)


def results_kernel(*refs):
    count = (len(refs) - 2) // 3
    in_sem, out_sem = refs[-2:]
    ins = [pltpu.make_async_copy(refs[n], refs[2 * count + n], in_sem.at[n]) for n in range(count)]
    outs = [pltpu.make_async_copy(refs[2 * count + n], refs[count + n], out_sem.at[n]) for n in range(count)]
    for copy in ins:
        copy.start()
    for n in range(count):
        ins[n].wait()
        outs[n].start()
    for copy in outs:
        copy.wait()


def results(*values):
    far = pl.BlockSpec(memory_space=pl.ANY)
    return pl.pallas_call(
        results_kernel,
        out_shape=[jax.ShapeDtypeStruct(value.shape, value.dtype) for value in values],
        in_specs=[far] * len(values),
        out_specs=[far] * len(values),
        scratch_shapes=[pltpu.VMEM(value.shape, value.dtype) for value in values]
        + [pltpu.SemaphoreType.DMA((len(values),))] * 2,
        name="results",
    )(*values)


def shards(tokens_in, out_grad, up_weight, down_weight, up_blocks, down_blocks, owners):
    input_grad, up_grad, down_grad = results(
        *main(
            up_blocks[0], down_blocks[0], owners[0], tokens_in, out_grad, up_weight[0, 0], down_weight[0, 0]
        )
    )
    return input_grad, up_grad[None, None], down_grad[None, None]


def solution(mesh):
    placed = (
        P("dp", "row"),
        P("dp", "row"),
        P("row", "col", None, None, None),
        P("row", "col", None, None, None),
        P("row", "col", None),
        P("row", "col", None),
        P("row", "col", None),
    )
    return jax.shard_map(
        shards,
        mesh=mesh,
        in_specs=placed,
        out_specs=(
            P(("dp", "col"), "row"),
            P("row", "col", "dp", None, None),
            P("row", "col", "dp", None, None),
        ),
        check_vma=False,
    )
```
